128 devices in a mesh: ctx: 16 (over z, x), exp: 4 (over y), dp: 2 (over core).
Axes of the slice: x: 4, y: 4, z: 4, core: 2. Of those that a mesh axis runs over, the one named last changes fastest.
Arguments:
- mixer_in: bfloat16 [2, 4096, 4096], P('dp', 'ctx', 'exp'), may hold values from -6 to 6
- gate_in: bfloat16 [2, 4096, 4096], P('dp', 'ctx', 'exp'), may hold values from -6 to 6
- state_write: bfloat16 [2, 4096, 4, 128], P('dp', 'ctx', 'exp'), may hold values from -0.5 to 0.5
- state_read: bfloat16 [2, 4096, 4, 128], P('dp', 'ctx', 'exp'), may hold values from -0.5 to 0.5
- decay_rate: float32 [2, 64, 4096], P('dp', 'exp', 'ctx'), may hold values from 0 to 1, as said below
- skip_gain: float32 [64], P('exp'), may hold values from 0.5 to 1.5
- norm_gain: float32 [4096], P('exp'), may hold values from 0.5 to 1.5
- start_state: float32 [2, 64, 64, 128], P('dp', 'exp'), may hold values from -12 to 12
- out_weight: bfloat16 [4096, 4096], P('exp'), may hold values from -0.09375 to 0.09375
- residual: bfloat16 [2, 4096, 4096], P('dp', ('ctx', 'exp')), may hold values from -6 to 6
- router_weight: bfloat16 [4096, 8], replicated, may hold values from -0.09375 to 0.09375
- chosen: int32 [2, 4096, 2], P('dp', ('ctx', 'exp')), may hold values from 0 to 7, as said below
- slot_index: int32 [2, 4096, 2], P('dp', ('ctx', 'exp')), may hold values from -1 to 13, as said below
- spill_index: int32 [2, 4096, 2], P('dp', ('ctx', 'exp')), may hold values from -1 to 15, as said below
- gate_weight: bfloat16 [8, 4096, 8192], P(('exp', 'dp'), None, 'ctx'), may hold values from -0.09375 to 0.09375
- up_weight: bfloat16 [8, 4096, 8192], P(('exp', 'dp'), None, 'ctx'), may hold values from -0.09375 to 0.09375
- down_weight: bfloat16 [8, 4096, 8192], P(('exp', 'dp'), None, 'ctx'), may hold values from -0.125 to 0.125
Outputs:
- layer_out: bfloat16 [2, 4096, 4096], P('dp', ('ctx', 'exp'))
The draws below stay inside these ranges and needn't reach their ends.
Inputs may be any that keep to these rules, and one draw needn't show every extreme that they name: `decay_rate`: positive. `chosen`: two different experts per token. `slot_index`: the rank of the assignment among the assignments of the same device to the same expert, in the order of affinity, where that rank is below 14; -1 otherwise; distinct per device and expert. `spill_index`: -1 where slot_index is 0 or more or the assignment is dropped; else target expert * 2 + a row below 2, distinct per device and target.
All inputs are finite; a program needn't handle non-finite values.
Results may differ from the reference program's by a relative error of at most 0.03.
Values may be sent and summed in bfloat16 or wider, within the bound.
A program may use at most 192 MiB of HBM per device.

```python
import math
import jax
import jax.numpy as jnp
from jax import lax

D = 4096
FF = 8192
SSM_ATTENDERS = 64
HEAD_DIM = 64
STATE = 128
GROUPS = 4
EXPERTS = 8
TOK_DEV = 64
HI = 4096
CTX_LEN = 256
SEQUENCE_LENGTH = 4096
CAP = 14
SPILL = 2
BLOCK = 16
N_CTX = 16


def route_tables(key):
    block_count = 2 * SEQUENCE_LENGTH // TOK_DEV
    derived_prng_keys = jax.random.split(key, 8)
    popularity = jax.random.randint(derived_prng_keys[0], (block_count, 1, EXPERTS), 1, 5)
    raw_draw = jax.random.randint(derived_prng_keys[1], (block_count, TOK_DEV, EXPERTS), 0, 4096)
    scores = raw_draw * popularity * EXPERTS + jnp.arange(EXPERTS, dtype=jnp.int32)
    top_values, top_two = lax.top_k(scores, 2)
    hot_one = jax.random.randint(derived_prng_keys[2], (), 0, EXPERTS)
    hot_two = (hot_one + jax.random.randint(derived_prng_keys[3], (block_count, 1), 1, EXPERTS)) % EXPERTS
    tickets = jax.random.randint(derived_prng_keys[4], (block_count, TOK_DEV), 0, 1 << 20) * TOK_DEV + jnp.arange(TOK_DEV, dtype=jnp.int32)
    row_rank = jnp.argsort(jnp.argsort(tickets, axis=1), axis=1)
    hot_rows = CAP + SPILL // 2
    first_pick = jnp.where(row_rank < hot_rows, hot_one, jnp.where(row_rank < 2 * hot_rows, hot_two, top_two[:, :, 0]))
    second_pick = jnp.where(top_two[:, :, 1] == first_pick, top_two[:, :, 0], top_two[:, :, 1])
    chosen = jnp.stack([first_pick, second_pick], axis=2)
    flat_ids = chosen.reshape(block_count, 2 * TOK_DEV)
    priority = jax.random.randint(derived_prng_keys[5], (block_count, 2 * TOK_DEV), 0, 1 << 20) * (2 * TOK_DEV) + jnp.arange(2 * TOK_DEV, dtype=jnp.int32)
    before = priority[:, None, :] < priority[:, :, None]
    same_expert = flat_ids[:, :, None] == flat_ids[:, None, :]
    expert_rank = jnp.sum(same_expert & before, axis=2)
    slot_table = jnp.where(expert_rank < CAP, expert_rank, -1)
    overflow = expert_rank >= CAP
    spill_rank = jnp.sum(overflow[:, None, :] & before, axis=2)
    target_one = (jax.random.permutation(derived_prng_keys[6], block_count) % EXPERTS)[:, None]
    target_two = (target_one + jax.random.randint(derived_prng_keys[7], (block_count, 1), 1, EXPERTS)) % EXPERTS
    spill_table = jnp.where(overflow & (spill_rank < SPILL), target_one * SPILL + spill_rank, jnp.where(overflow & (spill_rank < 2 * SPILL), target_two * SPILL + spill_rank - SPILL, -1))
    return (chosen.reshape(2, SEQUENCE_LENGTH, 2).astype(jnp.int32), slot_table.reshape(2, SEQUENCE_LENGTH, 2).astype(jnp.int32), spill_table.reshape(2, SEQUENCE_LENGTH, 2).astype(jnp.int32))


def draw_chosen(key, part):
    tables = route_tables(key)
    return tables[0]


def draw_slot_index(key, part):
    tables = route_tables(key)
    return tables[1]


def draw_spill_index(key, part):
    tables = route_tables(key)
    return tables[2]


def draw_decay_rate(key, part):
    key = jax.random.fold_in(key, 41)
    derived_prng_keys = jax.random.split(key, 7)
    slow_share = 0.5
    slow_heads = jax.random.uniform(derived_prng_keys[0], (2, SSM_ATTENDERS, 1)) < slow_share
    slow_rate = jax.random.uniform(derived_prng_keys[1], (2, SSM_ATTENDERS, 1), minval=0.1, maxval=0.5) / SEQUENCE_LENGTH
    fast_rate = jax.random.uniform(derived_prng_keys[2], (2, SSM_ATTENDERS, 1), minval=1.0 / 50.0, maxval=1.0 / 30.0)
    steady_decay_speed = jnp.where(slow_heads, slow_rate, fast_rate)
    each_place_entry = jnp.exp(jax.random.uniform(derived_prng_keys[3], (2, SSM_ATTENDERS, SEQUENCE_LENGTH), minval=math.log(0.6), maxval=math.log(1.5)))
    rough_tier = jnp.exp(jax.random.uniform(derived_prng_keys[4], (2, SSM_ATTENDERS, SEQUENCE_LENGTH // CTX_LEN, 1), minval=math.log(0.5), maxval=math.log(2.0)))
    rough_tier = jnp.broadcast_to(rough_tier, (2, SSM_ATTENDERS, SEQUENCE_LENGTH // CTX_LEN, CTX_LEN)).reshape(2, SSM_ATTENDERS, SEQUENCE_LENGTH)
    spike_positions = jax.random.randint(derived_prng_keys[5], (2, 1, 2), 0, SEQUENCE_LENGTH)
    locations = jnp.arange(SEQUENCE_LENGTH, dtype=jnp.int32)
    surge_indicator = jnp.any(locations[None, None, :, None] == spike_positions[:, :, None, :], axis=-1)
    surge_magnitude = jax.random.uniform(derived_prng_keys[6], (2, SSM_ATTENDERS, 1), minval=0.22, maxval=0.45)
    return (steady_decay_speed * each_place_entry * rough_tier + jnp.where(surge_indicator, surge_magnitude, 0.0)).astype(jnp.float32)


def shard_levels(key, shape, cuts, least, largest):
    level, own = 1.0, jax.random.fold_in(key, 6)
    for dim, parts in cuts:
        draws = jnp.exp(jax.random.uniform(jax.random.fold_in(own, dim), (parts,), jnp.float32, least / len(cuts), largest / len(cuts)))
        level = level * jnp.repeat(draws, shape[dim] // parts).reshape([-1 if axis == dim else 1 for axis in range(len(shape))])
    return level


def gaussian(rng, dims, width, bound, cuts=(), held_as=jnp.bfloat16):
    array = jax.random.normal(rng, dims, jnp.float32) * width
    if len(cuts) > 0:
        array = shard_levels(rng, dims, cuts, -0.22, 0.18) * array
    return jnp.clip(array, min=-bound, max=bound).astype(held_as)


def setup_inputs(seed: int = 0) -> dict:
    streams_of = jax.random.split(jax.random.key(seed), 18)
    mixer_in = gaussian(streams_of[0], (2, SEQUENCE_LENGTH, HI), 1.0, 6.0, ((0, 2), (1, 16), (2, 4)))
    gate_in = gaussian(streams_of[1], (2, SEQUENCE_LENGTH, HI), 1.0, 6.0, ((0, 2), (1, 16), (2, 4)))
    state_write = gaussian(streams_of[2], (2, SEQUENCE_LENGTH, GROUPS, STATE), STATE ** -0.5, 0.5, ((0, 2), (1, 16), (2, 4)))
    state_read = gaussian(streams_of[3], (2, SEQUENCE_LENGTH, GROUPS, STATE), STATE ** -0.5, 0.5, ((0, 2), (1, 16), (2, 4)))
    decay_rate = draw_decay_rate(jax.random.fold_in(streams_of[17], 71), 0)
    skip_gain = jnp.clip(0.5 + 1.0 * jax.random.uniform(streams_of[5], (SSM_ATTENDERS,), jnp.float32) ** shard_levels(streams_of[5], (SSM_ATTENDERS,), ((0, 4),), -0.2, 0.2), 0.5, 1.5)
    norm_gain = jnp.clip(0.5 + 1.0 * jax.random.uniform(streams_of[6], (HI,), jnp.float32) ** shard_levels(streams_of[6], (HI,), ((0, 4),), -0.2, 0.2), 0.5, 1.5)
    start_state = gaussian(streams_of[7], (2, SSM_ATTENDERS, HEAD_DIM, STATE), 2.0, 12.0, ((0, 2), (1, 4)), jnp.float32)
    out_weight = gaussian(streams_of[8], (HI, D), HI ** -0.5, 0.09375, ((0, 4),))
    residual = gaussian(streams_of[9], (2, SEQUENCE_LENGTH, D), 1.0, 6.0, ((0, 2), (1, 64)))
    router_weight = gaussian(streams_of[10], (D, EXPERTS), D ** -0.5, 0.09375)
    chosen = draw_chosen(jax.random.fold_in(streams_of[17], 71), 0)
    slot_index = draw_slot_index(jax.random.fold_in(streams_of[17], 71), 0)
    spill_index = draw_spill_index(jax.random.fold_in(streams_of[17], 71), 0)
    gate_weight = gaussian(streams_of[14], (EXPERTS, D, FF), D ** -0.5, 0.09375, ((0, 8), (2, 16)))
    up_weight = gaussian(streams_of[15], (EXPERTS, D, FF), D ** -0.5, 0.09375, ((0, 8), (2, 16)))
    down_weight = gaussian(streams_of[16], (EXPERTS, D, FF), (FF // 4) ** -0.5, 0.125, ((0, 8), (2, 16)))
    return {"mixer_in": mixer_in, "gate_in": gate_in, "state_write": state_write, "state_read": state_read, "decay_rate": decay_rate, "skip_gain": skip_gain, "norm_gain": norm_gain, "start_state": start_state, "out_weight": out_weight, "residual": residual, "router_weight": router_weight, "chosen": chosen, "slot_index": slot_index, "spill_index": spill_index, "gate_weight": gate_weight, "up_weight": up_weight, "down_weight": down_weight}


def expert_rows(operands):
    rows_in, gate_w, up_w, down_w = operands
    piece_width = FF // N_CTX
    summed = jnp.zeros((rows_in.shape[0], D), jnp.float32)
    for piece in range(N_CTX):
        lower_edge = piece * piece_width
        upper_edge = lower_edge + piece_width
        gate_val = jnp.dot(rows_in, gate_w[:, lower_edge:upper_edge], preferred_element_type=jnp.float32)
        up_val = jnp.dot(rows_in, up_w[:, lower_edge:upper_edge], preferred_element_type=jnp.float32)
        activated = (jax.nn.silu(gate_val) * up_val).astype(jnp.bfloat16)
        term = lax.dot_general(activated, down_w[:, lower_edge:upper_edge], (((1,), (1,)), ((), ())), preferred_element_type=jnp.float32).astype(jnp.bfloat16)
        summed = summed + lax.optimization_barrier(term).astype(jnp.float32)
    return summed.astype(jnp.bfloat16)

def reference(mixer_in, gate_in, state_write, state_read, decay_rate, skip_gain, norm_gain, start_state, out_weight, residual, router_weight, chosen, slot_index, spill_index, gate_weight, up_weight, down_weight):
    exact = lax.Precision.HIGHEST
    per_group = SSM_ATTENDERS // GROUPS
    group_width = HI // GROUPS
    hidden_list = []
    for seq_index in range(2):
        inputs = mixer_in[seq_index].astype(jnp.float32).reshape(SEQUENCE_LENGTH, SSM_ATTENDERS, HEAD_DIM)
        write_rows = jnp.repeat(state_write[seq_index].astype(jnp.float32), per_group, axis=1)
        read_rows = jnp.repeat(state_read[seq_index].astype(jnp.float32), per_group, axis=1)
        decays = jnp.exp(-decay_rate[seq_index]).T

        def advance(carried, slices):
            token_in, write_col, read_col, factor = slices
            carried = factor[:, None, None] * carried + token_in[:, :, None] * write_col[:, None, :]
            return (carried, jnp.einsum('hpn,hn->hp', carried, read_col, precision=exact))
        final_state, read_out = lax.scan(advance, start_state[seq_index], (inputs, write_rows, read_rows, decays))
        head_out = (read_out + skip_gain[None, :, None] * inputs).reshape(SEQUENCE_LENGTH, HI)
        gated_out = head_out * jax.nn.silu(gate_in[seq_index].astype(jnp.float32))
        grouped = gated_out.reshape(SEQUENCE_LENGTH, GROUPS, group_width)
        normed = (grouped * lax.rsqrt(lax.optimization_barrier(jnp.mean(grouped * grouped, axis=2, keepdims=True)) + 1e-05)).reshape(SEQUENCE_LENGTH, HI) * norm_gain
        normed = normed.astype(jnp.bfloat16)
        mixer_out = jnp.zeros((SEQUENCE_LENGTH, D), jnp.float32)
        for group in range(GROUPS):
            lower_edge = group * group_width
            upper_edge = lower_edge + group_width
            term = jnp.dot(normed[:, lower_edge:upper_edge], out_weight[lower_edge:upper_edge], preferred_element_type=jnp.float32).astype(jnp.bfloat16)
            mixer_out = mixer_out + lax.optimization_barrier(term).astype(jnp.float32)
        hidden_list.append((residual[seq_index].astype(jnp.float32) + mixer_out).astype(jnp.bfloat16))
    hidden = jnp.concatenate(hidden_list, axis=0)
    logits = jnp.dot(hidden, router_weight, preferred_element_type=jnp.float32)
    expert_ids = chosen.reshape(-1, 2).astype(jnp.int32)
    picked = jnp.take_along_axis(logits, expert_ids, axis=1)
    shares = jax.nn.sigmoid(picked - picked[:, ::-1])
    slot_ids = slot_index.reshape(-1, 2).astype(jnp.int32)
    spill_ids = spill_index.reshape(-1, 2).astype(jnp.int32)
    block_count = 2 * SEQUENCE_LENGTH // TOK_DEV
    block_rows = block_count * BLOCK
    target_expert = jnp.where(slot_ids >= 0, expert_ids, spill_ids // SPILL)
    target_place = jnp.where(slot_ids >= 0, slot_ids, CAP + spill_ids % SPILL)
    placed = (slot_ids >= 0) | (spill_ids >= 0)
    owner_block = (jnp.arange(2 * SEQUENCE_LENGTH, dtype=jnp.int32) // TOK_DEV)[:, None]
    row_index = jnp.where(placed, target_expert * block_rows + owner_block * BLOCK + target_place, EXPERTS * block_rows).astype(jnp.int32)
    expert_in = jnp.zeros((EXPERTS * block_rows, D), jnp.bfloat16).at[row_index.reshape(-1)].set(jnp.repeat(hidden, 2, axis=0), mode='drop')
    expert_out = lax.map(expert_rows, (expert_in.reshape(EXPERTS, block_rows, D), gate_weight, up_weight, down_weight)).reshape(EXPERTS * block_rows, D)
    fetched = expert_out[jnp.minimum(row_index, EXPERTS * block_rows - 1)].astype(jnp.float32) * placed[:, :, None].astype(jnp.float32)
    expert_sum = shares[:, 0:1] * fetched[:, 0] + shares[:, 1:2] * fetched[:, 1]
    layer_out = (hidden.astype(jnp.float32) + expert_sum).astype(jnp.bfloat16)
    return layer_out.reshape(2, SEQUENCE_LENGTH, D)
```

```python
import jax
import jax.numpy as jnp
from jax import lax
from jax.experimental import pallas as pl
from jax.experimental.pallas import tpu as pltpu
from jax.sharding import PartitionSpec as P

D = 4096
EXPERTS = 8
CAP = 14
SPILL = 2
BLOCK = 16
SIDE = 4
ROWS = EXPERTS * BLOCK
WIDTH = 512
PAIRS = D // WIDTH // 2
HALF = ROWS // 2
MESH = pl.DeviceIdType.MESH


def experts_kernel(
    rows_ref,
    gate_ref,
    up_ref,
    down_ref,
    out_ref,
    xg,
    acc,
    act,
    w_gate,
    w_up,
    w_down,
    part,
    line,
    ag_send,
    ag_recv,
    rs_send,
    rs_recv,
    load_sem,
    own_sem,
):
    here = lax.axis_index("ctx")
    my = {"x": lax.rem(here, SIDE), "z": lax.div(here, SIDE)}

    def around(axis, step):
        return lax.rem(my[axis] + step + SIDE, SIDE)

    def neighbour(axis, step):
        other = around(axis, step)
        if axis == "x":
            return {"ctx": my["z"] * SIDE + other}
        return {"ctx": other * SIDE + my["x"]}

    def along(axis, ref, place, at):
        if axis == "z":
            return ref.at[place, at]
        return ref.at[at, place]

    loads = [
        pltpu.make_async_copy(src, dst, load_sem.at[i])
        for i, (src, dst) in enumerate(((gate_ref, w_gate), (up_ref, w_up), (down_ref, w_down)))
    ]
    for load in loads:
        load.start()
    own = [
        pltpu.make_async_copy(
            rows_ref.at[:, pl.ds(k * WIDTH, WIDTH)], xg.at[k, my["z"], my["x"]], own_sem.at[k]
        )
        for k in range(2 * PAIRS)
    ]
    for copy in own:
        copy.start()

    barrier = pltpu.get_barrier_semaphore()
    for axis in ("x", "z"):
        for step in (1, -1):
            pl.semaphore_signal(
                barrier, inc=1, device_id=neighbour(axis, step), device_id_type=MESH
            )
    pl.semaphore_wait(barrier, 4)
    for copy in own:
        copy.wait()

    every = pl.ds(0, SIDE)
    halves = {1: pl.ds(0, SIDE // 2), -1: pl.ds(SIDE // 2, SIDE // 2)}
    half_rows = {1: pl.ds(0, HALF), -1: pl.ds(HALF, HALF)}
    axes = (("x", "z"), ("z", "x"))
    slot = {1: 0, -1: 1}

    def ag_copy(j, t, step, d, landing):
        near, far = axes[t]
        chunk = xg.at[2 * j + t]
        back = -d if landing else 0
        if step == 0:
            ref, to = along(near, chunk, around(near, back), my[far]), near
        elif step == 1:
            ref = along(near, chunk, around(near, -2 * d if landing else -d), my[far])
            ref, to = ref.at[half_rows[d]], near
        elif step == 2:
            ref, to = along(far, chunk, around(far, back), every), far
        else:
            ref = along(far, chunk, around(far, -2 * d if landing else -d), halves[d])
            to = far
        m = step * 2 + slot[d]
        return pltpu.make_async_remote_copy(
            src_ref=ref,
            dst_ref=ref,
            send_sem=ag_send.at[j, t, m],
            recv_sem=ag_recv.at[j, t, m],
            device_id=neighbour(to, d),
            device_id_type=MESH,
        )

    def ag_start(j, step):
        for t in range(2):
            for d in (1, -1):
                ag_copy(j, t, step, d, False).start()

    def ag_arrive(j, step):
        for t in range(2):
            for d in (1, -1):
                ag_copy(j, t, step, d, True).wait_recv()

    def ag_sent(j):
        for step in range(4):
            for t in range(2):
                for d in (1, -1):
                    ag_copy(j, t, step, d, False).wait_send()

    def gate_up(j, first):
        @pl.loop(0, SIDE * SIDE // 2)
        def _(b):
            zz, x0 = lax.div(b, 2), lax.rem(b, 2) * 2
            rows = pl.ds(pl.multiple_of(b * 2 * ROWS, 2 * ROWS), 2 * ROWS)
            for n, weight in enumerate((w_gate, w_up)):
                total = None
                for t in range(2):
                    k = 2 * j + t
                    left = xg[k, zz, pl.ds(x0, 2)].reshape(2 * ROWS, WIDTH)
                    right = weight[pl.ds(pl.multiple_of(k * WIDTH, WIDTH), WIDTH), :]
                    term = jnp.dot(left, right, preferred_element_type=jnp.float32)
                    total = term if total is None else total + term
                if first:
                    acc[n, rows, :] = total
                else:
                    acc[n, rows, :] += total

    ag_start(0, 0)
    ag_arrive(0, 0)
    ag_start(0, 1)
    ag_arrive(0, 1)
    ag_start(0, 2)
    for load in loads:
        load.wait()

    def ag_round(j, first):
        last = j == PAIRS - 1 if isinstance(j, int) else False
        if not last:
            ag_start(j + 1, 0)
        if not first:
            if isinstance(j, int) and j == 1:
                gate_up(0, True)
            else:
                gate_up(j - 1, False)
        if not last:
            ag_arrive(j + 1, 0)
            ag_start(j + 1, 1)
        ag_arrive(j, 2)
        if not first:
            ag_sent(j - 1)
        ag_start(j, 3)
        if not last:
            ag_arrive(j + 1, 1)
            ag_start(j + 1, 2)
        ag_arrive(j, 3)

    ag_round(0, True)
    ag_round(1, False)

    @pl.loop(2, PAIRS - 1)
    def _(j):
        ag_round(j, False)

    ag_round(PAIRS - 1, False)
    gate_up(PAIRS - 1, False)

    @pl.loop(0, SIDE * SIDE)
    def _(b):
        rows = pl.ds(pl.multiple_of(b * ROWS, ROWS), ROWS)
        gate_val = acc[0, rows, :]
        act[rows, :] = (gate_val / (1.0 + jnp.exp(-gate_val)) * acc[1, rows, :]).astype(jnp.bfloat16)

    ag_sent(PAIRS - 1)

    def rs_copy(j, t, step, d):
        near, far = axes[t]
        p = part.at[lax.rem(j, 2), t]
        room = xg.at[2 * j + t]
        if step == 0:
            src = along(far, p, around(far, 2), halves[d])
            dst, to = room.at[0, halves[d]], far
        elif step == 1:
            src = along(far, p, around(far, d), every)
            dst, to = room.at[1 + slot[d]], far
        elif step == 2:
            src = line.at[lax.rem(j, 2), t, around(near, 2), half_rows[d]]
            dst, to = room.at[3, 0, half_rows[d]], near
        else:
            src = line.at[lax.rem(j, 2), t, around(near, d)]
            dst, to = room.at[3, 1 + slot[d]], near
        m = step * 2 + slot[d]
        return pltpu.make_async_remote_copy(
            src_ref=src,
            dst_ref=dst,
            send_sem=rs_send.at[j, t, m],
            recv_sem=rs_recv.at[j, t, m],
            device_id=neighbour(to, d),
            device_id_type=MESH,
        )

    def rs_start(j, step, t):
        for d in (1, -1):
            rs_copy(j, t, step, d).start()

    def rs_arrive(j, step, t):
        for d in (1, -1):
            rs_copy(j, t, step, d).wait_recv()

    def rs_sent(j):
        for step in range(4):
            for t in range(2):
                for d in (1, -1):
                    rs_copy(j, t, step, d).wait_send()

    def down(j):
        @pl.loop(0, SIDE * SIDE // 2)
        def _(b):
            zz, x0 = lax.div(b, 2), lax.rem(b, 2) * 2
            rows = pl.ds(pl.multiple_of(b * 2 * ROWS, 2 * ROWS), 2 * ROWS)
            for t in range(2):
                k = 2 * j + t
                right = w_down[pl.ds(pl.multiple_of(k * WIDTH, WIDTH), WIDTH), :]
                term = lax.dot_general(
                    act[rows, :], right, (((1,), (1,)), ((), ())), preferred_element_type=jnp.float32
                )
                part[lax.rem(j, 2), t, zz, pl.ds(x0, 2)] = term.astype(jnp.bfloat16).reshape(
                    2, ROWS, WIDTH
                )

    f32 = jnp.float32

    def add_first(j, t):
        far, near = axes[t][1], axes[t][0]
        s = lax.rem(j, 2)
        for d in (1, -1):
            base = 0 if d == 1 else SIDE // 2
            place = around(far, d)

            @pl.loop(0, SIDE // 2)
            def _(i):
                at = (place, base + i) if far == "z" else (base + i, place)
                part[s, t, at[0], at[1]] = (
                    part[s, t, at[0], at[1]].astype(f32) + xg[2 * j + t, 0, base + i].astype(f32)
                ).astype(jnp.bfloat16)

    def add_line(j, t):
        far = axes[t][1]
        s = lax.rem(j, 2)

        @pl.loop(0, SIDE)
        def _(i):
            at = (my[far], i) if far == "z" else (i, my[far])
            line[s, t, i] = (
                part[s, t, at[0], at[1]].astype(f32)
                + xg[2 * j + t, 1, i].astype(f32)
                + xg[2 * j + t, 2, i].astype(f32)
            ).astype(jnp.bfloat16)

    def add_second(j, t):
        near = axes[t][0]
        s = lax.rem(j, 2)
        for d in (1, -1):
            at = around(near, d)
            line[s, t, at, half_rows[d]] = (
                line[s, t, at, half_rows[d]].astype(f32)
                + xg[2 * j + t, 3, 0, half_rows[d]].astype(f32)
            ).astype(jnp.bfloat16)

    def add_last(j, t):
        near = axes[t][0]
        s = lax.rem(j, 2)
        total = (
            line[s, t, my[near]].astype(f32)
            + xg[2 * j + t, 3, 1].astype(f32)
            + xg[2 * j + t, 3, 2].astype(f32)
        )
        start = (2 * j + t) * WIDTH
        out_ref[:, pl.ds(pl.multiple_of(start, WIDTH), WIDTH)] = total.astype(jnp.bfloat16)

    def rs_second(j):
        for t in range(2):
            rs_arrive(j, 1, t)
            add_line(j, t)
            rs_start(j, 2, t)

    def rs_third(j):
        for t in range(2):
            rs_arrive(j, 2, t)
            add_second(j, t)
            rs_start(j, 3, t)

    def rs_begin(j):
        for t in range(2):
            rs_arrive(j, 0, t)
            add_first(j, t)
            rs_start(j, 1, t)

    def rs_end(j):
        for t in range(2):
            rs_arrive(j, 3, t)
            add_last(j, t)
        rs_sent(j)

    def both(j):
        for t in range(2):
            rs_start(j, 0, t)

    down(0)
    both(0)
    down(1)
    rs_begin(0)
    both(1)

    @pl.loop(0, PAIRS - 1)
    def _(j):
        rs_second(j)
        rs_begin(j + 1)
        rs_third(j)
        rs_end(j)

        @pl.when(j + 2 < PAIRS)
        def _():
            down(j + 2)
            both(j + 2)

    rs_second(PAIRS - 1)
    rs_third(PAIRS - 1)
    rs_end(PAIRS - 1)


def experts(rows, gate_w, up_w, down_w):
    hidden = gate_w.shape[1]
    bf16 = jnp.bfloat16
    any_space = pl.BlockSpec(memory_space=pl.ANY)
    return pl.pallas_call(
        experts_kernel,
        out_shape=jax.ShapeDtypeStruct((ROWS, D), bf16),
        in_specs=[any_space] * 4,
        out_specs=pl.BlockSpec(memory_space=pltpu.VMEM),
        scratch_shapes=[
            pltpu.VMEM((2 * PAIRS, SIDE, SIDE, ROWS, WIDTH), bf16),
            pltpu.VMEM((2, SIDE * SIDE * ROWS, hidden), jnp.float32),
            pltpu.VMEM((SIDE * SIDE * ROWS, hidden), bf16),
            pltpu.VMEM((D, hidden), bf16),
            pltpu.VMEM((D, hidden), bf16),
            pltpu.VMEM((D, hidden), bf16),
            pltpu.VMEM((2, 2, SIDE, SIDE, ROWS, WIDTH), bf16),
            pltpu.VMEM((2, 2, SIDE, ROWS, WIDTH), bf16),
            pltpu.SemaphoreType.DMA((PAIRS, 2, 8)),
            pltpu.SemaphoreType.DMA((PAIRS, 2, 8)),
            pltpu.SemaphoreType.DMA((PAIRS, 2, 8)),
            pltpu.SemaphoreType.DMA((PAIRS, 2, 8)),
            pltpu.SemaphoreType.DMA((3,)),
            pltpu.SemaphoreType.DMA((2 * PAIRS,)),
        ],
        compiler_params=pltpu.CompilerParams(
            collective_id=0, has_side_effects=True, vmem_limit_bytes=60 << 20
        ),
        cost_estimate=pl.CostEstimate(
            flops=6 * 2048 * D * 512, bytes_accessed=14 << 20, transcendentals=1 << 20
        ),
    )(rows, gate_w, up_w, down_w)


def entering_2(value, axis, combine, identity):
    length, here = (lax.axis_size(axis), lax.axis_index(axis))
    everything = jax.tree.map(
        lambda part, kind: lax.all_gather(part.astype(kind), axis),
        value,
        (jnp.bfloat16, jnp.bfloat16),
    )
    start = jax.tree.map(
        lambda part, zero: jnp.broadcast_to(jnp.asarray(zero, part.dtype), part.shape),
        value,
        identity,
    )

    def hop(k, before):
        reached = k < here
        new = combine(
            before, jax.tree.map(lambda part, own: part[k].astype(own.dtype), everything, value)
        )
        return jax.tree.map(lambda a, b: jnp.where(reached, a, b), new, before)

    return lax.fori_loop(0, length, hop, start)


def chain_combine(earlier, later):
    return (earlier[0] * later[0], later[0][:, None, None] * earlier[1] + later[1])


def shards(
    mixer_in,
    gate_in,
    state_write,
    state_read,
    decay_rate,
    skip_gain,
    norm_gain,
    start_state,
    out_weight,
    residual,
    router_weight,
    chosen,
    slot_index,
    spill_index,
    gate_weight,
    up_weight,
    down_weight,
):
    exact = lax.Precision.HIGHEST
    length = mixer_in.shape[1]
    head_count = skip_gain.shape[0]
    inner_width = mixer_in.shape[2]
    head_size = inner_width // head_count
    inputs = mixer_in[0].astype(jnp.float32).reshape(length, head_count, head_size)
    write_rows = state_write[0, :, 0].astype(jnp.float32)
    read_rows = state_read[0, :, 0].astype(jnp.float32)
    levels = jnp.cumsum(decay_rate[0], axis=1)
    locations = jnp.arange(length)
    causal = locations[:, None] >= locations[None, :]
    span_levels = levels[:, :, None] - levels[:, None, :]
    decay_pairs = jnp.where(causal[None], jnp.exp(-jnp.where(causal[None], span_levels, 0.0)), 0.0)
    intersections = jnp.dot(read_rows, write_rows.T, precision=exact)
    within = jnp.einsum("hts,shp->thp", decay_pairs * intersections[None], inputs, precision=exact)
    to_end = jnp.exp(levels - levels[:, -1:])
    local_state = jnp.einsum("hs,shp,sn->hpn", to_end, inputs, write_rows, precision=exact)
    totals = jnp.exp(-levels[:, -1])
    before_decay, before_state = entering_2(
        (totals, local_state),
        "ctx",
        chain_combine,
        (jnp.ones_like(totals), jnp.zeros_like(local_state)),
    )
    entering = before_decay[:, None, None] * start_state[0] + before_state
    carried = (
        jnp.einsum("tn,hpn->thp", read_rows, entering, precision=exact)
        * jnp.exp(-levels).T[:, :, None]
    )
    head_out = within + carried + skip_gain[None, :, None] * inputs
    gated_out = head_out.reshape(length, inner_width) * jax.nn.silu(gate_in[0].astype(jnp.float32))
    normed = (
        gated_out
        * lax.rsqrt(jnp.mean(gated_out * gated_out, axis=1, keepdims=True) + 1e-05)
        * norm_gain
    ).astype(jnp.bfloat16)
    mixer_out = lax.psum_scatter(
        jnp.dot(normed, out_weight, preferred_element_type=jnp.float32).astype(jnp.bfloat16),
        "exp",
        scatter_dimension=0,
        tiled=True,
    ).astype(jnp.float32)
    hidden = (residual[0].astype(jnp.float32) + mixer_out).astype(jnp.bfloat16)
    logits = jnp.dot(hidden, router_weight, preferred_element_type=jnp.float32)
    expert_ids = chosen[0]
    matches = expert_ids[:, :, None] == jnp.arange(EXPERTS)[None, None, :]
    picked = jnp.sum(jnp.where(matches, logits[:, None, :], 0.0), axis=2)
    shares = jax.nn.sigmoid(picked - picked[:, ::-1])
    slot_ids = slot_index[0]
    spill_ids = spill_index[0]
    target_row = jnp.where(
        slot_ids >= 0,
        expert_ids * BLOCK + slot_ids,
        jnp.where(spill_ids >= 0, spill_ids // SPILL * BLOCK + CAP + spill_ids % SPILL, -1),
    )
    onehot = target_row[:, :, None] == jnp.arange(EXPERTS * BLOCK)[None, None, :]
    placing = jnp.sum(onehot, axis=1).astype(jnp.bfloat16)
    outgoing = lax.dot_general(
        placing, hidden, (((0,), (0,)), ((), ())), preferred_element_type=jnp.float32
    )
    outgoing = outgoing.astype(jnp.bfloat16).reshape(EXPERTS, BLOCK, D)
    own_gate = gate_weight[0]
    own_up = up_weight[0]
    own_down = down_weight[0]

    arrived = lax.all_to_all(outgoing, ("exp", "dp"), split_axis=0, concat_axis=0, tiled=True)
    summed = experts(arrived.reshape(ROWS, D), own_gate, own_up, own_down)
    returned = lax.all_to_all(
        summed.reshape(EXPERTS, BLOCK, D), ("exp", "dp"), split_axis=0, concat_axis=0, tiled=True
    )
    weighting = jnp.sum(jnp.where(onehot, shares[:, :, None], 0.0), axis=1)
    expert_sum = jnp.dot(
        weighting, returned.reshape(EXPERTS * BLOCK, D).astype(jnp.float32), precision=exact
    )
    return (hidden.astype(jnp.float32) + expert_sum).astype(jnp.bfloat16)[None]


def solution(mesh):
    placed = (
        P("dp", "ctx", "exp"),
        P("dp", "ctx", "exp"),
        P("dp", "ctx", "exp", None),
        P("dp", "ctx", "exp", None),
        P("dp", "exp", "ctx"),
        P("exp"),
        P("exp"),
        P("dp", "exp", None, None),
        P("exp", None),
        P("dp", ("ctx", "exp"), None),
        P(),
        P("dp", ("ctx", "exp"), None),
        P("dp", ("ctx", "exp"), None),
        P("dp", ("ctx", "exp"), None),
        P(("exp", "dp"), None, "ctx"),
        P(("exp", "dp"), None, "ctx"),
        P(("exp", "dp"), None, "ctx"),
    )
    return jax.shard_map(
        shards, mesh=mesh, in_specs=placed, out_specs=P("dp", ("ctx", "exp"), None), check_vma=False
    )
```

```python
import jax
import jax.numpy as jnp
from jax import lax
from jax.experimental import pallas as pl
from jax.experimental.pallas import tpu as pltpu
from jax.sharding import PartitionSpec as P

D = 4096
EXPERTS = 8
CAP = 14
SPILL = 2
BLOCK = 16
SIDE = 4
ROWS = EXPERTS * BLOCK
WIDTH = 256
PAIRS = D // WIDTH // 2
HALF = ROWS // 2
TOKENS = 64
GROUPS = 4
MESH = pl.DeviceIdType.MESH


def layer_kernel(
    normed_ref,
    mix_ref,
    residual_ref,
    router_ref,
    chosen_ref,
    slot_ref,
    spill_ref,
    gate_ref,
    up_ref,
    down_ref,
    out_ref,
    normed,
    w_mix,
    mixed,
    terms,
    hidden,
    placing,
    shares,
    logits,
    leaving,
    sums,
    returned,
    xg,
    acc,
    act,
    w_gate,
    w_up,
    w_down,
    part,
    line,
    ag_send,
    ag_recv,
    rs_send,
    rs_recv,
    mix_send,
    mix_recv,
    row_send,
    row_recv,
    back_send,
    back_recv,
    load_sem,
    mix_sem,
    normed_sem,
):
    here = lax.axis_index("ctx")
    my = {"x": lax.rem(here, SIDE), "z": lax.div(here, SIDE)}

    def around(axis, step):
        return lax.rem(my[axis] + step + SIDE, SIDE)

    def neighbour(axis, step):
        other = around(axis, step)
        if axis == "x":
            return {"ctx": my["z"] * SIDE + other}
        return {"ctx": other * SIDE + my["x"]}

    def along(axis, ref, place, at):
        if axis == "z":
            return ref.at[place, at]
        return ref.at[at, place]

    f32, bf16 = jnp.float32, jnp.bfloat16
    my_exp, my_dp = lax.axis_index("exp"), lax.axis_index("dp")
    owner = my_exp * 2 + my_dp

    fetch = pltpu.make_async_copy(normed_ref, normed, normed_sem)
    fetch.start()

    def mix_load(j):
        columns = pl.ds(pl.multiple_of(j * 2 * WIDTH, 2 * WIDTH), 2 * WIDTH)
        return pltpu.make_async_copy(mix_ref.at[:, columns], w_mix.at[:, columns], mix_sem.at[j])

    for j in range(PAIRS):
        mix_load(j).start()
    loads = [
        pltpu.make_async_copy(src, dst, load_sem.at[i])
        for i, (src, dst) in enumerate(((gate_ref, w_gate), (up_ref, w_up), (down_ref, w_down)))
    ]
    for load in loads:
        load.start()

    def partner(o):
        other = lax.rem(owner + o, EXPERTS)
        return other, {"exp": lax.div(other, 2), "dp": lax.rem(other, 2)}

    barrier = pltpu.get_barrier_semaphore()
    for axis in ("x", "z"):
        for step in (1, -1):
            pl.semaphore_signal(
                barrier, inc=1, device_id=neighbour(axis, step), device_id_type=MESH
            )
    for o in range(1, EXPERTS):
        pl.semaphore_signal(barrier, inc=1, device_id=partner(o)[1], device_id_type=MESH)

    row_id = lax.broadcasted_iota(jnp.int32, (ROWS, TOKENS), 0)
    expert_ids, slot_ids, spill_ids = chosen_ref[...], slot_ref[...], spill_ref[...]
    target = jnp.where(
        slot_ids >= 0,
        expert_ids * BLOCK + slot_ids,
        jnp.where(
            spill_ids >= 0,
            jnp.right_shift(spill_ids, 1) * BLOCK + CAP + jnp.bitwise_and(spill_ids, 1),
            -1,
        ),
    )
    places = [row_id == target[i : i + 1, :] for i in range(2)]
    placing[...] = (places[0].astype(f32) + places[1].astype(f32)).astype(bf16)
    logits[...] = jnp.zeros_like(logits)
    pl.semaphore_wait(barrier, 4 + EXPERTS - 1)

    def columns_of(k):
        return pl.ds(pl.multiple_of(k * WIDTH, WIDTH), WIDTH)

    def term_copy(j, t, i):
        other = lax.rem(my_exp + i, GROUPS)
        return pltpu.make_async_remote_copy(
            src_ref=mixed.at[lax.rem(j, 2), t, other],
            dst_ref=terms.at[2 * j + t, i - 1],
            send_sem=mix_send.at[2 * j + t, i - 1],
            recv_sem=mix_recv.at[2 * j + t, i - 1],
            device_id={"exp": other},
            device_id_type=MESH,
        )

    def mix(j):
        mix_load(j).wait()
        for t in range(2):
            term = jnp.dot(
                normed[...], w_mix[:, columns_of(2 * j + t)], preferred_element_type=f32
            )
            mixed[lax.rem(j, 2), t] = term.astype(bf16).reshape(GROUPS, TOKENS, WIDTH)
            for i in range(1, GROUPS):
                term_copy(j, t, i).start()

    def row_copy(j, t, o):
        other, place = partner(o)
        return pltpu.make_async_remote_copy(
            src_ref=leaving.at[lax.rem(j, 2), t, other],
            dst_ref=xg.at[
                2 * j + t, my["z"], my["x"], pl.ds(pl.multiple_of(owner * BLOCK, BLOCK), BLOCK)
            ],
            send_sem=row_send.at[2 * j + t],
            recv_sem=row_recv.at[2 * j + t],
            device_id=place,
            device_id_type=MESH,
        )

    def rows_wait(j, t):
        ref = xg.at[2 * j + t, my["z"], my["x"], pl.ds(0, ROWS - BLOCK)]
        return pltpu.make_async_remote_copy(
            src_ref=ref,
            dst_ref=ref,
            send_sem=row_send.at[2 * j + t],
            recv_sem=row_recv.at[2 * j + t],
            device_id=partner(1)[1],
            device_id_type=MESH,
        )

    def tokens(j):
        for t in range(2):
            k = 2 * j + t
            columns = columns_of(k)
            for i in range(1, GROUPS):
                term_copy(j, t, i).wait_recv()
            total = mixed[lax.rem(j, 2), t, my_exp].astype(f32)
            for i in range(1, GROUPS):
                total = total + terms[k, i - 1].astype(f32)
            value = (residual_ref[:, columns].astype(f32) + total).astype(bf16)
            hidden[:, columns] = value
            rows = jnp.dot(placing[...], value, preferred_element_type=f32).astype(bf16)
            leaving[lax.rem(j, 2), t] = rows.reshape(EXPERTS, BLOCK, WIDTH)
            for o in range(1, EXPERTS):
                row_copy(j, t, o).start()
            xg[k, my["z"], my["x"], pl.ds(pl.multiple_of(owner * BLOCK, BLOCK), BLOCK)] = leaving[
                lax.rem(j, 2), t, owner
            ]
            logits[...] += lax.dot_general(
                router_ref[:, columns],
                value,
                (((1,), (1,)), ((), ())),
                preferred_element_type=f32,
            )

    def rows_arrive(j):
        for t in range(2):
            rows_wait(j, t).wait_recv()

    def tokens_sent(j):
        for t in range(2):
            for i in range(1, GROUPS):
                term_copy(j, t, i).wait_send()
            rows_wait(j, t).wait_send()

    every = pl.ds(0, SIDE)
    halves = {1: pl.ds(0, SIDE // 2), -1: pl.ds(SIDE // 2, SIDE // 2)}
    half_rows = {1: pl.ds(0, HALF), -1: pl.ds(HALF, HALF)}
    axes = (("x", "z"), ("z", "x"))
    slot = {1: 0, -1: 1}

    def ag_copy(j, t, step, d, landing):
        near, far = axes[t]
        chunk = xg.at[2 * j + t]
        back = -d if landing else 0
        if step == 0:
            ref, to = along(near, chunk, around(near, back), my[far]), near
        elif step == 1:
            ref = along(near, chunk, around(near, -2 * d if landing else -d), my[far])
            ref, to = ref.at[half_rows[d]], near
        elif step == 2:
            ref, to = along(far, chunk, around(far, back), every), far
        else:
            ref = along(far, chunk, around(far, -2 * d if landing else -d), halves[d])
            to = far
        m = step * 2 + slot[d]
        return pltpu.make_async_remote_copy(
            src_ref=ref,
            dst_ref=ref,
            send_sem=ag_send.at[j, t, m],
            recv_sem=ag_recv.at[j, t, m],
            device_id=neighbour(to, d),
            device_id_type=MESH,
        )

    def ag_start(j, step):
        for t in range(2):
            for d in (1, -1):
                ag_copy(j, t, step, d, False).start()

    def ag_arrive(j, step):
        for t in range(2):
            for d in (1, -1):
                ag_copy(j, t, step, d, True).wait_recv()

    def ag_sent(j):
        for step in range(4):
            for t in range(2):
                for d in (1, -1):
                    ag_copy(j, t, step, d, False).wait_send()

    def gate_up(j, first):
        @pl.loop(0, SIDE * SIDE // 2)
        def _(b):
            zz, x0 = lax.div(b, 2), lax.rem(b, 2) * 2
            rows = pl.ds(pl.multiple_of(b * 2 * ROWS, 2 * ROWS), 2 * ROWS)
            for n, weight in enumerate((w_gate, w_up)):
                total = None
                for t in range(2):
                    k = 2 * j + t
                    left = xg[k, zz, pl.ds(x0, 2)].reshape(2 * ROWS, WIDTH)
                    right = weight[pl.ds(pl.multiple_of(k * WIDTH, WIDTH), WIDTH), :]
                    term = jnp.dot(left, right, preferred_element_type=jnp.float32)
                    total = term if total is None else total + term
                if first:
                    acc[n, rows, :] = total
                else:
                    acc[n, rows, :] += total

    fetch.wait()
    mix(0)
    mix(1)
    tokens(0)
    rows_arrive(0)
    ag_start(0, 0)
    tokens(1)
    ag_arrive(0, 0)
    ag_start(0, 1)
    tokens_sent(0)
    mix(2)
    ag_arrive(0, 1)
    ag_start(0, 2)
    for load in loads:
        load.wait()

    def ag_round(j, first):
        near_end = isinstance(j, int) and j > 1
        last = near_end and j == PAIRS - 1
        if not last:
            rows_arrive(j + 1)
            ag_start(j + 1, 0)
            if not (near_end and j + 2 >= PAIRS):
                tokens(j + 2)
        if not first:
            gate_up(j - 1, isinstance(j, int) and j == 1)
        if not last:
            ag_arrive(j + 1, 0)
            ag_start(j + 1, 1)
        ag_arrive(j, 2)
        if not first:
            ag_sent(j - 1)
        ag_start(j, 3)
        if not last:
            tokens_sent(j + 1)
            if not (near_end and j + 3 >= PAIRS):
                mix(j + 3)
            ag_arrive(j + 1, 1)
            ag_start(j + 1, 2)
        ag_arrive(j, 3)

    ag_round(0, True)
    ag_round(1, False)

    @pl.loop(2, PAIRS - 3)
    def _(j):
        ag_round(j, False)

    for j in range(PAIRS - 3, PAIRS):
        ag_round(j, False)
    gate_up(PAIRS - 1, False)

    @pl.loop(0, SIDE * SIDE)
    def _(b):
        rows = pl.ds(pl.multiple_of(b * ROWS, ROWS), ROWS)
        gate_val = acc[0, rows, :]
        act[rows, :] = (gate_val / (1.0 + jnp.exp(-gate_val)) * acc[1, rows, :]).astype(jnp.bfloat16)

    ag_sent(PAIRS - 1)

    def rs_copy(j, t, step, d):
        near, far = axes[t]
        p = part.at[lax.rem(j, 2), t]
        room = xg.at[2 * j + t]
        if step == 0:
            src = along(far, p, around(far, 2), halves[d])
            dst, to = room.at[0, halves[d]], far
        elif step == 1:
            src = along(far, p, around(far, d), every)
            dst, to = room.at[1 + slot[d]], far
        elif step == 2:
            src = line.at[lax.rem(j, 2), t, around(near, 2), half_rows[d]]
            dst, to = room.at[3, 0, half_rows[d]], near
        else:
            src = line.at[lax.rem(j, 2), t, around(near, d)]
            dst, to = room.at[3, 1 + slot[d]], near
        m = step * 2 + slot[d]
        return pltpu.make_async_remote_copy(
            src_ref=src,
            dst_ref=dst,
            send_sem=rs_send.at[j, t, m],
            recv_sem=rs_recv.at[j, t, m],
            device_id=neighbour(to, d),
            device_id_type=MESH,
        )

    def rs_start(j, step, t):
        for d in (1, -1):
            rs_copy(j, t, step, d).start()

    def rs_arrive(j, step, t):
        for d in (1, -1):
            rs_copy(j, t, step, d).wait_recv()

    def rs_sent(j):
        for step in range(4):
            for t in range(2):
                for d in (1, -1):
                    rs_copy(j, t, step, d).wait_send()

    def down(j):
        @pl.loop(0, SIDE * SIDE // 2)
        def _(b):
            zz, x0 = lax.div(b, 2), lax.rem(b, 2) * 2
            rows = pl.ds(pl.multiple_of(b * 2 * ROWS, 2 * ROWS), 2 * ROWS)
            for t in range(2):
                k = 2 * j + t
                right = w_down[pl.ds(pl.multiple_of(k * WIDTH, WIDTH), WIDTH), :]
                term = lax.dot_general(
                    act[rows, :], right, (((1,), (1,)), ((), ())), preferred_element_type=jnp.float32
                )
                part[lax.rem(j, 2), t, zz, pl.ds(x0, 2)] = term.astype(jnp.bfloat16).reshape(
                    2, ROWS, WIDTH
                )

    def back_copy(j, t, o):
        other, place = partner(o)
        return pltpu.make_async_remote_copy(
            src_ref=sums.at[lax.rem(j, 2), t, other],
            dst_ref=returned.at[2 * j + t, pl.ds(pl.multiple_of(owner * BLOCK, BLOCK), BLOCK)],
            send_sem=back_send.at[2 * j + t],
            recv_sem=back_recv.at[2 * j + t],
            device_id=place,
            device_id_type=MESH,
        )

    def back_wait(j, t):
        ref = returned.at[2 * j + t, pl.ds(0, ROWS - BLOCK)]
        return pltpu.make_async_remote_copy(
            src_ref=ref,
            dst_ref=ref,
            send_sem=back_send.at[2 * j + t],
            recv_sem=back_recv.at[2 * j + t],
            device_id=partner(1)[1],
            device_id_type=MESH,
        )

    def finish(j):
        for t in range(2):
            back_wait(j, t).wait_recv()
            columns = columns_of(2 * j + t)
            total = hidden[:, columns].astype(f32)
            for n in range(2):
                total = total + lax.dot_general(
                    shares[n],
                    returned[2 * j + t],
                    (((0,), (0,)), ((), ())),
                    preferred_element_type=f32,
                )
            out_ref[:, columns] = total.astype(bf16)

    def sums_sent(j):
        for t in range(2):
            back_wait(j, t).wait_send()

    def add_first(j, t):
        far, near = axes[t][1], axes[t][0]
        s = lax.rem(j, 2)
        for d in (1, -1):
            base = 0 if d == 1 else SIDE // 2
            place = around(far, d)

            @pl.loop(0, SIDE // 2)
            def _(i):
                at = (place, base + i) if far == "z" else (base + i, place)
                part[s, t, at[0], at[1]] = (
                    part[s, t, at[0], at[1]].astype(f32) + xg[2 * j + t, 0, base + i].astype(f32)
                ).astype(jnp.bfloat16)

    def add_line(j, t):
        far = axes[t][1]
        s = lax.rem(j, 2)

        @pl.loop(0, SIDE)
        def _(i):
            at = (my[far], i) if far == "z" else (i, my[far])
            line[s, t, i] = (
                part[s, t, at[0], at[1]].astype(f32)
                + xg[2 * j + t, 1, i].astype(f32)
                + xg[2 * j + t, 2, i].astype(f32)
            ).astype(jnp.bfloat16)

    def add_second(j, t):
        near = axes[t][0]
        s = lax.rem(j, 2)
        for d in (1, -1):
            at = around(near, d)
            line[s, t, at, half_rows[d]] = (
                line[s, t, at, half_rows[d]].astype(f32)
                + xg[2 * j + t, 3, 0, half_rows[d]].astype(f32)
            ).astype(jnp.bfloat16)

    def add_last(j, t):
        near = axes[t][0]
        s = lax.rem(j, 2)
        total = (
            line[s, t, my[near]].astype(f32)
            + xg[2 * j + t, 3, 1].astype(f32)
            + xg[2 * j + t, 3, 2].astype(f32)
        )
        sums[s, t] = total.astype(bf16).reshape(EXPERTS, BLOCK, WIDTH)
        for o in range(1, EXPERTS):
            back_copy(j, t, o).start()
        returned[2 * j + t, pl.ds(pl.multiple_of(owner * BLOCK, BLOCK), BLOCK)] = sums[s, t, owner]

    def rs_second(j):
        for t in range(2):
            rs_arrive(j, 1, t)
            add_line(j, t)
            rs_start(j, 2, t)

    def rs_third(j):
        for t in range(2):
            rs_arrive(j, 2, t)
            add_second(j, t)
            rs_start(j, 3, t)

    def rs_begin(j):
        for t in range(2):
            rs_arrive(j, 0, t)
            add_first(j, t)
            rs_start(j, 1, t)

    def rs_end(j):
        for t in range(2):
            rs_arrive(j, 3, t)
            add_last(j, t)
        rs_sent(j)

    def both(j):
        for t in range(2):
            rs_start(j, 0, t)

    down(0)
    both(0)
    down(1)

    match = [
        lax.broadcasted_iota(jnp.int32, (EXPERTS, TOKENS), 0) == chosen_ref[i : i + 1, :]
        for i in range(2)
    ]
    picked = [jnp.sum(jnp.where(m, logits[...], 0.0), axis=0, keepdims=True) for m in match]
    weights = jnp.zeros((ROWS, TOKENS), f32)
    for i in range(2):
        share = 1.0 / (1.0 + jnp.exp(picked[1 - i] - picked[i]))
        weights = weights + jnp.where(row_id == target[i : i + 1, :], share, 0.0)
    coarse = weights.astype(bf16)
    shares[0] = coarse
    shares[1] = (weights - coarse.astype(f32)).astype(bf16)

    rs_begin(0)
    both(1)

    def rs_round(j, first, last):
        rs_second(j)
        if not last:
            rs_begin(j + 1)
        rs_third(j)
        if not first:
            sums_sent(j - 1)
            finish(j - 1)
        rs_end(j)

    rs_round(0, True, False)
    down(2)
    both(2)

    @pl.loop(1, PAIRS - 2)
    def _(j):
        rs_round(j, False, False)
        down(j + 2)
        both(j + 2)

    rs_round(PAIRS - 2, False, False)
    rs_round(PAIRS - 1, False, True)
    sums_sent(PAIRS - 1)
    finish(PAIRS - 1)


def layer(normed, mix_w, residual, router, chosen, slots, spills, gate_w, up_w, down_w):
    hidden = gate_w.shape[1]
    length, inner = normed.shape
    bf16, f32 = jnp.bfloat16, jnp.float32
    any_space = pl.BlockSpec(memory_space=pl.ANY)
    vmem = pl.BlockSpec(memory_space=pltpu.VMEM)
    return pl.pallas_call(
        layer_kernel,
        out_shape=jax.ShapeDtypeStruct((TOKENS, D), bf16),
        in_specs=[any_space] * 2 + [vmem] * 5 + [any_space] * 3,
        out_specs=vmem,
        scratch_shapes=[
            pltpu.VMEM((length, inner), bf16),
            pltpu.VMEM((inner, D), bf16),
            pltpu.VMEM((2, 2, GROUPS, TOKENS, WIDTH), bf16),
            pltpu.VMEM((2 * PAIRS, GROUPS - 1, TOKENS, WIDTH), bf16),
            pltpu.VMEM((TOKENS, D), bf16),
            pltpu.VMEM((ROWS, TOKENS), bf16),
            pltpu.VMEM((2, ROWS, TOKENS), bf16),
            pltpu.VMEM((EXPERTS, TOKENS), f32),
            pltpu.VMEM((2, 2, EXPERTS, BLOCK, WIDTH), bf16),
            pltpu.VMEM((2, 2, EXPERTS, BLOCK, WIDTH), bf16),
            pltpu.VMEM((2 * PAIRS, ROWS, WIDTH), bf16),
            pltpu.VMEM((2 * PAIRS, SIDE, SIDE, ROWS, WIDTH), bf16),
            pltpu.VMEM((2, SIDE * SIDE * ROWS, hidden), f32),
            pltpu.VMEM((SIDE * SIDE * ROWS, hidden), bf16),
            pltpu.VMEM((D, hidden), bf16),
            pltpu.VMEM((D, hidden), bf16),
            pltpu.VMEM((D, hidden), bf16),
            pltpu.VMEM((2, 2, SIDE, SIDE, ROWS, WIDTH), bf16),
            pltpu.VMEM((2, 2, SIDE, ROWS, WIDTH), bf16),
            pltpu.SemaphoreType.DMA((PAIRS, 2, 8)),
            pltpu.SemaphoreType.DMA((PAIRS, 2, 8)),
            pltpu.SemaphoreType.DMA((PAIRS, 2, 8)),
            pltpu.SemaphoreType.DMA((PAIRS, 2, 8)),
            pltpu.SemaphoreType.DMA((2 * PAIRS, GROUPS - 1)),
            pltpu.SemaphoreType.DMA((2 * PAIRS, GROUPS - 1)),
            pltpu.SemaphoreType.DMA((2 * PAIRS,)),
            pltpu.SemaphoreType.DMA((2 * PAIRS,)),
            pltpu.SemaphoreType.DMA((2 * PAIRS,)),
            pltpu.SemaphoreType.DMA((2 * PAIRS,)),
            pltpu.SemaphoreType.DMA((3,)),
            pltpu.SemaphoreType.DMA((PAIRS,)),
            pltpu.SemaphoreType.DMA,
        ],
        compiler_params=pltpu.CompilerParams(
            collective_id=0, has_side_effects=True, vmem_limit_bytes=62 << 20
        ),
        cost_estimate=pl.CostEstimate(
            flops=6 * 2048 * D * 512, bytes_accessed=24 << 20, transcendentals=1 << 20
        ),
    )(normed, mix_w, residual, router, chosen, slots, spills, gate_w, up_w, down_w)


HEADS = 16
SIZE = 64
STATE = 128
CTX = SIDE * SIDE
MESSAGE = SIZE + 16


def scan_kernel(
    mixer_ref,
    gate_ref,
    write_ref,
    read_ref,
    decay_ref,
    skip_ref,
    gain_ref,
    start_ref,
    out_ref,
    leaving,
    gathered,
    entering,
    returned,
    start,
    acc,
    out_send,
    out_recv,
    back_send,
    back_recv,
    start_sem,
):
    here = lax.axis_index("ctx")
    f32, bf16 = jnp.float32, jnp.bfloat16
    length = mixer_ref.shape[0]
    mine = pltpu.make_async_copy(
        start_ref.at[pl.ds(pl.multiple_of(here * SIZE, SIZE), SIZE), :], start, start_sem
    )
    mine.start()

    barrier = pltpu.get_barrier_semaphore()

    def greet(k, _):
        other = lax.rem(here + k, CTX)
        pl.semaphore_signal(barrier, inc=1, device_id={"ctx": other}, device_id_type=MESH)
        return 0

    lax.fori_loop(1, CTX, greet, 0)

    row_id = lax.broadcasted_iota(jnp.int32, (length, length), 0)
    col_id = lax.broadcasted_iota(jnp.int32, (length, length), 1)
    causal = row_id >= col_id
    upper = jnp.where(row_id <= col_id, 1.0, 0.0).astype(f32)
    levels = jnp.dot(
        decay_ref[...], upper, precision=lax.Precision.HIGHEST, preferred_element_type=f32
    )
    last = levels[:, length - 1 : length]
    to_end = jnp.exp(levels - last).T
    total = jnp.exp(-last)
    levels_t = levels.T
    from_start = jnp.exp(-levels_t)
    low = lax.broadcasted_iota(jnp.int32, (length, 2 * SIZE), 1) < SIZE
    top = lax.broadcasted_iota(jnp.int32, (16, STATE), 0) < 8

    def spread(columns, q):
        return jnp.where(low, columns[:, 2 * q : 2 * q + 1], columns[:, 2 * q + 1 : 2 * q + 2])

    for q in range(HEADS // 2):
        lanes = pl.ds(q * 2 * SIZE, 2 * SIZE)
        scaled = (spread(to_end, q) * mixer_ref[:, lanes].astype(f32)).astype(bf16)
        local = lax.dot_general(
            scaled, write_ref[...], (((0,), (0,)), ((), ())), preferred_element_type=f32
        )
        for i in range(2):
            h = 2 * q + i
            leaving[h, 0:SIZE] = local[i * SIZE : (i + 1) * SIZE].astype(bf16)
            value = jnp.broadcast_to(total[h : h + 1, :], (16, STATE))
            coarse = value.astype(bf16)
            rest = (value - coarse.astype(f32)).astype(bf16)
            leaving[h, SIZE:MESSAGE] = jnp.where(top, coarse, rest)

    pl.semaphore_wait(barrier, CTX - 1)

    def out_copy(k):
        other = lax.rem(here + k, CTX)
        return pltpu.make_async_remote_copy(
            src_ref=leaving.at[other],
            dst_ref=gathered.at[here],
            send_sem=out_send.at[k],
            recv_sem=out_recv.at[k],
            device_id={"ctx": other},
            device_id_type=MESH,
        )

    def back_copy(k):
        other = lax.rem(here + k, CTX)
        return pltpu.make_async_remote_copy(
            src_ref=entering.at[other],
            dst_ref=returned.at[here],
            send_sem=back_send.at[k],
            recv_sem=back_recv.at[k],
            device_id={"ctx": other},
            device_id_type=MESH,
        )

    def each(action):
        def step(k, _):
            action(k)
            return 0

        lax.fori_loop(1, CTX, step, 0)

    each(lambda k: out_copy(k).start())
    gathered[here] = leaving[here]

    meet = lax.dot_general(
        read_ref[...], write_ref[...], (((1,), (1,)), ((), ())), preferred_element_type=f32
    )

    def within(q):
        lanes = pl.ds(q * 2 * SIZE, 2 * SIZE)
        pair = mixer_ref[:, lanes]
        halves = []
        for i in range(2):
            h = 2 * q + i
            span = levels[h : h + 1, :] - levels_t[:, h : h + 1]
            weight = jnp.exp(jnp.where(causal, span, -1e30)) * meet
            halves.append(jnp.dot(weight.astype(bf16), pair, preferred_element_type=f32))
        skip = jnp.where(low, skip_ref[2 * q], skip_ref[2 * q + 1])
        acc[:, lanes] = jnp.where(low, halves[0], halves[1]) + skip * pair.astype(f32)

    EARLY = 3
    for q in range(EARLY):
        within(q)

    mine.wait()
    each(lambda k: out_copy(k).wait_recv())
    state = start[...]
    for k in range(CTX):
        entering[k] = state.astype(bf16)
        if k < CTX - 1:
            factor = gathered[k, SIZE:MESSAGE].astype(f32)
            factor = factor[0:1, :] + factor[8:9, :]
            state = factor * state + gathered[k, 0:SIZE].astype(f32)
    each(lambda k: back_copy(k).start())
    returned[here] = entering[here]

    for q in range(EARLY, HEADS // 2):
        within(q)

    each(lambda k: back_copy(k).wait_recv())
    square = jnp.zeros((length, 1), f32)
    for q in range(HEADS // 2):
        lanes = pl.ds(q * 2 * SIZE, 2 * SIZE)
        entered = returned[2 * q : 2 * q + 2].reshape(2 * SIZE, STATE)
        carried = lax.dot_general(
            read_ref[...], entered, (((1,), (1,)), ((), ())), preferred_element_type=f32
        )
        gate = gate_ref[:, lanes].astype(f32)
        gated = (acc[:, lanes] + carried * spread(from_start, q)) * (gate / (1.0 + jnp.exp(-gate)))
        acc[:, lanes] = gated
        square = square + jnp.sum(gated * gated, axis=1, keepdims=True)
    scale = lax.rsqrt(square / (HEADS * SIZE) + 1e-05)
    for q in range(HEADS // 2):
        lanes = pl.ds(q * 2 * SIZE, 2 * SIZE)
        out_ref[:, lanes] = (acc[:, lanes] * scale * gain_ref[:, lanes]).astype(bf16)

    each(lambda k: out_copy(k).wait_send())
    each(lambda k: back_copy(k).wait_send())


def scan(mixer, gate, write, read, decay, skip, gain, start_state):
    length, inner = mixer.shape
    f32, bf16 = jnp.float32, jnp.bfloat16
    vmem = pl.BlockSpec(memory_space=pltpu.VMEM)
    return pl.pallas_call(
        scan_kernel,
        out_shape=jax.ShapeDtypeStruct((length, inner), bf16),
        in_specs=[vmem] * 5
        + [
            pl.BlockSpec(memory_space=pltpu.SMEM),
            vmem,
            pl.BlockSpec(memory_space=pl.ANY),
        ],
        out_specs=vmem,
        scratch_shapes=[
            pltpu.VMEM((CTX, MESSAGE, STATE), bf16),
            pltpu.VMEM((CTX, MESSAGE, STATE), bf16),
            pltpu.VMEM((CTX, SIZE, STATE), bf16),
            pltpu.VMEM((CTX, SIZE, STATE), bf16),
            pltpu.VMEM((SIZE, STATE), f32),
            pltpu.VMEM((length, inner), f32),
            pltpu.SemaphoreType.DMA((CTX,)),
            pltpu.SemaphoreType.DMA((CTX,)),
            pltpu.SemaphoreType.DMA((CTX,)),
            pltpu.SemaphoreType.DMA((CTX,)),
            pltpu.SemaphoreType.DMA,
        ],
        compiler_params=pltpu.CompilerParams(
            collective_id=1, has_side_effects=True, vmem_limit_bytes=60 << 20
        ),
        cost_estimate=pl.CostEstimate(
            flops=1 << 29, bytes_accessed=4 << 20, transcendentals=1 << 20
        ),
    )(mixer, gate, write, read, decay, skip, gain, start_state)


def shards(
    mixer_in,
    gate_in,
    state_write,
    state_read,
    decay_rate,
    skip_gain,
    norm_gain,
    start_state,
    out_weight,
    residual,
    router_weight,
    chosen,
    slot_index,
    spill_index,
    gate_weight,
    up_weight,
    down_weight,
):
    normed = scan(
        mixer_in[0],
        gate_in[0],
        state_write[0, :, 0],
        state_read[0, :, 0],
        decay_rate[0],
        skip_gain,
        norm_gain[None],
        start_state[0].reshape(HEADS * SIZE, STATE),
    )
    return layer(
        normed,
        out_weight,
        residual[0],
        router_weight.T,
        chosen[0].T,
        slot_index[0].T,
        spill_index[0].T,
        gate_weight[0],
        up_weight[0],
        down_weight[0],
    )[None]


def solution(mesh):
    placed = (
        P("dp", "ctx", "exp"),
        P("dp", "ctx", "exp"),
        P("dp", "ctx", "exp", None),
        P("dp", "ctx", "exp", None),
        P("dp", "exp", "ctx"),
        P("exp"),
        P("exp"),
        P("dp", "exp", None, None),
        P("exp", None),
        P("dp", ("ctx", "exp"), None),
        P(),
        P("dp", ("ctx", "exp"), None),
        P("dp", ("ctx", "exp"), None),
        P("dp", ("ctx", "exp"), None),
        P(("exp", "dp"), None, "ctx"),
        P(("exp", "dp"), None, "ctx"),
        P(("exp", "dp"), None, "ctx"),
    )
    return jax.shard_map(
        shards, mesh=mesh, in_specs=placed, out_specs=P("dp", ("ctx", "exp"), None), check_vma=False
    )
```

```python
import functools

import jax
import jax.numpy as jnp
from jax import lax
from jax.experimental import pallas as pl
from jax.experimental.pallas import tpu as pltpu
from jax.sharding import PartitionSpec as P

D = 4096
EXPERTS = 8
CAP = 14
SPILL = 2
BLOCK = 16
SIDE = 4
ROWS = EXPERTS * BLOCK
WIDTH = 256
PAIRS = D // WIDTH // 2
HALF = ROWS // 2
TOKENS = 64
GROUPS = 4
MESH = pl.DeviceIdType.MESH


def layer_kernel(
    normed_ref,
    mix_ref,
    residual_ref,
    router_ref,
    chosen_ref,
    slot_ref,
    spill_ref,
    gate_ref,
    up_ref,
    down_ref,
    out_ref,
    normed,
    mixed,
    terms,
    hidden,
    placing,
    shares,
    logits,
    leaving,
    sums,
    returned,
    xg,
    acc,
    act,
    w_gate,
    w_up,
    w_down,
    part,
    line,
    ag_send,
    ag_recv,
    rs_send,
    rs_recv,
    mix_send,
    mix_recv,
    row_send,
    row_recv,
    back_send,
    back_recv,
    load_sem,
    mix_sem,
    normed_sem,
):
    here = lax.axis_index("ctx")
    my = {"x": lax.rem(here, SIDE), "z": lax.div(here, SIDE)}

    def around(axis, step):
        return lax.rem(my[axis] + step + SIDE, SIDE)

    def neighbour(axis, step):
        other = around(axis, step)
        if axis == "x":
            return {"ctx": my["z"] * SIDE + other}
        return {"ctx": other * SIDE + my["x"]}

    def along(axis, ref, place, at):
        if axis == "z":
            return ref.at[place, at]
        return ref.at[at, place]

    f32, bf16 = jnp.float32, jnp.bfloat16
    my_exp, my_dp = lax.axis_index("exp"), lax.axis_index("dp")
    owner = my_exp * 2 + my_dp

    def columns_of(k):
        return pl.ds(pl.multiple_of(k * WIDTH, WIDTH), WIDTH)

    fetch = pltpu.make_async_copy(normed_ref, normed, normed_sem)
    fetch.start()

    def mix_room(k):
        slot, rest = lax.div(k, 4), lax.rem(k, 4)
        return part.at[slot, lax.div(rest, 2), pl.ds(lax.rem(rest, 2) * 2, 2)]

    def mix_load(k):
        return pltpu.make_async_copy(
            mix_ref.at[:, :, :, columns_of(k)], mix_room(k), mix_sem.at[k]
        )

    def load_mix(k, _):
        mix_load(k).start()
        return 0

    lax.fori_loop(0, 2 * PAIRS, load_mix, 0)
    loads = [
        pltpu.make_async_copy(src, dst, load_sem.at[i])
        for i, (src, dst) in enumerate(((gate_ref, w_gate), (up_ref, w_up), (down_ref, w_down)))
    ]
    for load in loads:
        load.start()

    def partner(o):
        other = lax.rem(owner + o, EXPERTS)
        return other, {"exp": lax.div(other, 2), "dp": lax.rem(other, 2)}

    barrier = pltpu.get_barrier_semaphore()
    for axis in ("x", "z"):
        for step in (1, -1):
            pl.semaphore_signal(
                barrier, inc=1, device_id=neighbour(axis, step), device_id_type=MESH
            )
    for o in range(1, EXPERTS):
        pl.semaphore_signal(barrier, inc=1, device_id=partner(o)[1], device_id_type=MESH)

    row_id = lax.broadcasted_iota(jnp.int32, (ROWS, TOKENS), 0)
    expert_ids, slot_ids, spill_ids = chosen_ref[...], slot_ref[...], spill_ref[...]
    target = jnp.where(
        slot_ids >= 0,
        expert_ids * BLOCK + slot_ids,
        jnp.where(
            spill_ids >= 0,
            jnp.right_shift(spill_ids, 1) * BLOCK + CAP + jnp.bitwise_and(spill_ids, 1),
            -1,
        ),
    )
    places = [row_id == target[i : i + 1, :] for i in range(2)]
    placing[...] = (places[0].astype(f32) + places[1].astype(f32)).astype(bf16)
    logits[...] = jnp.zeros_like(logits)
    pl.semaphore_wait(barrier, 4 + EXPERTS - 1)

    def term_copy(j, t, i):
        other = lax.rem(my_exp + i, GROUPS)
        return pltpu.make_async_remote_copy(
            src_ref=mixed.at[lax.rem(j, 2), t, other],
            dst_ref=terms.at[2 * j + t, i - 1],
            send_sem=mix_send.at[2 * j + t, i - 1],
            recv_sem=mix_recv.at[2 * j + t, i - 1],
            device_id={"exp": other},
            device_id_type=MESH,
        )

    def mix(j):
        for t in range(2):
            mix_load(2 * j + t).wait()
            term = jnp.dot(
                normed[...],
                mix_room(2 * j + t)[...].reshape(normed.shape[1], WIDTH),
                preferred_element_type=f32,
            )
            mixed[lax.rem(j, 2), t] = term.astype(bf16).reshape(GROUPS, TOKENS, WIDTH)
            for i in range(1, GROUPS):
                term_copy(j, t, i).start()

    def row_copy(j, t, o):
        other, place = partner(o)
        return pltpu.make_async_remote_copy(
            src_ref=leaving.at[lax.rem(j, 2), t, other],
            dst_ref=xg.at[
                2 * j + t, my["z"], my["x"], pl.ds(pl.multiple_of(owner * BLOCK, BLOCK), BLOCK)
            ],
            send_sem=row_send.at[2 * j + t],
            recv_sem=row_recv.at[2 * j + t],
            device_id=place,
            device_id_type=MESH,
        )

    def rows_wait(j, t):
        ref = xg.at[2 * j + t, my["z"], my["x"], pl.ds(0, ROWS - BLOCK)]
        return pltpu.make_async_remote_copy(
            src_ref=ref,
            dst_ref=ref,
            send_sem=row_send.at[2 * j + t],
            recv_sem=row_recv.at[2 * j + t],
            device_id=partner(1)[1],
            device_id_type=MESH,
        )

    def tokens(j):
        for t in range(2):
            k = 2 * j + t
            columns = columns_of(k)
            for i in range(1, GROUPS):
                term_copy(j, t, i).wait_recv()
            total = mixed[lax.rem(j, 2), t, my_exp].astype(f32)
            for i in range(1, GROUPS):
                total = total + terms[k, i - 1].astype(f32)
            value = (residual_ref[:, columns].astype(f32) + total).astype(bf16)
            hidden[:, columns] = value
            rows = jnp.dot(placing[...], value, preferred_element_type=f32).astype(bf16)
            leaving[lax.rem(j, 2), t] = rows.reshape(EXPERTS, BLOCK, WIDTH)
            for o in range(1, EXPERTS):
                row_copy(j, t, o).start()
            xg[k, my["z"], my["x"], pl.ds(pl.multiple_of(owner * BLOCK, BLOCK), BLOCK)] = leaving[
                lax.rem(j, 2), t, owner
            ]
            logits[...] += lax.dot_general(
                router_ref[:, columns],
                value,
                (((1,), (1,)), ((), ())),
                preferred_element_type=f32,
            )

    def rows_arrive(j):
        for t in range(2):
            rows_wait(j, t).wait_recv()

    def terms_sent(j):
        for t in range(2):
            for i in range(1, GROUPS):
                term_copy(j, t, i).wait_send()

    def rows_sent(j):
        for t in range(2):
            rows_wait(j, t).wait_send()

    every = pl.ds(0, SIDE)
    halves = {1: pl.ds(0, SIDE // 2), -1: pl.ds(SIDE // 2, SIDE // 2)}
    half_rows = {1: pl.ds(0, HALF), -1: pl.ds(HALF, HALF)}
    axes = (("x", "z"), ("z", "x"))
    slot = {1: 0, -1: 1}

    def ag_copy(j, t, step, d, landing):
        near, far = axes[t]
        chunk = xg.at[2 * j + t]
        back = -d if landing else 0
        if step == 0:
            ref, to = along(near, chunk, around(near, back), my[far]), near
        elif step == 1:
            ref = along(near, chunk, around(near, -2 * d if landing else -d), my[far])
            ref, to = ref.at[half_rows[d]], near
        elif step == 2:
            ref, to = along(far, chunk, around(far, back), every), far
        else:
            ref = along(far, chunk, around(far, -2 * d if landing else -d), halves[d])
            to = far
        m = step * 2 + slot[d]
        return pltpu.make_async_remote_copy(
            src_ref=ref,
            dst_ref=ref,
            send_sem=ag_send.at[j, t, m],
            recv_sem=ag_recv.at[j, t, m],
            device_id=neighbour(to, d),
            device_id_type=MESH,
        )

    def ag_start(j, step):
        for t in range(2):
            for d in (1, -1):
                ag_copy(j, t, step, d, False).start()

    def ag_arrive(j, step):
        for t in range(2):
            for d in (1, -1):
                ag_copy(j, t, step, d, True).wait_recv()

    def ag_sent(j):
        for step in range(4):
            for t in range(2):
                for d in (1, -1):
                    ag_copy(j, t, step, d, False).wait_send()

    def gate_up(j):
        @pl.loop(0, SIDE)
        def _(zz):
            rows = pl.ds(pl.multiple_of(zz * SIDE * ROWS, SIDE * ROWS), SIDE * ROWS)
            for n, weight in enumerate((w_gate, w_up)):
                total = acc[n, rows, :]
                for t in range(2):
                    k = 2 * j + t
                    total += jnp.dot(
                        xg[k, zz].reshape(SIDE * ROWS, WIDTH),
                        weight[columns_of(k), :],
                        preferred_element_type=f32,
                    )
                acc[n, rows, :] = total

    def stages(tick, count, steps):
        for lag, action in steps:
            pl.when(jnp.logical_and(tick >= lag, tick < count + lag))(
                functools.partial(action, tick - lag)
            )

    def gather_first(j):
        rows_arrive(j)
        ag_start(j, 0)
        terms_sent(j)

    def gather_second(j):
        ag_arrive(j, 0)
        ag_start(j, 1)
        rows_sent(j)

    def gather_third(j):
        ag_arrive(j, 1)
        ag_start(j, 2)

    def gather_last(j):
        ag_arrive(j, 2)
        ag_start(j, 3)

    def gathered(j):
        ag_arrive(j, 3)
        ag_sent(j)
        gate_up(j)

    acc[...] = jnp.zeros_like(acc)
    fetch.wait()
    mix(0)
    for load in loads:
        load.wait()

    @pl.loop(1, PAIRS + 7)
    def _(tick):
        stages(
            tick,
            PAIRS,
            (
                (6, gather_last),
                (4, gather_third),
                (3, gather_second),
                (2, gather_first),
                (1, tokens),
                (0, mix),
                (7, gathered),
            ),
        )

    @pl.loop(0, SIDE * SIDE)
    def _(b):
        rows = pl.ds(pl.multiple_of(b * ROWS, ROWS), ROWS)
        gate_val = acc[0, rows, :]
        act[rows, :] = (gate_val / (1.0 + jnp.exp(-gate_val)) * acc[1, rows, :]).astype(jnp.bfloat16)

    def rs_copy(j, t, step, d):
        near, far = axes[t]
        p = part.at[lax.rem(j, 4), t]
        room = xg.at[2 * j + t]
        if step == 0:
            src = along(far, p, around(far, 2), halves[d])
            dst, to = room.at[0, halves[d]], far
        elif step == 1:
            src = along(far, p, around(far, d), every)
            dst, to = room.at[1 + slot[d]], far
        elif step == 2:
            src = line.at[lax.rem(j, 4), t, around(near, 2), half_rows[d]]
            dst, to = room.at[3, 0, half_rows[d]], near
        else:
            src = line.at[lax.rem(j, 4), t, around(near, d)]
            dst, to = room.at[3, 1 + slot[d]], near
        m = step * 2 + slot[d]
        return pltpu.make_async_remote_copy(
            src_ref=src,
            dst_ref=dst,
            send_sem=rs_send.at[j, t, m],
            recv_sem=rs_recv.at[j, t, m],
            device_id=neighbour(to, d),
            device_id_type=MESH,
        )

    def rs_start(j, step, t):
        for d in (1, -1):
            rs_copy(j, t, step, d).start()

    def rs_arrive(j, step, t):
        for d in (1, -1):
            rs_copy(j, t, step, d).wait_recv()

    def rs_sent(j, steps):
        for step in steps:
            for t in range(2):
                for d in (1, -1):
                    rs_copy(j, t, step, d).wait_send()

    def down(j):
        @pl.loop(0, SIDE)
        def _(zz):
            rows = pl.ds(pl.multiple_of(zz * SIDE * ROWS, SIDE * ROWS), SIDE * ROWS)
            for t in range(2):
                term = lax.dot_general(
                    act[rows, :],
                    w_down[columns_of(2 * j + t), :],
                    (((1,), (1,)), ((), ())),
                    preferred_element_type=f32,
                )
                part[lax.rem(j, 4), t, zz] = term.astype(bf16).reshape(SIDE, ROWS, WIDTH)

    def back_copy(j, t, o):
        other, place = partner(o)
        return pltpu.make_async_remote_copy(
            src_ref=sums.at[lax.rem(j, 2), t, other],
            dst_ref=returned.at[2 * j + t, pl.ds(pl.multiple_of(owner * BLOCK, BLOCK), BLOCK)],
            send_sem=back_send.at[2 * j + t],
            recv_sem=back_recv.at[2 * j + t],
            device_id=place,
            device_id_type=MESH,
        )

    def back_wait(j, t):
        ref = returned.at[2 * j + t, pl.ds(0, ROWS - BLOCK)]
        return pltpu.make_async_remote_copy(
            src_ref=ref,
            dst_ref=ref,
            send_sem=back_send.at[2 * j + t],
            recv_sem=back_recv.at[2 * j + t],
            device_id=partner(1)[1],
            device_id_type=MESH,
        )

    def finish(j):
        for t in range(2):
            back_wait(j, t).wait_recv()
            columns = columns_of(2 * j + t)
            total = hidden[:, columns].astype(f32)
            for n in range(2):
                total = total + lax.dot_general(
                    shares[n],
                    returned[2 * j + t],
                    (((0,), (0,)), ((), ())),
                    preferred_element_type=f32,
                )
            out_ref[:, columns] = total.astype(bf16)

    def sums_sent(j):
        for t in range(2):
            back_wait(j, t).wait_send()

    def add_first(j, t):
        far, near = axes[t][1], axes[t][0]
        s = lax.rem(j, 4)
        for d in (1, -1):
            base = 0 if d == 1 else SIDE // 2
            place = around(far, d)

            @pl.loop(0, SIDE // 2)
            def _(i):
                at = (place, base + i) if far == "z" else (base + i, place)
                part[s, t, at[0], at[1]] = (
                    part[s, t, at[0], at[1]].astype(f32) + xg[2 * j + t, 0, base + i].astype(f32)
                ).astype(jnp.bfloat16)

    def add_line(j, t):
        far = axes[t][1]
        s = lax.rem(j, 4)

        @pl.loop(0, SIDE)
        def _(i):
            at = (my[far], i) if far == "z" else (i, my[far])
            line[s, t, i] = (
                part[s, t, at[0], at[1]].astype(f32)
                + xg[2 * j + t, 1, i].astype(f32)
                + xg[2 * j + t, 2, i].astype(f32)
            ).astype(jnp.bfloat16)

    def add_second(j, t):
        near = axes[t][0]
        s = lax.rem(j, 4)
        for d in (1, -1):
            at = around(near, d)
            line[s, t, at, half_rows[d]] = (
                line[s, t, at, half_rows[d]].astype(f32)
                + xg[2 * j + t, 3, 0, half_rows[d]].astype(f32)
            ).astype(jnp.bfloat16)

    def add_last(j, t):
        near = axes[t][0]
        s = lax.rem(j, 4)
        total = (
            line[s, t, my[near]].astype(f32)
            + xg[2 * j + t, 3, 1].astype(f32)
            + xg[2 * j + t, 3, 2].astype(f32)
        )
        s = lax.rem(j, 2)
        sums[s, t] = total.astype(bf16).reshape(EXPERTS, BLOCK, WIDTH)
        for o in range(1, EXPERTS):
            back_copy(j, t, o).start()
        returned[2 * j + t, pl.ds(pl.multiple_of(owner * BLOCK, BLOCK), BLOCK)] = sums[s, t, owner]

    def sum_start(j):
        down(j)
        for t in range(2):
            rs_start(j, 0, t)

    def sum_first(j):
        for t in range(2):
            rs_arrive(j, 0, t)
            add_first(j, t)
            rs_start(j, 1, t)

    def sum_second(j):
        for t in range(2):
            rs_arrive(j, 1, t)
            add_line(j, t)
            rs_start(j, 2, t)
        rs_sent(j, (0, 1))

    def sum_third(j):
        for t in range(2):
            rs_arrive(j, 2, t)
            add_second(j, t)
            rs_start(j, 3, t)

    def sum_last(j):
        for t in range(2):
            rs_arrive(j, 3, t)
            add_last(j, t)
        rs_sent(j, (2, 3))

    def sum_back(j):
        finish(j)
        sums_sent(j)

    def weigh():
        match = [
            lax.broadcasted_iota(jnp.int32, (EXPERTS, TOKENS), 0) == chosen_ref[i : i + 1, :]
            for i in range(2)
        ]
        picked = [jnp.sum(jnp.where(m, logits[...], 0.0), axis=0, keepdims=True) for m in match]
        weights = jnp.zeros((ROWS, TOKENS), f32)
        for i in range(2):
            share = 1.0 / (1.0 + jnp.exp(picked[1 - i] - picked[i]))
            weights = weights + jnp.where(row_id == target[i : i + 1, :], share, 0.0)
        coarse = weights.astype(bf16)
        shares[0] = coarse
        shares[1] = (weights - coarse.astype(f32)).astype(bf16)

    sum_start(0)
    weigh()

    @pl.loop(1, PAIRS + 7)
    def _(tick):
        stages(
            tick,
            PAIRS,
            (
                (4, sum_second),
                (2, sum_first),
                (0, sum_start),
                (5, sum_third),
                (6, sum_last),
                (7, sum_back),
            ),
        )


def layer(normed, mix_w, residual, router, chosen, slots, spills, gate_w, up_w, down_w):
    hidden = gate_w.shape[1]
    length, inner = normed.shape
    bf16, f32 = jnp.bfloat16, jnp.float32
    any_space = pl.BlockSpec(memory_space=pl.ANY)
    vmem = pl.BlockSpec(memory_space=pltpu.VMEM)
    return pl.pallas_call(
        layer_kernel,
        out_shape=jax.ShapeDtypeStruct((TOKENS, D), bf16),
        in_specs=[any_space] * 2 + [vmem] * 5 + [any_space] * 3,
        out_specs=vmem,
        scratch_shapes=[
            pltpu.VMEM((length, inner), bf16),
            pltpu.VMEM((2, 2, GROUPS, TOKENS, WIDTH), bf16),
            pltpu.VMEM((2 * PAIRS, GROUPS - 1, TOKENS, WIDTH), bf16),
            pltpu.VMEM((TOKENS, D), bf16),
            pltpu.VMEM((ROWS, TOKENS), bf16),
            pltpu.VMEM((2, ROWS, TOKENS), bf16),
            pltpu.VMEM((EXPERTS, TOKENS), f32),
            pltpu.VMEM((2, 2, EXPERTS, BLOCK, WIDTH), bf16),
            pltpu.VMEM((2, 2, EXPERTS, BLOCK, WIDTH), bf16),
            pltpu.VMEM((2 * PAIRS, ROWS, WIDTH), bf16),
            pltpu.VMEM((2 * PAIRS, SIDE, SIDE, ROWS, WIDTH), bf16),
            pltpu.VMEM((2, SIDE * SIDE * ROWS, hidden), f32),
            pltpu.VMEM((SIDE * SIDE * ROWS, hidden), bf16),
            pltpu.VMEM((D, hidden), bf16),
            pltpu.VMEM((D, hidden), bf16),
            pltpu.VMEM((D, hidden), bf16),
            pltpu.VMEM((4, 2, SIDE, SIDE, ROWS, WIDTH), bf16),
            pltpu.VMEM((4, 2, SIDE, ROWS, WIDTH), bf16),
            pltpu.SemaphoreType.DMA((PAIRS, 2, 8)),
            pltpu.SemaphoreType.DMA((PAIRS, 2, 8)),
            pltpu.SemaphoreType.DMA((PAIRS, 2, 8)),
            pltpu.SemaphoreType.DMA((PAIRS, 2, 8)),
            pltpu.SemaphoreType.DMA((2 * PAIRS, GROUPS - 1)),
            pltpu.SemaphoreType.DMA((2 * PAIRS, GROUPS - 1)),
            pltpu.SemaphoreType.DMA((2 * PAIRS,)),
            pltpu.SemaphoreType.DMA((2 * PAIRS,)),
            pltpu.SemaphoreType.DMA((2 * PAIRS,)),
            pltpu.SemaphoreType.DMA((2 * PAIRS,)),
            pltpu.SemaphoreType.DMA((3,)),
            pltpu.SemaphoreType.DMA((2 * PAIRS,)),
            pltpu.SemaphoreType.DMA,
        ],
        compiler_params=pltpu.CompilerParams(
            collective_id=0, has_side_effects=True, vmem_limit_bytes=62 << 20
        ),
        cost_estimate=pl.CostEstimate(
            flops=6 * 2048 * D * 512, bytes_accessed=24 << 20, transcendentals=1 << 20
        ),
    )(normed, mix_w, residual, router, chosen, slots, spills, gate_w, up_w, down_w)


HEADS = 16
SIZE = 64
STATE = 128
CTX = SIDE * SIDE
MESSAGE = SIZE + 16


def scan_kernel(
    mixer_ref,
    gate_ref,
    write_ref,
    read_ref,
    decay_ref,
    skip_ref,
    gain_ref,
    start_ref,
    out_ref,
    leaving,
    gathered,
    entering,
    returned,
    start,
    acc,
    out_send,
    out_recv,
    back_send,
    back_recv,
    start_sem,
):
    here = lax.axis_index("ctx")
    f32, bf16 = jnp.float32, jnp.bfloat16
    length = mixer_ref.shape[0]
    mine = pltpu.make_async_copy(
        start_ref.at[pl.ds(pl.multiple_of(here * SIZE, SIZE), SIZE), :], start, start_sem
    )
    mine.start()

    barrier = pltpu.get_barrier_semaphore()

    def greet(k, _):
        other = lax.rem(here + k, CTX)
        pl.semaphore_signal(barrier, inc=1, device_id={"ctx": other}, device_id_type=MESH)
        return 0

    lax.fori_loop(1, CTX, greet, 0)

    row_id = lax.broadcasted_iota(jnp.int32, (length, length), 0)
    col_id = lax.broadcasted_iota(jnp.int32, (length, length), 1)
    causal = row_id >= col_id
    upper = jnp.where(row_id <= col_id, 1.0, 0.0).astype(f32)
    levels = jnp.dot(
        decay_ref[...], upper, precision=lax.Precision.HIGHEST, preferred_element_type=f32
    )
    last = levels[:, length - 1 : length]
    to_end = jnp.exp(levels - last).T
    total = jnp.exp(-last)
    levels_t = levels.T
    from_start = jnp.exp(-levels_t)
    low = lax.broadcasted_iota(jnp.int32, (length, 2 * SIZE), 1) < SIZE
    top = lax.broadcasted_iota(jnp.int32, (16, STATE), 0) < 8

    def spread(columns, q):
        return jnp.where(low, columns[:, 2 * q : 2 * q + 1], columns[:, 2 * q + 1 : 2 * q + 2])

    for q in range(HEADS // 2):
        lanes = pl.ds(q * 2 * SIZE, 2 * SIZE)
        scaled = (spread(to_end, q) * mixer_ref[:, lanes].astype(f32)).astype(bf16)
        local = lax.dot_general(
            scaled, write_ref[...], (((0,), (0,)), ((), ())), preferred_element_type=f32
        )
        for i in range(2):
            h = 2 * q + i
            leaving[h, 0:SIZE] = local[i * SIZE : (i + 1) * SIZE].astype(bf16)
            value = jnp.broadcast_to(total[h : h + 1, :], (16, STATE))
            coarse = value.astype(bf16)
            rest = (value - coarse.astype(f32)).astype(bf16)
            leaving[h, SIZE:MESSAGE] = jnp.where(top, coarse, rest)

    pl.semaphore_wait(barrier, CTX - 1)

    def out_copy(k):
        other = lax.rem(here + k, CTX)
        return pltpu.make_async_remote_copy(
            src_ref=leaving.at[other],
            dst_ref=gathered.at[here],
            send_sem=out_send.at[k],
            recv_sem=out_recv.at[k],
            device_id={"ctx": other},
            device_id_type=MESH,
        )

    def back_copy(k):
        other = lax.rem(here + k, CTX)
        return pltpu.make_async_remote_copy(
            src_ref=entering.at[other],
            dst_ref=returned.at[here],
            send_sem=back_send.at[k],
            recv_sem=back_recv.at[k],
            device_id={"ctx": other},
            device_id_type=MESH,
        )

    def each(action):
        def step(k, _):
            action(k)
            return 0

        lax.fori_loop(1, CTX, step, 0)

    each(lambda k: out_copy(k).start())
    gathered[here] = leaving[here]

    meet = lax.dot_general(
        read_ref[...], write_ref[...], (((1,), (1,)), ((), ())), preferred_element_type=f32
    )

    def within(q):
        lanes = pl.ds(q * 2 * SIZE, 2 * SIZE)
        pair = mixer_ref[:, lanes]
        halves = []
        for i in range(2):
            h = 2 * q + i
            span = levels[h : h + 1, :] - levels_t[:, h : h + 1]
            weight = jnp.exp(jnp.where(causal, span, -1e30)) * meet
            halves.append(jnp.dot(weight.astype(bf16), pair, preferred_element_type=f32))
        skip = jnp.where(low, skip_ref[2 * q], skip_ref[2 * q + 1])
        acc[:, lanes] = jnp.where(low, halves[0], halves[1]) + skip * pair.astype(f32)

    EARLY = 3
    for q in range(EARLY):
        within(q)

    mine.wait()
    each(lambda k: out_copy(k).wait_recv())
    state = start[...]
    for k in range(CTX):
        entering[k] = state.astype(bf16)
        if k < CTX - 1:
            factor = gathered[k, SIZE:MESSAGE].astype(f32)
            factor = factor[0:1, :] + factor[8:9, :]
            state = factor * state + gathered[k, 0:SIZE].astype(f32)
    each(lambda k: back_copy(k).start())
    returned[here] = entering[here]

    for q in range(EARLY, HEADS // 2):
        within(q)

    each(lambda k: back_copy(k).wait_recv())
    square = jnp.zeros((length, 1), f32)
    for q in range(HEADS // 2):
        lanes = pl.ds(q * 2 * SIZE, 2 * SIZE)
        entered = returned[2 * q : 2 * q + 2].reshape(2 * SIZE, STATE)
        carried = lax.dot_general(
            read_ref[...], entered, (((1,), (1,)), ((), ())), preferred_element_type=f32
        )
        gate = gate_ref[:, lanes].astype(f32)
        gated = (acc[:, lanes] + carried * spread(from_start, q)) * (gate / (1.0 + jnp.exp(-gate)))
        acc[:, lanes] = gated
        square = square + jnp.sum(gated * gated, axis=1, keepdims=True)
    scale = lax.rsqrt(square / (HEADS * SIZE) + 1e-05)
    for q in range(HEADS // 2):
        lanes = pl.ds(q * 2 * SIZE, 2 * SIZE)
        out_ref[:, lanes] = (acc[:, lanes] * scale * gain_ref[:, lanes]).astype(bf16)

    each(lambda k: out_copy(k).wait_send())
    each(lambda k: back_copy(k).wait_send())


def scan(mixer, gate, write, read, decay, skip, gain, start_state):
    length, inner = mixer.shape
    f32, bf16 = jnp.float32, jnp.bfloat16
    vmem = pl.BlockSpec(memory_space=pltpu.VMEM)
    return pl.pallas_call(
        scan_kernel,
        out_shape=jax.ShapeDtypeStruct((length, inner), bf16),
        in_specs=[vmem] * 5
        + [
            pl.BlockSpec(memory_space=pltpu.SMEM),
            vmem,
            pl.BlockSpec(memory_space=pl.ANY),
        ],
        out_specs=vmem,
        scratch_shapes=[
            pltpu.VMEM((CTX, MESSAGE, STATE), bf16),
            pltpu.VMEM((CTX, MESSAGE, STATE), bf16),
            pltpu.VMEM((CTX, SIZE, STATE), bf16),
            pltpu.VMEM((CTX, SIZE, STATE), bf16),
            pltpu.VMEM((SIZE, STATE), f32),
            pltpu.VMEM((length, inner), f32),
            pltpu.SemaphoreType.DMA((CTX,)),
            pltpu.SemaphoreType.DMA((CTX,)),
            pltpu.SemaphoreType.DMA((CTX,)),
            pltpu.SemaphoreType.DMA((CTX,)),
            pltpu.SemaphoreType.DMA,
        ],
        compiler_params=pltpu.CompilerParams(
            collective_id=1, has_side_effects=True, vmem_limit_bytes=60 << 20
        ),
        cost_estimate=pl.CostEstimate(
            flops=1 << 29, bytes_accessed=4 << 20, transcendentals=1 << 20
        ),
    )(mixer, gate, write, read, decay, skip, gain, start_state)


def shards(
    mixer_in,
    gate_in,
    state_write,
    state_read,
    decay_rate,
    skip_gain,
    norm_gain,
    start_state,
    out_weight,
    residual,
    router_weight,
    chosen,
    slot_index,
    spill_index,
    gate_weight,
    up_weight,
    down_weight,
):
    normed = scan(
        mixer_in[0],
        gate_in[0],
        state_write[0, :, 0],
        state_read[0, :, 0],
        decay_rate[0],
        skip_gain,
        norm_gain[None],
        start_state[0].reshape(HEADS * SIZE, STATE),
    )
    return layer(
        normed,
        out_weight.reshape(2, SIDE, ROWS, D),
        residual[0],
        router_weight.T,
        chosen[0].T,
        slot_index[0].T,
        spill_index[0].T,
        gate_weight[0],
        up_weight[0],
        down_weight[0],
    )[None]


def solution(mesh):
    placed = (
        P("dp", "ctx", "exp"),
        P("dp", "ctx", "exp"),
        P("dp", "ctx", "exp", None),
        P("dp", "ctx", "exp", None),
        P("dp", "exp", "ctx"),
        P("exp"),
        P("exp"),
        P("dp", "exp", None, None),
        P("exp", None),
        P("dp", ("ctx", "exp"), None),
        P(),
        P("dp", ("ctx", "exp"), None),
        P("dp", ("ctx", "exp"), None),
        P("dp", ("ctx", "exp"), None),
        P(("exp", "dp"), None, "ctx"),
        P(("exp", "dp"), None, "ctx"),
        P(("exp", "dp"), None, "ctx"),
    )
    return jax.shard_map(
        shards, mesh=mesh, in_specs=placed, out_specs=P("dp", ("ctx", "exp"), None), check_vma=False
    )
```

```python
import functools

import jax
import jax.numpy as jnp
from jax import lax
from jax.experimental import pallas as pl
from jax.experimental.pallas import tpu as pltpu
from jax.sharding import PartitionSpec as P

D = 4096
EXPERTS = 8
CAP = 14
BLOCK = 16
TOKENS = 64
GROUPS = 4
SIDE = 4
WIDTH = 512
QUADS = D // WIDTH // 2
PAIRS = 2 * QUADS
PIECE = GROUPS * BLOCK
HALF = PIECE // 2
PLANE = SIDE * SIDE * PIECE
SUMS = 10
LAST = 7
MESH = pl.DeviceIdType.MESH


def layer_kernel(
    normed_ref,
    mix_ref,
    residual_ref,
    router_ref,
    chosen_ref,
    slot_ref,
    spill_ref,
    gate_ref,
    up_ref,
    down_ref,
    out_ref,
    normed,
    mixed,
    terms,
    hidden,
    placing,
    shares,
    logits,
    leaving,
    sums,
    returned,
    xg,
    acc,
    act,
    w_gate,
    w_up,
    w_down,
    part,
    line,
    ag_send,
    ag_recv,
    rs_send,
    rs_recv,
    mix_send,
    mix_recv,
    row_send,
    row_recv,
    back_send,
    back_recv,
    load_sem,
    mix_sem,
    normed_sem,
):
    f32, bf16 = jnp.float32, jnp.bfloat16
    here = lax.axis_index("ctx")
    my = {"x": lax.rem(here, SIDE), "z": lax.div(here, SIDE)}
    my_exp, my_dp = lax.axis_index("exp"), lax.axis_index("dp")
    owner = my_exp * 2 + my_dp

    def around(axis, step):
        return lax.rem(my[axis] + step + SIDE, SIDE)

    def neighbour(axis, step):
        other = around(axis, step)
        if axis == "x":
            return {"ctx": my["z"] * SIDE + other}
        return {"ctx": other * SIDE + my["x"]}

    def along(axis, ref, place, at):
        if axis == "z":
            return ref.at[place, at]
        return ref.at[at, place]

    def partner(o):
        other = lax.rem(owner + o, EXPERTS)
        return other, {"exp": lax.div(other, 2), "dp": lax.rem(other, 2)}

    def remote(src, dst, send, recv, place):
        return pltpu.make_async_remote_copy(
            src_ref=src,
            dst_ref=dst,
            send_sem=send,
            recv_sem=recv,
            device_id=place,
            device_id_type=MESH,
        )

    def columns_of(q):
        return pl.ds(pl.multiple_of(q * WIDTH, WIDTH), WIDTH)

    def rows_of(index, count):
        return pl.ds(pl.multiple_of(index * count, count), count)

    def mix_room(q):
        return part.at[lax.div(q, 2), lax.rem(q, 2)]

    def mix_load(q):
        return pltpu.make_async_copy(
            mix_ref.at[:, :, :, columns_of(q)], mix_room(q), mix_sem.at[q]
        )

    fetch = pltpu.make_async_copy(normed_ref, normed, normed_sem)
    fetch.start()
    loads = [
        pltpu.make_async_copy(src, dst, load_sem.at[i])
        for i, (src, dst) in enumerate(((gate_ref, w_gate), (up_ref, w_up), (down_ref, w_down)))
    ]

    def load_mix(q, _):
        mix_load(q).start()
        return 0

    lax.fori_loop(0, 2 * QUADS, load_mix, 0)

    barrier = pltpu.get_barrier_semaphore()
    for axis in ("x", "z"):
        for step in (1, -1):
            pl.semaphore_signal(
                barrier, inc=1, device_id=neighbour(axis, step), device_id_type=MESH
            )
    for o in range(1, EXPERTS):
        pl.semaphore_signal(barrier, inc=1, device_id=partner(o)[1], device_id_type=MESH)

    row_id = lax.broadcasted_iota(jnp.int32, (EXPERTS * BLOCK, TOKENS), 0)
    expert_ids, slot_ids, spill_ids = chosen_ref[...], slot_ref[...], spill_ref[...]
    target = jnp.where(
        slot_ids >= 0,
        expert_ids * BLOCK + slot_ids,
        jnp.where(
            spill_ids >= 0,
            jnp.right_shift(spill_ids, 1) * BLOCK + CAP + jnp.bitwise_and(spill_ids, 1),
            -1,
        ),
    )
    places = [row_id == target[i : i + 1, :] for i in range(2)]
    placing[...] = (places[0].astype(f32) + places[1].astype(f32)).astype(bf16)
    logits[...] = jnp.zeros_like(logits)
    fetch.wait()
    pl.semaphore_wait(barrier, 4 + EXPERTS - 1)

    every = pl.ds(0, SIDE)
    halves = {1: pl.ds(0, SIDE // 2), -1: pl.ds(SIDE // 2, SIDE // 2)}
    half_rows = {1: pl.ds(0, HALF), -1: pl.ds(HALF, HALF)}
    axes = (("x", "z"), ("z", "x"))
    slot = {1: 0, -1: 1}
    both = [(t, d) for t in range(2) for d in (1, -1)]


    def term_copy(c, t, i):
        other = lax.rem(my_exp + i, GROUPS)
        q = 2 * c + t
        return remote(
            mixed.at[lax.rem(c, 2), t, other],
            terms.at[q, i - 1],
            mix_send.at[q, i - 1],
            mix_recv.at[q, i - 1],
            {"exp": other},
        )

    def mix(c):
        for t in range(2):
            q = 2 * c + t
            mix_load(q).wait()
            term = jnp.dot(
                normed[...],
                mix_room(q)[...].reshape(normed.shape[1], WIDTH),
                preferred_element_type=f32,
            )
            mixed[lax.rem(c, 2), t] = term.astype(bf16).reshape(GROUPS, TOKENS, WIDTH)
            for i in range(1, GROUPS):
                term_copy(c, t, i).start()


    def row_copy(c, t, o):
        other, place = partner(o)
        k = 2 * (my_dp * QUADS + c) + t
        return remote(
            leaving.at[lax.rem(c, 2), t, other],
            xg.at[k, my["z"], my["x"], rows_of(my_exp, BLOCK)],
            row_send.at[2 * c + t],
            row_recv.at[k],
            place,
        )

    def tokens(c):
        for t in range(2):
            q = 2 * c + t
            columns = columns_of(q)
            for i in range(1, GROUPS):
                term_copy(c, t, i).wait_recv()
            total = mixed[lax.rem(c, 2), t, my_exp].astype(f32)
            for i in range(1, GROUPS):
                total = total + terms[q, i - 1].astype(f32)
            value = (residual_ref[:, columns].astype(f32) + total).astype(bf16)
            hidden[:, columns] = value
            rows = jnp.dot(placing[...], value, preferred_element_type=f32).astype(bf16)
            leaving[lax.rem(c, 2), t] = rows.reshape(EXPERTS, BLOCK, WIDTH)
            for o in range(1, EXPERTS):
                row_copy(c, t, o).start()
            k = 2 * (my_dp * QUADS + c) + t
            xg[k, my["z"], my["x"], rows_of(my_exp, BLOCK)] = leaving[lax.rem(c, 2), t, owner]
            logits[...] += lax.dot_general(
                router_ref[:, columns],
                value,
                (((1,), (1,)), ((), ())),
                preferred_element_type=f32,
            )
        for t in range(2):
            for i in range(1, GROUPS):
                term_copy(c, t, i).wait_send()

    def rows_sent(c):
        for t in range(2):
            ref = leaving.at[lax.rem(c, 2), t, pl.ds(0, EXPERTS - 1)]
            remote(ref, ref, row_send.at[2 * c + t], row_recv.at[0], partner(1)[1]).wait_send()


    def ag_copy(j, t, step, d, landing, off=0):
        near, far = axes[t]
        chunk = xg.at[2 * j + t]
        back = -d if landing else 0
        if step == 0:
            ref, to = along(near, chunk, around(near, back), my[far]), near
        elif step == 1:
            ref = along(near, chunk, around(near, -2 * d if landing else -d), my[far])
            ref, to = ref.at[half_rows[d]], near
        elif step == 2 and off is None:
            ref, to = along(far, chunk, around(far, back), every), far
        elif step == 2:
            ref, to = along(near, chunk, around(near, off), my[far]), far
        else:
            ref = along(far, chunk, around(far, -2 * d if landing else -d), halves[d])
            to = far
        m = step * 2 + slot[d]
        return remote(ref, ref, ag_send.at[j, t, m], ag_recv.at[j, t, m], neighbour(to, d))

    def ag_arrive(j, step):
        for t, d in both:
            ag_copy(j, t, step, d, True, None).wait_recv()

    def gather_first(j):
        mine = my_dp == lax.div(j, QUADS)
        for t in range(2):
            k = 2 * j + t

            def arrive(count):
                ref = xg.at[k, my["z"], my["x"], pl.ds(0, count)]
                remote(ref, ref, row_send.at[0], row_recv.at[k], partner(1)[1]).wait_recv()

            pl.when(mine)(functools.partial(arrive, PIECE - BLOCK))
            pl.when(jnp.logical_not(mine))(functools.partial(arrive, PIECE))
            for d in (1, -1):
                ag_copy(j, t, 0, d, False).start()
        for t, d in both:
            ag_copy(j, t, 2, d, False, 0).start()

    def gather_second(j):
        ag_arrive(j, 0)
        for t, d in both:
            ag_copy(j, t, 1, d, False).start()
        for t, d in both:
            for off in (1, -1):
                ag_copy(j, t, 2, d, False, off).start()

    def gather_third(j):
        ag_arrive(j, 1)
        for t, d in both:
            ag_copy(j, t, 2, d, False, 2).start()

    def gather_last(j):
        ag_arrive(j, 2)
        for t, d in both:
            ag_copy(j, t, 3, d, False).start()

    def gathered(j):
        h = lax.div(j, QUADS)
        c = lax.rem(j, QUADS)
        ag_arrive(j, 3)
        for step in range(4):
            for t, d in both:
                ag_copy(j, t, step, d, False, None).wait_send()

        @pl.when(j == 0)
        def _():
            for load in loads:
                load.wait()

        @pl.loop(0, 2)
        def _(b):
            rows = rows_of(h * 2 + b, PLANE // 2)
            for n, weight in enumerate((w_gate, w_up)):
                total = acc[n, rows, :]
                for t in range(2):
                    total += jnp.dot(
                        xg[2 * j + t, pl.ds(b * 2, 2)].reshape(PLANE // 2, WIDTH),
                        weight[columns_of(2 * c + t), :],
                        preferred_element_type=f32,
                    )
                acc[n, rows, :] = total

        @pl.when(c == QUADS - 1)
        def _():
            @pl.loop(0, 8)
            def _(b):
                rows = rows_of(h * 8 + b, PLANE // 8)
                gate = acc[0, rows, :]
                act[rows, :] = (gate / (1.0 + jnp.exp(-gate)) * acc[1, rows, :]).astype(bf16)


    def rs_copy(j, t, step, d):
        near, far = axes[t]
        p = part.at[lax.rem(j, 4), t]
        room = xg.at[2 * j + t]
        if step == 0:
            src = along(far, p, around(far, 2), halves[d])
            dst, to = room.at[0, halves[d]], far
        elif step == 1:
            src = along(far, p, around(far, d), every)
            dst, to = room.at[1 + slot[d]], far
        elif step == 2:
            src = line.at[lax.rem(j, 4), t, around(near, 2), half_rows[d]]
            dst, to = room.at[3, 0, half_rows[d]], near
        else:
            src = line.at[lax.rem(j, 4), t, around(near, d)]
            dst, to = room.at[3, 1 + slot[d]], near
        m = step * 2 + slot[d]
        return remote(src, dst, rs_send.at[j, t, m], rs_recv.at[j, t, m], neighbour(to, d))

    def rs_start(j, step, t):
        for d in (1, -1):
            rs_copy(j, t, step, d).start()

    def rs_arrive(j, step, t):
        for d in (1, -1):
            rs_copy(j, t, step, d).wait_recv()

    def rs_sent(j, steps):
        for step in steps:
            for t, d in both:
                rs_copy(j, t, step, d).wait_send()

    def sum_start(j):
        h = lax.div(j, QUADS)
        c = lax.rem(j, QUADS)

        @pl.loop(0, 2)
        def _(b):
            rows = rows_of(h * 2 + b, PLANE // 2)
            for t in range(2):
                term = lax.dot_general(
                    act[rows, :],
                    w_down[columns_of(2 * c + t), :],
                    (((1,), (1,)), ((), ())),
                    preferred_element_type=f32,
                )
                part[lax.rem(j, 4), t, pl.ds(b * 2, 2)] = term.astype(bf16).reshape(
                    2, SIDE, PIECE, WIDTH
                )

        for t in range(2):
            rs_start(j, 0, t)

    def sum_first(j):
        s = lax.rem(j, 4)
        for t in range(2):
            far = axes[t][1]
            rs_arrive(j, 0, t)
            for d in (1, -1):
                base = 0 if d == 1 else SIDE // 2
                place = around(far, d)

                @pl.loop(0, SIDE // 2)
                def _(i):
                    at = (place, base + i) if far == "z" else (base + i, place)
                    part[s, t, at[0], at[1]] = (
                        part[s, t, at[0], at[1]].astype(f32)
                        + xg[2 * j + t, 0, base + i].astype(f32)
                    ).astype(bf16)

            rs_start(j, 1, t)

    def sum_second(j):
        s = lax.rem(j, 4)
        for t in range(2):
            far = axes[t][1]
            rs_arrive(j, 1, t)

            @pl.loop(0, SIDE)
            def _(i):
                at = (my[far], i) if far == "z" else (i, my[far])
                line[s, t, i] = (
                    part[s, t, at[0], at[1]].astype(f32)
                    + xg[2 * j + t, 1, i].astype(f32)
                    + xg[2 * j + t, 2, i].astype(f32)
                ).astype(bf16)

            rs_start(j, 2, t)
        rs_sent(j, (0, 1))

    def sum_third(j):
        s = lax.rem(j, 4)
        for t in range(2):
            rs_arrive(j, 2, t)
            for d in (1, -1):
                at = around(axes[t][0], d)
                line[s, t, at, half_rows[d]] = (
                    line[s, t, at, half_rows[d]].astype(f32)
                    + xg[2 * j + t, 3, 0, half_rows[d]].astype(f32)
                ).astype(bf16)
            rs_start(j, 3, t)


    def back_copy(j, t, o):
        other = lax.rem(my_exp + o, GROUPS)
        k = 2 * lax.rem(j, QUADS) + t
        return remote(
            sums.at[lax.rem(j, 2), t, other],
            returned.at[k, rows_of(owner, BLOCK)],
            back_send.at[2 * j + t],
            back_recv.at[k],
            {"exp": other, "dp": lax.div(j, QUADS)},
        )

    def sum_last(j):
        mine = my_dp == lax.div(j, QUADS)
        for t in range(2):
            rs_arrive(j, 3, t)
            total = (
                line[lax.rem(j, 4), t, my[axes[t][0]]].astype(f32)
                + xg[2 * j + t, 3, 1].astype(f32)
                + xg[2 * j + t, 3, 2].astype(f32)
            )
            s = lax.rem(j, 2)
            sums[s, t] = total.astype(bf16).reshape(GROUPS, BLOCK, WIDTH)
            for o in range(1, GROUPS):
                back_copy(j, t, o).start()

            @pl.when(mine)
            def _():
                k = 2 * lax.rem(j, QUADS) + t
                returned[k, rows_of(owner, BLOCK)] = sums[s, t, my_exp]

            @pl.when(jnp.logical_not(mine))
            def _():
                back_copy(j, t, 0).start()

        rs_sent(j, (2, 3))

    def sum_back(j):
        mine = my_dp == lax.div(j, QUADS)
        for t in range(2):
            q = 2 * lax.rem(j, QUADS) + t

            def sent(count):
                ref = sums.at[lax.rem(j, 2), t, pl.ds(0, count)]
                remote(
                    ref, ref, back_send.at[2 * j + t], back_recv.at[0], partner(1)[1]
                ).wait_send()

            @pl.when(mine)
            def _():
                ref = returned.at[q, pl.ds(0, (EXPERTS - 1) * BLOCK)]
                remote(ref, ref, back_send.at[0], back_recv.at[q], partner(1)[1]).wait_recv()
                columns = columns_of(q)
                total = hidden[:, columns].astype(f32)
                for n in range(2):
                    total = total + lax.dot_general(
                        shares[n],
                        returned[q],
                        (((0,), (0,)), ((), ())),
                        preferred_element_type=f32,
                    )
                out_ref[:, columns] = total.astype(bf16)
                sent(GROUPS - 1)

            pl.when(jnp.logical_not(mine))(functools.partial(sent, GROUPS))

    def weigh():
        match = [
            lax.broadcasted_iota(jnp.int32, (EXPERTS, TOKENS), 0) == chosen_ref[i : i + 1, :]
            for i in range(2)
        ]
        picked = [jnp.sum(jnp.where(m, logits[...], 0.0), axis=0, keepdims=True) for m in match]
        weights = jnp.zeros((EXPERTS * BLOCK, TOKENS), f32)
        for i in range(2):
            share = 1.0 / (1.0 + jnp.exp(picked[1 - i] - picked[i]))
            weights = weights + jnp.where(row_id == target[i : i + 1, :], share, 0.0)
        coarse = weights.astype(bf16)
        shares[0] = coarse
        shares[1] = (weights - coarse.astype(f32)).astype(bf16)

    def stages(tick, count, steps):
        for lag, action in steps:
            pl.when(jnp.logical_and(tick >= lag, tick < count + lag))(
                functools.partial(action, tick - lag)
            )

    for load in loads:
        load.start()
    acc[...] = jnp.zeros_like(acc)

    @pl.loop(0, 1 + SUMS + PAIRS + LAST)
    def _(turn):
        tick = turn - 1
        own = tick - my_dp * QUADS
        stages(
            tick,
            PAIRS,
            ((5, gather_last), (4, gather_third), (3, gather_second), (2, gather_first)),
        )
        stages(tick - SUMS, PAIRS, ((4, sum_second), (2, sum_first)))
        stages(own, QUADS, ((3, rows_sent), (1, tokens), (-1, mix)))
        stages(tick, PAIRS, ((6, gathered),))
        pl.when(tick == SUMS)(weigh)
        stages(
            tick - SUMS,
            PAIRS,
            ((0, sum_start), (5, sum_third), (6, sum_last), (7, sum_back)),
        )


def layer(normed, mix_w, residual, router, chosen, slots, spills, gate_w, up_w, down_w):
    units = gate_w.shape[1]
    length, inner = normed.shape
    bf16, f32 = jnp.bfloat16, jnp.float32
    any_space = pl.BlockSpec(memory_space=pl.ANY)
    vmem = pl.BlockSpec(memory_space=pltpu.VMEM)
    return pl.pallas_call(
        layer_kernel,
        out_shape=jax.ShapeDtypeStruct((TOKENS, D), bf16),
        in_specs=[any_space] * 2 + [vmem] * 5 + [any_space] * 3,
        out_specs=vmem,
        scratch_shapes=[
            pltpu.VMEM((length, inner), bf16),
            pltpu.VMEM((2, 2, GROUPS, TOKENS, WIDTH), bf16),
            pltpu.VMEM((2 * QUADS, GROUPS - 1, TOKENS, WIDTH), bf16),
            pltpu.VMEM((TOKENS, D), bf16),
            pltpu.VMEM((EXPERTS * BLOCK, TOKENS), bf16),
            pltpu.VMEM((2, EXPERTS * BLOCK, TOKENS), bf16),
            pltpu.VMEM((EXPERTS, TOKENS), f32),
            pltpu.VMEM((2, 2, EXPERTS, BLOCK, WIDTH), bf16),
            pltpu.VMEM((2, 2, GROUPS, BLOCK, WIDTH), bf16),
            pltpu.VMEM((2 * QUADS, EXPERTS * BLOCK, WIDTH), bf16),
            pltpu.VMEM((2 * PAIRS, SIDE, SIDE, PIECE, WIDTH), bf16),
            pltpu.VMEM((2, 2 * PLANE, units), f32),
            pltpu.VMEM((2 * PLANE, units), bf16),
            pltpu.VMEM((D, units), bf16),
            pltpu.VMEM((D, units), bf16),
            pltpu.VMEM((D, units), bf16),
            pltpu.VMEM((4, 2, SIDE, SIDE, PIECE, WIDTH), bf16),
            pltpu.VMEM((4, 2, SIDE, PIECE, WIDTH), bf16),
            pltpu.SemaphoreType.DMA((PAIRS, 2, 8)),
            pltpu.SemaphoreType.DMA((PAIRS, 2, 8)),
            pltpu.SemaphoreType.DMA((PAIRS, 2, 8)),
            pltpu.SemaphoreType.DMA((PAIRS, 2, 8)),
            pltpu.SemaphoreType.DMA((2 * QUADS, GROUPS - 1)),
            pltpu.SemaphoreType.DMA((2 * QUADS, GROUPS - 1)),
            pltpu.SemaphoreType.DMA((2 * QUADS,)),
            pltpu.SemaphoreType.DMA((2 * PAIRS,)),
            pltpu.SemaphoreType.DMA((2 * PAIRS,)),
            pltpu.SemaphoreType.DMA((2 * QUADS,)),
            pltpu.SemaphoreType.DMA((3,)),
            pltpu.SemaphoreType.DMA((2 * QUADS,)),
            pltpu.SemaphoreType.DMA,
        ],
        compiler_params=pltpu.CompilerParams(
            collective_id=0, has_side_effects=True, vmem_limit_bytes=62 << 20
        ),
        cost_estimate=pl.CostEstimate(
            flops=6 * 2048 * D * 512, bytes_accessed=24 << 20, transcendentals=1 << 20
        ),
    )(normed, mix_w, residual, router, chosen, slots, spills, gate_w, up_w, down_w)


HEADS = 16
SIZE = 64
STATE = 128
CTX = SIDE * SIDE
MESSAGE = SIZE + 16


def scan_kernel(
    mixer_ref,
    gate_ref,
    write_ref,
    read_ref,
    decay_ref,
    skip_ref,
    gain_ref,
    start_ref,
    out_ref,
    leaving,
    gathered,
    entering,
    returned,
    start,
    acc,
    out_send,
    out_recv,
    back_send,
    back_recv,
    start_sem,
):
    here = lax.axis_index("ctx")
    f32, bf16 = jnp.float32, jnp.bfloat16
    length = mixer_ref.shape[0]
    mine = pltpu.make_async_copy(
        start_ref.at[pl.ds(pl.multiple_of(here * SIZE, SIZE), SIZE), :], start, start_sem
    )
    mine.start()

    barrier = pltpu.get_barrier_semaphore()

    def greet(k, _):
        other = lax.rem(here + k, CTX)
        pl.semaphore_signal(barrier, inc=1, device_id={"ctx": other}, device_id_type=MESH)
        return 0

    lax.fori_loop(1, CTX, greet, 0)

    row_id = lax.broadcasted_iota(jnp.int32, (length, length), 0)
    col_id = lax.broadcasted_iota(jnp.int32, (length, length), 1)
    causal = row_id >= col_id
    upper = jnp.where(row_id <= col_id, 1.0, 0.0).astype(f32)
    levels = jnp.dot(
        decay_ref[...], upper, precision=lax.Precision.HIGHEST, preferred_element_type=f32
    )
    last = levels[:, length - 1 : length]
    to_end = jnp.exp(levels - last).T
    total = jnp.exp(-last)
    levels_t = levels.T
    from_start = jnp.exp(-levels_t)
    low = lax.broadcasted_iota(jnp.int32, (length, 2 * SIZE), 1) < SIZE
    top = lax.broadcasted_iota(jnp.int32, (16, STATE), 0) < 8

    def spread(columns, q):
        return jnp.where(low, columns[:, 2 * q : 2 * q + 1], columns[:, 2 * q + 1 : 2 * q + 2])

    for q in range(HEADS // 2):
        lanes = pl.ds(q * 2 * SIZE, 2 * SIZE)
        scaled = (spread(to_end, q) * mixer_ref[:, lanes].astype(f32)).astype(bf16)
        local = lax.dot_general(
            scaled, write_ref[...], (((0,), (0,)), ((), ())), preferred_element_type=f32
        )
        for i in range(2):
            h = 2 * q + i
            leaving[h, 0:SIZE] = local[i * SIZE : (i + 1) * SIZE].astype(bf16)
            value = jnp.broadcast_to(total[h : h + 1, :], (16, STATE))
            coarse = value.astype(bf16)
            rest = (value - coarse.astype(f32)).astype(bf16)
            leaving[h, SIZE:MESSAGE] = jnp.where(top, coarse, rest)

    pl.semaphore_wait(barrier, CTX - 1)

    def out_copy(k):
        other = lax.rem(here + k, CTX)
        return pltpu.make_async_remote_copy(
            src_ref=leaving.at[other],
            dst_ref=gathered.at[here],
            send_sem=out_send.at[k],
            recv_sem=out_recv.at[k],
            device_id={"ctx": other},
            device_id_type=MESH,
        )

    def back_copy(k):
        other = lax.rem(here + k, CTX)
        return pltpu.make_async_remote_copy(
            src_ref=entering.at[other],
            dst_ref=returned.at[here],
            send_sem=back_send.at[k],
            recv_sem=back_recv.at[k],
            device_id={"ctx": other},
            device_id_type=MESH,
        )

    def each(action):
        def step(k, _):
            action(k)
            return 0

        lax.fori_loop(1, CTX, step, 0)

    each(lambda k: out_copy(k).start())
    gathered[here] = leaving[here]

    meet = lax.dot_general(
        read_ref[...], write_ref[...], (((1,), (1,)), ((), ())), preferred_element_type=f32
    )

    def within(q):
        lanes = pl.ds(q * 2 * SIZE, 2 * SIZE)
        pair = mixer_ref[:, lanes]
        halves = []
        for i in range(2):
            h = 2 * q + i
            span = levels[h : h + 1, :] - levels_t[:, h : h + 1]
            weight = jnp.exp(jnp.where(causal, span, -1e30)) * meet
            halves.append(jnp.dot(weight.astype(bf16), pair, preferred_element_type=f32))
        skip = jnp.where(low, skip_ref[2 * q], skip_ref[2 * q + 1])
        acc[:, lanes] = jnp.where(low, halves[0], halves[1]) + skip * pair.astype(f32)

    EARLY = 3
    for q in range(EARLY):
        within(q)

    mine.wait()
    each(lambda k: out_copy(k).wait_recv())
    state = start[...]
    for k in range(CTX):
        entering[k] = state.astype(bf16)
        if k < CTX - 1:
            factor = gathered[k, SIZE:MESSAGE].astype(f32)
            factor = factor[0:1, :] + factor[8:9, :]
            state = factor * state + gathered[k, 0:SIZE].astype(f32)
    each(lambda k: back_copy(k).start())
    returned[here] = entering[here]

    for q in range(EARLY, HEADS // 2):
        within(q)

    each(lambda k: back_copy(k).wait_recv())
    square = jnp.zeros((length, 1), f32)
    for q in range(HEADS // 2):
        lanes = pl.ds(q * 2 * SIZE, 2 * SIZE)
        entered = returned[2 * q : 2 * q + 2].reshape(2 * SIZE, STATE)
        carried = lax.dot_general(
            read_ref[...], entered, (((1,), (1,)), ((), ())), preferred_element_type=f32
        )
        gate = gate_ref[:, lanes].astype(f32)
        gated = (acc[:, lanes] + carried * spread(from_start, q)) * (gate / (1.0 + jnp.exp(-gate)))
        acc[:, lanes] = gated
        square = square + jnp.sum(gated * gated, axis=1, keepdims=True)
    scale = lax.rsqrt(square / (HEADS * SIZE) + 1e-05)
    for q in range(HEADS // 2):
        lanes = pl.ds(q * 2 * SIZE, 2 * SIZE)
        out_ref[:, lanes] = (acc[:, lanes] * scale * gain_ref[:, lanes]).astype(bf16)

    each(lambda k: out_copy(k).wait_send())
    each(lambda k: back_copy(k).wait_send())


def scan(mixer, gate, write, read, decay, skip, gain, start_state):
    length, inner = mixer.shape
    f32, bf16 = jnp.float32, jnp.bfloat16
    vmem = pl.BlockSpec(memory_space=pltpu.VMEM)
    return pl.pallas_call(
        scan_kernel,
        out_shape=jax.ShapeDtypeStruct((length, inner), bf16),
        in_specs=[vmem] * 5
        + [
            pl.BlockSpec(memory_space=pltpu.SMEM),
            vmem,
            pl.BlockSpec(memory_space=pl.ANY),
        ],
        out_specs=vmem,
        scratch_shapes=[
            pltpu.VMEM((CTX, MESSAGE, STATE), bf16),
            pltpu.VMEM((CTX, MESSAGE, STATE), bf16),
            pltpu.VMEM((CTX, SIZE, STATE), bf16),
            pltpu.VMEM((CTX, SIZE, STATE), bf16),
            pltpu.VMEM((SIZE, STATE), f32),
            pltpu.VMEM((length, inner), f32),
            pltpu.SemaphoreType.DMA((CTX,)),
            pltpu.SemaphoreType.DMA((CTX,)),
            pltpu.SemaphoreType.DMA((CTX,)),
            pltpu.SemaphoreType.DMA((CTX,)),
            pltpu.SemaphoreType.DMA,
        ],
        compiler_params=pltpu.CompilerParams(
            collective_id=1, has_side_effects=True, vmem_limit_bytes=60 << 20
        ),
        cost_estimate=pl.CostEstimate(
            flops=1 << 29, bytes_accessed=4 << 20, transcendentals=1 << 20
        ),
    )(mixer, gate, write, read, decay, skip, gain, start_state)


def shards(
    mixer_in,
    gate_in,
    state_write,
    state_read,
    decay_rate,
    skip_gain,
    norm_gain,
    start_state,
    out_weight,
    residual,
    router_weight,
    chosen,
    slot_index,
    spill_index,
    gate_weight,
    up_weight,
    down_weight,
):
    normed = scan(
        mixer_in[0],
        gate_in[0],
        state_write[0, :, 0],
        state_read[0, :, 0],
        decay_rate[0],
        skip_gain,
        norm_gain[None],
        start_state[0].reshape(HEADS * SIZE, STATE),
    )
    return layer(
        normed,
        out_weight.reshape(SIDE, SIDE, PIECE, D),
        residual[0],
        router_weight.T,
        chosen[0].T,
        slot_index[0].T,
        spill_index[0].T,
        gate_weight[0],
        up_weight[0],
        down_weight[0],
    )[None]


def solution(mesh):
    placed = (
        P("dp", "ctx", "exp"),
        P("dp", "ctx", "exp"),
        P("dp", "ctx", "exp", None),
        P("dp", "ctx", "exp", None),
        P("dp", "exp", "ctx"),
        P("exp"),
        P("exp"),
        P("dp", "exp", None, None),
        P("exp", None),
        P("dp", ("ctx", "exp"), None),
        P(),
        P("dp", ("ctx", "exp"), None),
        P("dp", ("ctx", "exp"), None),
        P("dp", ("ctx", "exp"), None),
        P(("exp", "dp"), None, "ctx"),
        P(("exp", "dp"), None, "ctx"),
        P(("exp", "dp"), None, "ctx"),
    )
    return jax.shard_map(
        shards, mesh=mesh, in_specs=placed, out_specs=P("dp", ("ctx", "exp"), None), check_vma=False
    )
```

```python
import functools

import jax
import jax.numpy as jnp
from jax import lax
from jax.experimental import pallas as pl
from jax.experimental.pallas import tpu as pltpu
from jax.sharding import PartitionSpec as P

D = 4096
EXPERTS = 8
CAP = 14
BLOCK = 16
TOKENS = 64
GROUPS = 4
SIDE = 4
WIDTH = 512
QUADS = D // WIDTH // 2
PAIRS = 2 * QUADS
PIECE = GROUPS * BLOCK
HALF = PIECE // 2
PLANE = SIDE * SIDE * PIECE
HEADS = 16
SIZE = 64
STATE = 128
CTX = SIDE * SIDE
LENGTH = 256
INNER = HEADS * SIZE
MESSAGE = SIZE + 16
EARLY = 3
SUMS = 10
LAST = 7
MESH = pl.DeviceIdType.MESH


def layer_kernel(
    mixer_ref,
    switch_ref,
    write_ref,
    read_ref,
    decay_ref,
    skip_ref,
    gain_ref,
    start_ref,
    mix_ref,
    residual_ref,
    router_ref,
    chosen_ref,
    slot_ref,
    spill_ref,
    gate_ref,
    up_ref,
    down_ref,
    out_ref,
    mixer,
    switch,
    write,
    read,
    decay,
    start,
    residual,
    router,
    inner,
    states,
    gathered_states,
    entering,
    entered,
    normed,
    mixed,
    terms,
    hidden,
    placing,
    shares,
    logits,
    leaving,
    sums,
    returned,
    xg,
    acc,
    act,
    w_gate,
    w_up,
    w_down,
    part,
    line,
    ag_send,
    ag_recv,
    rs_send,
    rs_recv,
    mix_send,
    mix_recv,
    row_send,
    row_recv,
    back_send,
    back_recv,
    load_sem,
    mix_sem,
    input_sem,
    out_send,
    out_recv,
    in_send,
    in_recv,
):
    f32, bf16 = jnp.float32, jnp.bfloat16
    here = lax.axis_index("ctx")
    my = {"x": lax.rem(here, SIDE), "z": lax.div(here, SIDE)}
    my_exp, my_dp = lax.axis_index("exp"), lax.axis_index("dp")
    owner = my_exp * 2 + my_dp

    def around(axis, step):
        return lax.rem(my[axis] + step + SIDE, SIDE)

    def neighbour(axis, step):
        other = around(axis, step)
        if axis == "x":
            return {"ctx": my["z"] * SIDE + other}
        return {"ctx": other * SIDE + my["x"]}

    def along(axis, ref, place, at):
        if axis == "z":
            return ref.at[place, at]
        return ref.at[at, place]

    def partner(o):
        other = lax.rem(owner + o, EXPERTS)
        return other, {"exp": lax.div(other, 2), "dp": lax.rem(other, 2)}

    def remote(src, dst, send, recv, place):
        return pltpu.make_async_remote_copy(
            src_ref=src,
            dst_ref=dst,
            send_sem=send,
            recv_sem=recv,
            device_id=place,
            device_id_type=MESH,
        )

    def columns_of(q):
        return pl.ds(pl.multiple_of(q * WIDTH, WIDTH), WIDTH)

    def rows_of(index, count):
        return pl.ds(pl.multiple_of(index * count, count), count)

    def mix_room(q):
        return part.at[lax.div(q, 2), lax.rem(q, 2)]

    def mix_load(q):
        return pltpu.make_async_copy(
            mix_ref.at[:, :, :, columns_of(q)], mix_room(q), mix_sem.at[q]
        )

    inputs = {
        name: pltpu.make_async_copy(src, dst, input_sem.at[i])
        for i, (name, src, dst) in enumerate(
            (
                ("decay", decay_ref, decay),
                ("mixer", mixer_ref, mixer),
                ("write", write_ref, write),
                ("read", read_ref, read),
                ("start", start_ref.at[rows_of(here, SIZE), :], start),
                ("switch", switch_ref, switch),
                ("residual", residual_ref, residual),
                ("router", router_ref, router),
            )
        )
    }
    for copy in inputs.values():
        copy.start()
    loads = [
        pltpu.make_async_copy(src, dst, load_sem.at[i])
        for i, (src, dst) in enumerate(((gate_ref, w_gate), (up_ref, w_up), (down_ref, w_down)))
    ]

    barrier = pltpu.get_barrier_semaphore()

    def greet(k, _):
        other = lax.rem(here + k, CTX)
        pl.semaphore_signal(barrier, inc=1, device_id={"ctx": other}, device_id_type=MESH)
        return 0

    lax.fori_loop(1, CTX, greet, 0)
    for o in range(1, EXPERTS):
        pl.semaphore_signal(barrier, inc=1, device_id=partner(o)[1], device_id_type=MESH)


    row_id = lax.broadcasted_iota(jnp.int32, (LENGTH, LENGTH), 0)
    col_id = lax.broadcasted_iota(jnp.int32, (LENGTH, LENGTH), 1)
    causal = row_id >= col_id
    upper = jnp.where(row_id <= col_id, 1.0, 0.0).astype(f32)
    inputs["decay"].wait()
    levels = jnp.dot(
        decay[...], upper, precision=lax.Precision.HIGHEST, preferred_element_type=f32
    )
    last = levels[:, LENGTH - 1 : LENGTH]
    to_end = jnp.exp(levels - last).T
    total_decay = jnp.exp(-last)
    levels_t = levels.T
    from_start = jnp.exp(-levels_t)
    low = lax.broadcasted_iota(jnp.int32, (LENGTH, 2 * SIZE), 1) < SIZE
    top = lax.broadcasted_iota(jnp.int32, (16, STATE), 0) < 8

    def spread(columns, q):
        return jnp.where(low, columns[:, 2 * q : 2 * q + 1], columns[:, 2 * q + 1 : 2 * q + 2])

    inputs["mixer"].wait()
    inputs["write"].wait()
    for q in range(HEADS // 2):
        lanes = pl.ds(q * 2 * SIZE, 2 * SIZE)
        scaled = (spread(to_end, q) * mixer[:, lanes].astype(f32)).astype(bf16)
        local = lax.dot_general(
            scaled, write[...], (((0,), (0,)), ((), ())), preferred_element_type=f32
        )
        for i in range(2):
            h = 2 * q + i
            states[h, 0:SIZE] = local[i * SIZE : (i + 1) * SIZE].astype(bf16)
            value = jnp.broadcast_to(total_decay[h : h + 1, :], (16, STATE))
            coarse = value.astype(bf16)
            rest = (value - coarse.astype(f32)).astype(bf16)
            states[h, SIZE:MESSAGE] = jnp.where(top, coarse, rest)

    pl.semaphore_wait(barrier, CTX - 1 + EXPERTS - 1)

    def out_copy(k):
        other = lax.rem(here + k, CTX)
        return remote(
            states.at[other],
            gathered_states.at[here],
            out_send.at[k],
            out_recv.at[k],
            {"ctx": other},
        )

    def in_copy(k):
        other = lax.rem(here + k, CTX)
        return remote(
            entering.at[other], entered.at[here], in_send.at[k], in_recv.at[k], {"ctx": other}
        )

    def each(action):
        def step(k, _):
            action(k)
            return 0

        lax.fori_loop(1, CTX, step, 0)

    each(lambda k: out_copy(k).start())
    gathered_states[here] = states[here]

    def load_mix(q, _):
        mix_load(q).start()
        return 0

    lax.fori_loop(0, 2 * QUADS, load_mix, 0)
    for load in loads:
        load.start()


    inputs["read"].wait()
    meet = lax.dot_general(
        read[...], write[...], (((1,), (1,)), ((), ())), preferred_element_type=f32
    )

    def within(q):
        lanes = pl.ds(q * 2 * SIZE, 2 * SIZE)
        pair = mixer[:, lanes]
        heads = []
        for i in range(2):
            h = 2 * q + i
            span = levels[h : h + 1, :] - levels_t[:, h : h + 1]
            weight = jnp.exp(jnp.where(causal, span, -1e30)) * meet
            heads.append(jnp.dot(weight.astype(bf16), pair, preferred_element_type=f32))
        skip = jnp.where(low, skip_ref[2 * q], skip_ref[2 * q + 1])
        inner[:, lanes] = jnp.where(low, heads[0], heads[1]) + skip * pair.astype(f32)

    for q in range(EARLY):
        within(q)


    inputs["start"].wait()
    each(lambda k: out_copy(k).wait_recv())
    state = start[...]
    for k in range(CTX):
        entering[k] = state.astype(bf16)
        if k < CTX - 1:
            factor = gathered_states[k, SIZE:MESSAGE].astype(f32)
            factor = factor[0:1, :] + factor[8:9, :]
            state = factor * state + gathered_states[k, 0:SIZE].astype(f32)
    each(lambda k: in_copy(k).start())
    entered[here] = entering[here]

    for q in range(EARLY, HEADS // 2):
        within(q)

    place_id = lax.broadcasted_iota(jnp.int32, (EXPERTS * BLOCK, TOKENS), 0)
    expert_ids, slot_ids, spill_ids = chosen_ref[...], slot_ref[...], spill_ref[...]
    target = jnp.where(
        slot_ids >= 0,
        expert_ids * BLOCK + slot_ids,
        jnp.where(
            spill_ids >= 0,
            jnp.right_shift(spill_ids, 1) * BLOCK + CAP + jnp.bitwise_and(spill_ids, 1),
            -1,
        ),
    )
    places = [place_id == target[i : i + 1, :] for i in range(2)]
    placing[...] = (places[0].astype(f32) + places[1].astype(f32)).astype(bf16)
    logits[...] = jnp.zeros_like(logits)
    acc[...] = jnp.zeros_like(acc)

    inputs["switch"].wait()
    each(lambda k: in_copy(k).wait_recv())
    square = jnp.zeros((LENGTH, 1), f32)
    for q in range(HEADS // 2):
        lanes = pl.ds(q * 2 * SIZE, 2 * SIZE)
        carried = lax.dot_general(
            read[...],
            entered[2 * q : 2 * q + 2].reshape(2 * SIZE, STATE),
            (((1,), (1,)), ((), ())),
            preferred_element_type=f32,
        )
        gate = switch[:, lanes].astype(f32)
        gated = (inner[:, lanes] + carried * spread(from_start, q)) * (
            gate / (1.0 + jnp.exp(-gate))
        )
        inner[:, lanes] = gated
        square = square + jnp.sum(gated * gated, axis=1, keepdims=True)
    scale = lax.rsqrt(square / INNER + 1e-05)
    for q in range(HEADS // 2):
        lanes = pl.ds(q * 2 * SIZE, 2 * SIZE)
        normed[:, lanes] = (inner[:, lanes] * scale * gain_ref[:, lanes]).astype(bf16)

    inputs["residual"].wait()
    inputs["router"].wait()
    each(lambda k: out_copy(k).wait_send())
    each(lambda k: in_copy(k).wait_send())

    every = pl.ds(0, SIDE)
    halves = {1: pl.ds(0, SIDE // 2), -1: pl.ds(SIDE // 2, SIDE // 2)}
    half_rows = {1: pl.ds(0, HALF), -1: pl.ds(HALF, HALF)}
    axes = (("x", "z"), ("z", "x"))
    slot = {1: 0, -1: 1}
    both = [(t, d) for t in range(2) for d in (1, -1)]


    def term_copy(c, t, i):
        other = lax.rem(my_exp + i, GROUPS)
        q = 2 * c + t
        return remote(
            mixed.at[lax.rem(c, 2), t, other],
            terms.at[q, i - 1],
            mix_send.at[q, i - 1],
            mix_recv.at[q, i - 1],
            {"exp": other},
        )

    def mix(c):
        for t in range(2):
            q = 2 * c + t
            mix_load(q).wait()
            term = jnp.dot(
                normed[...],
                mix_room(q)[...].reshape(INNER, WIDTH),
                preferred_element_type=f32,
            )
            mixed[lax.rem(c, 2), t] = term.astype(bf16).reshape(GROUPS, TOKENS, WIDTH)
            for i in range(1, GROUPS):
                term_copy(c, t, i).start()


    def row_copy(c, t, o):
        other, place = partner(o)
        k = 2 * (my_dp * QUADS + c) + t
        return remote(
            leaving.at[lax.rem(c, 2), t, other],
            xg.at[k, my["z"], my["x"], rows_of(my_exp, BLOCK)],
            row_send.at[2 * c + t],
            row_recv.at[k],
            place,
        )

    def tokens(c):
        for t in range(2):
            q = 2 * c + t
            columns = columns_of(q)
            for i in range(1, GROUPS):
                term_copy(c, t, i).wait_recv()
            total = mixed[lax.rem(c, 2), t, my_exp].astype(f32)
            for i in range(1, GROUPS):
                total = total + terms[q, i - 1].astype(f32)
            value = (residual[:, columns].astype(f32) + total).astype(bf16)
            hidden[:, columns] = value
            rows = jnp.dot(placing[...], value, preferred_element_type=f32).astype(bf16)
            leaving[lax.rem(c, 2), t] = rows.reshape(EXPERTS, BLOCK, WIDTH)
            for o in range(1, EXPERTS):
                row_copy(c, t, o).start()
            k = 2 * (my_dp * QUADS + c) + t
            xg[k, my["z"], my["x"], rows_of(my_exp, BLOCK)] = leaving[lax.rem(c, 2), t, owner]
            logits[...] += lax.dot_general(
                router[:, columns],
                value,
                (((1,), (1,)), ((), ())),
                preferred_element_type=f32,
            )
        for t in range(2):
            for i in range(1, GROUPS):
                term_copy(c, t, i).wait_send()

    def rows_sent(c):
        for t in range(2):
            ref = leaving.at[lax.rem(c, 2), t, pl.ds(0, EXPERTS - 1)]
            remote(ref, ref, row_send.at[2 * c + t], row_recv.at[0], partner(1)[1]).wait_send()


    def ag_copy(j, t, step, d, landing, off=0):
        near, far = axes[t]
        chunk = xg.at[2 * j + t]
        back = -d if landing else 0
        if step == 0:
            ref, to = along(near, chunk, around(near, back), my[far]), near
        elif step == 1:
            ref = along(near, chunk, around(near, -2 * d if landing else -d), my[far])
            ref, to = ref.at[half_rows[d]], near
        elif step == 2 and off is None:
            ref, to = along(far, chunk, around(far, back), every), far
        elif step == 2:
            ref, to = along(near, chunk, around(near, off), my[far]), far
        else:
            ref = along(far, chunk, around(far, -2 * d if landing else -d), halves[d])
            to = far
        m = step * 2 + slot[d]
        return remote(ref, ref, ag_send.at[j, t, m], ag_recv.at[j, t, m], neighbour(to, d))

    def ag_arrive(j, step):
        for t, d in both:
            ag_copy(j, t, step, d, True, None).wait_recv()

    def gather_first(j):
        mine = my_dp == lax.div(j, QUADS)
        for t in range(2):
            k = 2 * j + t

            def arrive(count):
                ref = xg.at[k, my["z"], my["x"], pl.ds(0, count)]
                remote(ref, ref, row_send.at[0], row_recv.at[k], partner(1)[1]).wait_recv()

            pl.when(mine)(functools.partial(arrive, PIECE - BLOCK))
            pl.when(jnp.logical_not(mine))(functools.partial(arrive, PIECE))
            for d in (1, -1):
                ag_copy(j, t, 0, d, False).start()
        for t, d in both:
            ag_copy(j, t, 2, d, False, 0).start()

    def gather_second(j):
        ag_arrive(j, 0)
        for t, d in both:
            ag_copy(j, t, 1, d, False).start()
        for t, d in both:
            for off in (1, -1):
                ag_copy(j, t, 2, d, False, off).start()

    def gather_third(j):
        ag_arrive(j, 1)
        for t, d in both:
            ag_copy(j, t, 2, d, False, 2).start()

    def gather_last(j):
        ag_arrive(j, 2)
        for t, d in both:
            ag_copy(j, t, 3, d, False).start()

    def gathered(j):
        h = lax.div(j, QUADS)
        c = lax.rem(j, QUADS)
        ag_arrive(j, 3)
        for step in range(4):
            for t, d in both:
                ag_copy(j, t, step, d, False, None).wait_send()

        @pl.when(j == 0)
        def _():
            for load in loads:
                load.wait()

        @pl.loop(0, 2)
        def _(b):
            rows = rows_of(h * 2 + b, PLANE // 2)
            for n, weight in enumerate((w_gate, w_up)):
                total = acc[n, rows, :]
                for t in range(2):
                    total += jnp.dot(
                        xg[2 * j + t, pl.ds(b * 2, 2)].reshape(PLANE // 2, WIDTH),
                        weight[columns_of(2 * c + t), :],
                        preferred_element_type=f32,
                    )
                acc[n, rows, :] = total

        @pl.when(c == QUADS - 1)
        def _():
            @pl.loop(0, 8)
            def _(b):
                rows = rows_of(h * 8 + b, PLANE // 8)
                gate = acc[0, rows, :]
                act[rows, :] = (gate / (1.0 + jnp.exp(-gate)) * acc[1, rows, :]).astype(bf16)


    def rs_copy(j, t, step, d):
        near, far = axes[t]
        p = part.at[lax.rem(j, 4), t]
        room = xg.at[2 * j + t]
        if step == 0:
            src = along(far, p, around(far, 2), halves[d])
            dst, to = room.at[0, halves[d]], far
        elif step == 1:
            src = along(far, p, around(far, d), every)
            dst, to = room.at[1 + slot[d]], far
        elif step == 2:
            src = line.at[lax.rem(j, 4), t, around(near, 2), half_rows[d]]
            dst, to = room.at[3, 0, half_rows[d]], near
        else:
            src = line.at[lax.rem(j, 4), t, around(near, d)]
            dst, to = room.at[3, 1 + slot[d]], near
        m = step * 2 + slot[d]
        return remote(src, dst, rs_send.at[j, t, m], rs_recv.at[j, t, m], neighbour(to, d))

    def rs_start(j, step, t):
        for d in (1, -1):
            rs_copy(j, t, step, d).start()

    def rs_arrive(j, step, t):
        for d in (1, -1):
            rs_copy(j, t, step, d).wait_recv()

    def rs_sent(j, steps):
        for step in steps:
            for t, d in both:
                rs_copy(j, t, step, d).wait_send()

    def sum_start(j):
        h = lax.div(j, QUADS)
        c = lax.rem(j, QUADS)

        @pl.loop(0, 2)
        def _(b):
            rows = rows_of(h * 2 + b, PLANE // 2)
            for t in range(2):
                term = lax.dot_general(
                    act[rows, :],
                    w_down[columns_of(2 * c + t), :],
                    (((1,), (1,)), ((), ())),
                    preferred_element_type=f32,
                )
                part[lax.rem(j, 4), t, pl.ds(b * 2, 2)] = term.astype(bf16).reshape(
                    2, SIDE, PIECE, WIDTH
                )

        for t in range(2):
            rs_start(j, 0, t)

    def sum_first(j):
        s = lax.rem(j, 4)
        for t in range(2):
            far = axes[t][1]
            rs_arrive(j, 0, t)
            for d in (1, -1):
                base = 0 if d == 1 else SIDE // 2
                place = around(far, d)

                @pl.loop(0, SIDE // 2)
                def _(i):
                    at = (place, base + i) if far == "z" else (base + i, place)
                    part[s, t, at[0], at[1]] = (
                        part[s, t, at[0], at[1]].astype(f32)
                        + xg[2 * j + t, 0, base + i].astype(f32)
                    ).astype(bf16)

            rs_start(j, 1, t)

    def sum_second(j):
        s = lax.rem(j, 4)
        for t in range(2):
            far = axes[t][1]
            rs_arrive(j, 1, t)

            @pl.loop(0, SIDE)
            def _(i):
                at = (my[far], i) if far == "z" else (i, my[far])
                line[s, t, i] = (
                    part[s, t, at[0], at[1]].astype(f32)
                    + xg[2 * j + t, 1, i].astype(f32)
                    + xg[2 * j + t, 2, i].astype(f32)
                ).astype(bf16)

            rs_start(j, 2, t)
        rs_sent(j, (0, 1))

    def sum_third(j):
        s = lax.rem(j, 4)
        for t in range(2):
            rs_arrive(j, 2, t)
            for d in (1, -1):
                at = around(axes[t][0], d)
                line[s, t, at, half_rows[d]] = (
                    line[s, t, at, half_rows[d]].astype(f32)
                    + xg[2 * j + t, 3, 0, half_rows[d]].astype(f32)
                ).astype(bf16)
            rs_start(j, 3, t)


    def back_copy(j, t, o):
        other = lax.rem(my_exp + o, GROUPS)
        k = 2 * lax.rem(j, QUADS) + t
        return remote(
            sums.at[lax.rem(j, 2), t, other],
            returned.at[k, rows_of(owner, BLOCK)],
            back_send.at[2 * j + t],
            back_recv.at[k],
            {"exp": other, "dp": lax.div(j, QUADS)},
        )

    def sum_last(j):
        mine = my_dp == lax.div(j, QUADS)
        for t in range(2):
            rs_arrive(j, 3, t)
            total = (
                line[lax.rem(j, 4), t, my[axes[t][0]]].astype(f32)
                + xg[2 * j + t, 3, 1].astype(f32)
                + xg[2 * j + t, 3, 2].astype(f32)
            )
            s = lax.rem(j, 2)
            sums[s, t] = total.astype(bf16).reshape(GROUPS, BLOCK, WIDTH)
            for o in range(1, GROUPS):
                back_copy(j, t, o).start()

            @pl.when(mine)
            def _():
                k = 2 * lax.rem(j, QUADS) + t
                returned[k, rows_of(owner, BLOCK)] = sums[s, t, my_exp]

            @pl.when(jnp.logical_not(mine))
            def _():
                back_copy(j, t, 0).start()

        rs_sent(j, (2, 3))

    def sum_back(j):
        mine = my_dp == lax.div(j, QUADS)
        for t in range(2):
            q = 2 * lax.rem(j, QUADS) + t

            def sent(count):
                ref = sums.at[lax.rem(j, 2), t, pl.ds(0, count)]
                remote(
                    ref, ref, back_send.at[2 * j + t], back_recv.at[0], partner(1)[1]
                ).wait_send()

            @pl.when(mine)
            def _():
                ref = returned.at[q, pl.ds(0, (EXPERTS - 1) * BLOCK)]
                remote(ref, ref, back_send.at[0], back_recv.at[q], partner(1)[1]).wait_recv()
                columns = columns_of(q)
                total = hidden[:, columns].astype(f32)
                for n in range(2):
                    total = total + lax.dot_general(
                        shares[n],
                        returned[q],
                        (((0,), (0,)), ((), ())),
                        preferred_element_type=f32,
                    )
                out_ref[:, columns] = total.astype(bf16)
                sent(GROUPS - 1)

            pl.when(jnp.logical_not(mine))(functools.partial(sent, GROUPS))

    def weigh():
        match = [
            lax.broadcasted_iota(jnp.int32, (EXPERTS, TOKENS), 0) == chosen_ref[i : i + 1, :]
            for i in range(2)
        ]
        picked = [jnp.sum(jnp.where(m, logits[...], 0.0), axis=0, keepdims=True) for m in match]
        weights = jnp.zeros((EXPERTS * BLOCK, TOKENS), f32)
        for i in range(2):
            share = 1.0 / (1.0 + jnp.exp(picked[1 - i] - picked[i]))
            weights = weights + jnp.where(place_id == target[i : i + 1, :], share, 0.0)
        coarse = weights.astype(bf16)
        shares[0] = coarse
        shares[1] = (weights - coarse.astype(f32)).astype(bf16)

    def stages(tick, count, steps):
        for lag, action in steps:
            pl.when(jnp.logical_and(tick >= lag, tick < count + lag))(
                functools.partial(action, tick - lag)
            )

    @pl.loop(0, 1 + SUMS + PAIRS + LAST)
    def _(turn):
        tick = turn - 1
        own = tick - my_dp * QUADS
        stages(
            tick,
            PAIRS,
            ((5, gather_last), (4, gather_third), (3, gather_second), (2, gather_first)),
        )
        stages(tick - SUMS, PAIRS, ((4, sum_second), (2, sum_first)))
        stages(own, QUADS, ((3, rows_sent), (1, tokens), (-1, mix)))
        stages(tick, PAIRS, ((6, gathered),))
        pl.when(tick == SUMS)(weigh)
        stages(
            tick - SUMS,
            PAIRS,
            ((0, sum_start), (5, sum_third), (6, sum_last), (7, sum_back)),
        )


def layer(*args):
    units = args[-1].shape[1]
    bf16, f32 = jnp.bfloat16, jnp.float32
    any_space = pl.BlockSpec(memory_space=pl.ANY)
    vmem = pl.BlockSpec(memory_space=pltpu.VMEM)
    smem = pl.BlockSpec(memory_space=pltpu.SMEM)
    return pl.pallas_call(
        layer_kernel,
        out_shape=jax.ShapeDtypeStruct((TOKENS, D), bf16),
        in_specs=[any_space] * 5
        + [smem, vmem]
        + [any_space] * 4
        + [vmem] * 3
        + [any_space] * 3,
        out_specs=vmem,
        scratch_shapes=[
            pltpu.VMEM((LENGTH, INNER), bf16),
            pltpu.VMEM((LENGTH, INNER), bf16),
            pltpu.VMEM((LENGTH, STATE), bf16),
            pltpu.VMEM((LENGTH, STATE), bf16),
            pltpu.VMEM((HEADS, LENGTH), f32),
            pltpu.VMEM((SIZE, STATE), f32),
            pltpu.VMEM((TOKENS, D), bf16),
            pltpu.VMEM((EXPERTS, D), bf16),
            pltpu.VMEM((LENGTH, INNER), f32),
            pltpu.VMEM((CTX, MESSAGE, STATE), bf16),
            pltpu.VMEM((CTX, MESSAGE, STATE), bf16),
            pltpu.VMEM((CTX, SIZE, STATE), bf16),
            pltpu.VMEM((CTX, SIZE, STATE), bf16),
            pltpu.VMEM((LENGTH, INNER), bf16),
            pltpu.VMEM((2, 2, GROUPS, TOKENS, WIDTH), bf16),
            pltpu.VMEM((2 * QUADS, GROUPS - 1, TOKENS, WIDTH), bf16),
            pltpu.VMEM((TOKENS, D), bf16),
            pltpu.VMEM((EXPERTS * BLOCK, TOKENS), bf16),
            pltpu.VMEM((2, EXPERTS * BLOCK, TOKENS), bf16),
            pltpu.VMEM((EXPERTS, TOKENS), f32),
            pltpu.VMEM((2, 2, EXPERTS, BLOCK, WIDTH), bf16),
            pltpu.VMEM((2, 2, GROUPS, BLOCK, WIDTH), bf16),
            pltpu.VMEM((2 * QUADS, EXPERTS * BLOCK, WIDTH), bf16),
            pltpu.VMEM((2 * PAIRS, SIDE, SIDE, PIECE, WIDTH), bf16),
            pltpu.VMEM((2, 2 * PLANE, units), f32),
            pltpu.VMEM((2 * PLANE, units), bf16),
            pltpu.VMEM((D, units), bf16),
            pltpu.VMEM((D, units), bf16),
            pltpu.VMEM((D, units), bf16),
            pltpu.VMEM((4, 2, SIDE, SIDE, PIECE, WIDTH), bf16),
            pltpu.VMEM((4, 2, SIDE, PIECE, WIDTH), bf16),
            pltpu.SemaphoreType.DMA((PAIRS, 2, 8)),
            pltpu.SemaphoreType.DMA((PAIRS, 2, 8)),
            pltpu.SemaphoreType.DMA((PAIRS, 2, 8)),
            pltpu.SemaphoreType.DMA((PAIRS, 2, 8)),
            pltpu.SemaphoreType.DMA((2 * QUADS, GROUPS - 1)),
            pltpu.SemaphoreType.DMA((2 * QUADS, GROUPS - 1)),
            pltpu.SemaphoreType.DMA((2 * QUADS,)),
            pltpu.SemaphoreType.DMA((2 * PAIRS,)),
            pltpu.SemaphoreType.DMA((2 * PAIRS,)),
            pltpu.SemaphoreType.DMA((2 * QUADS,)),
            pltpu.SemaphoreType.DMA((3,)),
            pltpu.SemaphoreType.DMA((2 * QUADS,)),
            pltpu.SemaphoreType.DMA((8,)),
            pltpu.SemaphoreType.DMA((CTX,)),
            pltpu.SemaphoreType.DMA((CTX,)),
            pltpu.SemaphoreType.DMA((CTX,)),
            pltpu.SemaphoreType.DMA((CTX,)),
        ],
        compiler_params=pltpu.CompilerParams(
            collective_id=0, has_side_effects=True, vmem_limit_bytes=62 << 20
        ),
        cost_estimate=pl.CostEstimate(
            flops=6 * 2048 * D * 512, bytes_accessed=24 << 20, transcendentals=1 << 20
        ),
    )(*args)


def shards(
    mixer_in,
    gate_in,
    state_write,
    state_read,
    decay_rate,
    skip_gain,
    norm_gain,
    start_state,
    out_weight,
    residual,
    router_weight,
    chosen,
    slot_index,
    spill_index,
    gate_weight,
    up_weight,
    down_weight,
):
    return layer(
        mixer_in[0],
        gate_in[0],
        state_write[0, :, 0],
        state_read[0, :, 0],
        decay_rate[0],
        skip_gain,
        norm_gain[None],
        start_state[0].reshape(HEADS * SIZE, STATE),
        out_weight.reshape(SIDE, SIDE, PIECE, D),
        residual[0],
        router_weight.T,
        chosen[0].T,
        slot_index[0].T,
        spill_index[0].T,
        gate_weight[0],
        up_weight[0],
        down_weight[0],
    )[None]


def solution(mesh):
    placed = (
        P("dp", "ctx", "exp"),
        P("dp", "ctx", "exp"),
        P("dp", "ctx", "exp", None),
        P("dp", "ctx", "exp", None),
        P("dp", "exp", "ctx"),
        P("exp"),
        P("exp"),
        P("dp", "exp", None, None),
        P("exp", None),
        P("dp", ("ctx", "exp"), None),
        P(),
        P("dp", ("ctx", "exp"), None),
        P("dp", ("ctx", "exp"), None),
        P("dp", ("ctx", "exp"), None),
        P(("exp", "dp"), None, "ctx"),
        P(("exp", "dp"), None, "ctx"),
        P(("exp", "dp"), None, "ctx"),
    )
    return jax.shard_map(
        shards, mesh=mesh, in_specs=placed, out_specs=P("dp", ("ctx", "exp"), None), check_vma=False
    )
```

```python
import functools

import jax
import jax.numpy as jnp
from jax import lax
from jax.experimental import pallas as pl
from jax.experimental.pallas import tpu as pltpu
from jax.sharding import PartitionSpec as P

D = 4096
EXPERTS = 8
CAP = 14
BLOCK = 16
TOKENS = 64
GROUPS = 4
SIDE = 4
WIDTH = 512
QUADS = D // WIDTH // 2
PAIRS = 2 * QUADS
PIECE = GROUPS * BLOCK
HALF = PIECE // 2
PLANE = SIDE * SIDE * PIECE
HEADS = 16
SIZE = 64
STATE = 128
CTX = SIDE * SIDE
LENGTH = 256
INNER = HEADS * SIZE
MESSAGE = SIZE + 16
EARLY = 3
APART = QUADS - 1
ROUNDS = 2 * APART + 1
SUMS = 10
LAST = 7
MESH = pl.DeviceIdType.MESH


def layer_kernel(
    mixer_ref,
    switch_ref,
    write_ref,
    read_ref,
    decay_ref,
    skip_ref,
    gain_ref,
    start_ref,
    mix_ref,
    residual_ref,
    router_ref,
    chosen_ref,
    slot_ref,
    spill_ref,
    gate_ref,
    up_ref,
    down_ref,
    out_ref,
    mixer,
    switch,
    write,
    read,
    decay,
    start,
    residual,
    router,
    chosen,
    slots,
    spills,
    skips,
    gains,
    out,
    inner,
    states,
    gathered_states,
    entering,
    entered,
    normed,
    pool,
    hidden,
    placing,
    shares,
    logits,
    leaving,
    sums,
    returned,
    xg,
    acc,
    act,
    w_gate,
    w_up,
    w_down,
    part,
    line,
    apart,
    weights,
    ag_send,
    ag_recv,
    rs_send,
    rs_recv,
    mix_send,
    mix_recv,
    row_send,
    row_recv,
    back_send,
    back_recv,
    apart_send,
    apart_recv,
    weight_send,
    weight_recv,
    ready,
    load_sem,
    mix_sem,
    input_sem,
    done_sem,
    out_send,
    out_recv,
    in_send,
    in_recv,
):
    f32, bf16 = jnp.float32, jnp.bfloat16
    here = lax.axis_index("ctx")
    my = {"x": lax.rem(here, SIDE), "z": lax.div(here, SIDE)}
    my_exp, my_dp = lax.axis_index("exp"), lax.axis_index("dp")
    owner = my_exp * 2 + my_dp

    def around(axis, step):
        return lax.rem(my[axis] + step + SIDE, SIDE)

    def neighbour(axis, step):
        other = around(axis, step)
        if axis == "x":
            return {"ctx": my["z"] * SIDE + other}
        return {"ctx": other * SIDE + my["x"]}

    def along(axis, ref, place, at):
        if axis == "z":
            return ref.at[place, at]
        return ref.at[at, place]

    def partner(o):
        other = lax.rem(owner + o, EXPERTS)
        return other, {"exp": lax.div(other, 2), "dp": lax.rem(other, 2)}

    def remote(src, dst, send, recv, place):
        return pltpu.make_async_remote_copy(
            src_ref=src,
            dst_ref=dst,
            send_sem=send,
            recv_sem=recv,
            device_id=place,
            device_id_type=MESH,
        )

    def columns_of(q):
        return pl.ds(pl.multiple_of(q * WIDTH, WIDTH), WIDTH)

    def rows_of(index, count):
        return pl.ds(pl.multiple_of(index * count, count), count)

    def mix_room(q):
        return part.at[lax.div(q, 2), lax.rem(q, 2)]

    def mix_load(q):
        return pltpu.make_async_copy(
            mix_ref.at[:, :, :, columns_of(q)], mix_room(q), mix_sem.at[q]
        )

    barrier = pltpu.get_barrier_semaphore()

    def greet(k, _):
        other = lax.rem(here + k, CTX)
        pl.semaphore_signal(barrier, inc=1, device_id={"ctx": other}, device_id_type=MESH)
        return 0

    lax.fori_loop(1, CTX, greet, 0)
    for o in range(1, EXPERTS):
        pl.semaphore_signal(barrier, inc=1, device_id=partner(o)[1], device_id_type=MESH)

    inputs = {
        name: pltpu.make_async_copy(src, dst, input_sem.at[i])
        for i, (name, src, dst) in enumerate(
            (
                ("decay", decay_ref, decay),
                ("mixer", mixer_ref, mixer),
                ("write", write_ref, write),
                ("read", read_ref, read),
                ("start", start_ref.at[rows_of(here, SIZE), :], start),
                ("switch", switch_ref, switch),
                ("residual", residual_ref, residual),
                ("router", router_ref, router),
                ("skip", skip_ref, skips),
                ("gain", gain_ref, gains),
                ("chosen", chosen_ref, chosen),
                ("slots", slot_ref, slots),
                ("spills", spill_ref, spills),
            )
        )
    }
    for copy in inputs.values():
        copy.start()
    loads = [
        pltpu.make_async_copy(src, dst, load_sem.at[i])
        for i, (src, dst) in enumerate(((gate_ref, w_gate), (up_ref, w_up), (down_ref, w_down)))
    ]


    row_id = lax.broadcasted_iota(jnp.int32, (LENGTH, LENGTH), 0)
    col_id = lax.broadcasted_iota(jnp.int32, (LENGTH, LENGTH), 1)
    causal = row_id >= col_id
    upper = jnp.where(row_id <= col_id, 1.0, 0.0).astype(f32)
    inputs["decay"].wait()
    levels = jnp.dot(
        decay[...], upper, precision=lax.Precision.HIGHEST, preferred_element_type=f32
    )
    last = levels[:, LENGTH - 1 : LENGTH]
    to_end = jnp.exp(levels - last).T
    total_decay = jnp.exp(-last)
    levels_t = levels.T
    from_start = jnp.exp(-levels_t)
    low = lax.broadcasted_iota(jnp.int32, (LENGTH, 2 * SIZE), 1) < SIZE
    top = lax.broadcasted_iota(jnp.int32, (16, STATE), 0) < 8

    def spread(columns, q):
        return jnp.where(low, columns[:, 2 * q : 2 * q + 1], columns[:, 2 * q + 1 : 2 * q + 2])

    inputs["mixer"].wait()
    inputs["write"].wait()
    for q in range(HEADS // 2):
        lanes = pl.ds(q * 2 * SIZE, 2 * SIZE)
        scaled = (spread(to_end, q) * mixer[:, lanes].astype(f32)).astype(bf16)
        local = lax.dot_general(
            scaled, write[...], (((0,), (0,)), ((), ())), preferred_element_type=f32
        )
        for i in range(2):
            h = 2 * q + i
            states[h, 0:SIZE] = local[i * SIZE : (i + 1) * SIZE].astype(bf16)
            value = jnp.broadcast_to(total_decay[h : h + 1, :], (16, STATE))
            coarse = value.astype(bf16)
            rest = (value - coarse.astype(f32)).astype(bf16)
            states[h, SIZE:MESSAGE] = jnp.where(top, coarse, rest)

    pl.semaphore_wait(barrier, CTX - 1 + EXPERTS - 1)

    def out_copy(k):
        other = lax.rem(here + k, CTX)
        return remote(
            states.at[other],
            gathered_states.at[here],
            out_send.at[k],
            out_recv.at[k],
            {"ctx": other},
        )

    def in_copy(k):
        other = lax.rem(here + k, CTX)
        return remote(
            entering.at[other], entered.at[here], in_send.at[k], in_recv.at[k], {"ctx": other}
        )

    def each(action):
        def step(k, _):
            action(k)
            return 0

        lax.fori_loop(1, CTX, step, 0)

    each(lambda k: out_copy(k).start())
    gathered_states[here] = states[here]

    def load_mix(q, _):
        mix_load(q).start()
        return 0

    lax.fori_loop(0, 2 * QUADS, load_mix, 0)
    for load in loads:
        load.start()


    inputs["read"].wait()
    inputs["skip"].wait()
    meet = lax.dot_general(
        read[...], write[...], (((1,), (1,)), ((), ())), preferred_element_type=f32
    )

    def within(q):
        lanes = pl.ds(q * 2 * SIZE, 2 * SIZE)
        pair = mixer[:, lanes]
        heads = []
        for i in range(2):
            h = 2 * q + i
            span = levels[h : h + 1, :] - levels_t[:, h : h + 1]
            weight = jnp.exp(jnp.where(causal, span, -1e30)) * meet
            heads.append(jnp.dot(weight.astype(bf16), pair, preferred_element_type=f32))
        skip = spread(skips[...], q)
        inner[:, lanes] = jnp.where(low, heads[0], heads[1]) + skip * pair.astype(f32)

    for q in range(EARLY):
        within(q)


    inputs["start"].wait()
    each(lambda k: out_copy(k).wait_recv())
    state = start[...]
    for k in range(CTX):
        entering[k] = state.astype(bf16)
        if k < CTX - 1:
            factor = gathered_states[k, SIZE:MESSAGE].astype(f32)
            factor = factor[0:1, :] + factor[8:9, :]
            state = factor * state + gathered_states[k, 0:SIZE].astype(f32)
    each(lambda k: in_copy(k).start())
    entered[here] = entering[here]

    for q in range(EARLY, HEADS // 2):
        within(q)

    for name in ("chosen", "slots", "spills", "gain"):
        inputs[name].wait()

    place_id = lax.broadcasted_iota(jnp.int32, (EXPERTS * BLOCK, TOKENS), 0)
    expert_ids, slot_ids, spill_ids = chosen[...], slots[...], spills[...]
    target = jnp.where(
        slot_ids >= 0,
        expert_ids * BLOCK + slot_ids,
        jnp.where(
            spill_ids >= 0,
            jnp.right_shift(spill_ids, 1) * BLOCK + CAP + jnp.bitwise_and(spill_ids, 1),
            -1,
        ),
    )
    places = [place_id == target[i : i + 1, :] for i in range(2)]
    placing[...] = (places[0].astype(f32) + places[1].astype(f32)).astype(bf16)
    logits[...] = jnp.zeros_like(logits)
    acc[...] = jnp.zeros_like(acc)

    inputs["switch"].wait()
    each(lambda k: in_copy(k).wait_recv())
    square = jnp.zeros((LENGTH, 1), f32)
    for q in range(HEADS // 2):
        lanes = pl.ds(q * 2 * SIZE, 2 * SIZE)
        carried = lax.dot_general(
            read[...],
            entered[2 * q : 2 * q + 2].reshape(2 * SIZE, STATE),
            (((1,), (1,)), ((), ())),
            preferred_element_type=f32,
        )
        gate = switch[:, lanes].astype(f32)
        gated = (inner[:, lanes] + carried * spread(from_start, q)) * (
            gate / (1.0 + jnp.exp(-gate))
        )
        inner[:, lanes] = gated
        square = square + jnp.sum(gated * gated, axis=1, keepdims=True)
    scale = lax.rsqrt(square / INNER + 1e-05)
    for q in range(HEADS // 2):
        lanes = pl.ds(q * 2 * SIZE, 2 * SIZE)
        normed[:, lanes] = (inner[:, lanes] * scale * gains[:, lanes]).astype(bf16)

    inputs["residual"].wait()
    inputs["router"].wait()
    each(lambda k: out_copy(k).wait_send())
    each(lambda k: in_copy(k).wait_send())

    every = pl.ds(0, SIDE)
    halves = {1: pl.ds(0, SIDE // 2), -1: pl.ds(SIDE // 2, SIDE // 2)}
    half_rows = {1: pl.ds(0, HALF), -1: pl.ds(HALF, HALF)}
    axes = (("x", "z"), ("z", "x"))
    slot = {1: 0, -1: 1}
    both = [(t, d) for t in range(2) for d in (1, -1)]


    def mixed(c, t):
        return pool.at[lax.rem(c, 2) * 2 + t]

    def term(q, i):
        b = q * (GROUPS - 1) + i - 1
        return pool.at[4 + lax.div(b, GROUPS), lax.rem(b, GROUPS)]

    def term_copy(c, t, i):
        other = lax.rem(my_exp + i, GROUPS)
        q = 2 * c + t
        return remote(
            mixed(c, t).at[other],
            term(q, i),
            mix_send.at[q, i - 1],
            mix_recv.at[q, i - 1],
            {"exp": other},
        )

    def mix(c):
        for t in range(2):
            q = 2 * c + t
            mix_load(q).wait()
            value = jnp.dot(
                normed[...],
                mix_room(q)[...].reshape(INNER, WIDTH),
                preferred_element_type=f32,
            )
            mixed(c, t)[...] = value.astype(bf16).reshape(GROUPS, TOKENS, WIDTH)
            for i in range(1, GROUPS):
                term_copy(c, t, i).start()


    def row_copy(c, t, o):
        other, place = partner(o)
        k = 2 * (my_dp * QUADS + c) + t
        return remote(
            leaving.at[lax.rem(c, 2), t, other],
            xg.at[k, my["z"], my["x"], rows_of(my_exp, BLOCK)],
            row_send.at[2 * c + t],
            row_recv.at[k],
            place,
        )

    def tokens(c):
        for t in range(2):
            q = 2 * c + t
            columns = columns_of(q)
            for i in range(1, GROUPS):
                term_copy(c, t, i).wait_recv()
            total = mixed(c, t)[my_exp].astype(f32)
            for i in range(1, GROUPS):
                total = total + term(q, i)[...].astype(f32)
            value = (residual[:, columns].astype(f32) + total).astype(bf16)
            hidden[:, columns] = value
            rows = jnp.dot(placing[...], value, preferred_element_type=f32).astype(bf16)
            leaving[lax.rem(c, 2), t] = rows.reshape(EXPERTS, BLOCK, WIDTH)
            for o in range(1, EXPERTS):
                row_copy(c, t, o).start()
            k = 2 * (my_dp * QUADS + c) + t
            xg[k, my["z"], my["x"], rows_of(my_exp, BLOCK)] = leaving[lax.rem(c, 2), t, owner]
            logits[...] += lax.dot_general(
                router[:, columns],
                value,
                (((1,), (1,)), ((), ())),
                preferred_element_type=f32,
            )
        for t in range(2):
            for i in range(1, GROUPS):
                term_copy(c, t, i).wait_send()

    def rows_sent(c):
        for t in range(2):
            ref = leaving.at[lax.rem(c, 2), t, pl.ds(0, EXPERTS - 1)]
            remote(ref, ref, row_send.at[2 * c + t], row_recv.at[0], partner(1)[1]).wait_send()


    def ag_copy(j, t, step, d, landing, off=0):
        near, far = axes[t]
        chunk = xg.at[2 * j + t]
        back = -d if landing else 0
        if step == 0:
            ref, to = along(near, chunk, around(near, back), my[far]), near
        elif step == 1:
            ref = along(near, chunk, around(near, -2 * d if landing else -d), my[far])
            ref, to = ref.at[half_rows[d]], near
        elif step == 2 and off is None:
            ref, to = along(far, chunk, around(far, back), every), far
        elif step == 2:
            ref, to = along(near, chunk, around(near, off), my[far]), far
        else:
            ref = along(far, chunk, around(far, -2 * d if landing else -d), halves[d])
            to = far
        m = step * 2 + slot[d]
        return remote(ref, ref, ag_send.at[j, t, m], ag_recv.at[j, t, m], neighbour(to, d))

    def ag_arrive(j, step):
        for t, d in both:
            ag_copy(j, t, step, d, True, None).wait_recv()

    def gather_first(j):
        mine = my_dp == lax.div(j, QUADS)
        for t in range(2):
            k = 2 * j + t

            def arrive(count):
                ref = xg.at[k, my["z"], my["x"], pl.ds(0, count)]
                remote(ref, ref, row_send.at[0], row_recv.at[k], partner(1)[1]).wait_recv()

            pl.when(mine)(functools.partial(arrive, PIECE - BLOCK))
            pl.when(jnp.logical_not(mine))(functools.partial(arrive, PIECE))
            for d in (1, -1):
                ag_copy(j, t, 0, d, False).start()
        for t, d in both:
            ag_copy(j, t, 2, d, False, 0).start()

    def gather_second(j):
        ag_arrive(j, 0)
        for t, d in both:
            ag_copy(j, t, 1, d, False).start()
        for t, d in both:
            for off in (1, -1):
                ag_copy(j, t, 2, d, False, off).start()

    def gather_third(j):
        ag_arrive(j, 1)
        for t, d in both:
            ag_copy(j, t, 2, d, False, 2).start()

    def gather_last(j):
        ag_arrive(j, 2)
        for t, d in both:
            ag_copy(j, t, 3, d, False).start()

    def gathered(j):
        h = lax.div(j, QUADS)
        c = lax.rem(j, QUADS)
        ag_arrive(j, 3)
        for step in range(4):
            for t, d in both:
                ag_copy(j, t, step, d, False, None).wait_send()

        @pl.when(j == 0)
        def _():
            for load in loads:
                load.wait()

        @pl.loop(0, 2)
        def _(b):
            rows = rows_of(h * 2 + b, PLANE // 2)
            for n, weight in enumerate((w_gate, w_up)):
                total = acc[n, rows, :]
                for t in range(2):
                    total += jnp.dot(
                        xg[2 * j + t, pl.ds(b * 2, 2)].reshape(PLANE // 2, WIDTH),
                        weight[columns_of(2 * c + t), :],
                        preferred_element_type=f32,
                    )
                acc[n, rows, :] = total

        @pl.when(j == QUADS - 1)
        def _():
            for o in range(1, EXPERTS):
                pl.semaphore_signal(ready, inc=1, device_id=partner(o)[1], device_id_type=MESH)

        @pl.when(c == QUADS - 1)
        def _():
            @pl.loop(0, 8)
            def _(b):
                rows = rows_of(h * 8 + b, PLANE // 8)
                gate = acc[0, rows, :]
                act[rows, :] = (gate / (1.0 + jnp.exp(-gate)) * acc[1, rows, :]).astype(bf16)


    def room_of(j, t):
        pair = j + lax.div(j, APART) - lax.div(j, 2 * APART)
        return xg.at[2 * pair + t]

    def rs_copy(j, t, step, d):
        near, far = axes[t]
        p = part.at[lax.rem(j, 4), t]
        room = room_of(j, t)
        if step == 0:
            src = along(far, p, around(far, 2), halves[d])
            dst, to = room.at[0, halves[d]], far
        elif step == 1:
            src = along(far, p, around(far, d), every)
            dst, to = room.at[1 + slot[d]], far
        elif step == 2:
            src = line.at[lax.rem(j, 4), t, around(near, 2), half_rows[d]]
            dst, to = room.at[3, 0, half_rows[d]], near
        else:
            src = line.at[lax.rem(j, 4), t, around(near, d)]
            dst, to = room.at[3, 1 + slot[d]], near
        m = step * 2 + slot[d]
        return remote(src, dst, rs_send.at[j, t, m], rs_recv.at[j, t, m], neighbour(to, d))

    def rs_start(j, step, t):
        for d in (1, -1):
            rs_copy(j, t, step, d).start()

    def rs_arrive(j, step, t):
        for d in (1, -1):
            rs_copy(j, t, step, d).wait_recv()

    def rs_sent(j, steps):
        for step in steps:
            for t, d in both:
                rs_copy(j, t, step, d).wait_send()

    def down(h, b, q):
        rows = rows_of(h * 2 + b, PLANE // 2)
        value = lax.dot_general(
            act[rows, :],
            w_down[columns_of(q), :],
            (((1,), (1,)), ((), ())),
            preferred_element_type=f32,
        )
        return value.astype(bf16)

    def by_rows(j):
        h = lax.div(j, APART)
        c = lax.rem(j, APART)

        @pl.loop(0, 2)
        def _(b):
            for t in range(2):
                part[lax.rem(j, 4), t, pl.ds(b * 2, 2)] = down(h, b, 2 * c + t).reshape(
                    2, SIDE, PIECE, WIDTH
                )


    def apart_room(t, e):
        if t == 0:
            return xg.at[2 * APART + lax.div(e, SIDE), lax.rem(e, SIDE)]
        return pool.at[e]

    def apart_copy(h, t, o):
        other = lax.rem(my_exp + o, GROUPS)
        return remote(
            apart.at[t, other],
            apart_room(t, owner),
            apart_send.at[h, t],
            apart_recv.at[t],
            {"exp": other, "dp": h},
        )

    def apart_sent(h):
        for t in range(2):

            def sent(count):
                ref = pool.at[pl.ds(0, count)]
                remote(
                    ref, ref, apart_send.at[h, t], apart_recv.at[0], partner(1)[1]
                ).wait_send()

            pl.when(my_dp == h)(functools.partial(sent, GROUPS - 1))
            pl.when(my_dp != h)(functools.partial(sent, GROUPS))

    def apart_start(h):
        if h == 0:
            pl.semaphore_wait(ready, EXPERTS - 1)
        else:
            apart_sent(0)
        for t in range(2):

            @pl.loop(0, 2)
            def _(b):
                value = down(h, b, 2 * APART + t)
                for i in range(2):
                    for x in range(SIDE):
                        for y in range(GROUPS):
                            low_row = (i * SIDE + x) * PIECE + y * BLOCK
                            apart[t, y, 2 * b + i, x * BLOCK : (x + 1) * BLOCK] = value[
                                low_row : low_row + BLOCK
                            ]

            for o in range(1, GROUPS):
                apart_copy(h, t, o).start()

            @pl.when(my_dp == h)
            def _():
                apart_room(t, owner)[...] = apart[t, my_exp]

            @pl.when(my_dp != h)
            def _():
                apart_copy(h, t, 0).start()

    def weight_copy(k):
        other = lax.rem(here + k, CTX)
        return remote(
            weights.at[here],
            weights.at[here],
            weight_send.at[k],
            weight_recv.at[k],
            {"ctx": other},
        )

    def by_tokens(j):
        each(lambda k: weight_copy(k).wait_recv())
        for t in range(2):
            ref = pool.at[pl.ds(0, EXPERTS - 1)]
            remote(ref, ref, apart_send.at[0, 0], apart_recv.at[t], partner(1)[1]).wait_recv()

            @pl.loop(0, SIDE)
            def _(z):
                for x in range(SIDE):
                    rows = jnp.concatenate(
                        [
                            apart_room(t, e)[z, x * BLOCK : (x + 1) * BLOCK]
                            for e in range(EXPERTS)
                        ],
                        axis=0,
                    )
                    value = jnp.dot(
                        weights[z * SIDE + x], rows, preferred_element_type=f32
                    )
                    part[lax.rem(j, 4), t, z, x] = value.astype(bf16)

    def sum_start(j):
        pl.when(j < 2 * APART)(functools.partial(by_rows, j))
        pl.when(j == 2 * APART)(functools.partial(by_tokens, j))
        for t in range(2):
            rs_start(j, 0, t)

    def sum_first(j):
        s = lax.rem(j, 4)
        for t in range(2):
            far = axes[t][1]
            rs_arrive(j, 0, t)
            for d in (1, -1):
                base = 0 if d == 1 else SIDE // 2
                place = around(far, d)

                @pl.loop(0, SIDE // 2)
                def _(i):
                    at = (place, base + i) if far == "z" else (base + i, place)
                    part[s, t, at[0], at[1]] = (
                        part[s, t, at[0], at[1]].astype(f32)
                        + room_of(j, t)[0, base + i].astype(f32)
                    ).astype(bf16)

            rs_start(j, 1, t)

    def sum_second(j):
        s = lax.rem(j, 4)
        for t in range(2):
            far = axes[t][1]
            rs_arrive(j, 1, t)

            @pl.loop(0, SIDE)
            def _(i):
                at = (my[far], i) if far == "z" else (i, my[far])
                line[s, t, i] = (
                    part[s, t, at[0], at[1]].astype(f32)
                    + room_of(j, t)[1, i].astype(f32)
                    + room_of(j, t)[2, i].astype(f32)
                ).astype(bf16)

            rs_start(j, 2, t)
        rs_sent(j, (0, 1))

    def sum_third(j):
        s = lax.rem(j, 4)
        for t in range(2):
            rs_arrive(j, 2, t)
            for d in (1, -1):
                at = around(axes[t][0], d)
                line[s, t, at, half_rows[d]] = (
                    line[s, t, at, half_rows[d]].astype(f32)
                    + room_of(j, t)[3, 0, half_rows[d]].astype(f32)
                ).astype(bf16)
            rs_start(j, 3, t)


    def back_copy(j, t, o):
        other = lax.rem(my_exp + o, GROUPS)
        k = 2 * lax.rem(j, APART) + t
        return remote(
            sums.at[lax.rem(j, 2), t, other],
            returned.at[k, rows_of(owner, BLOCK)],
            back_send.at[2 * j + t],
            back_recv.at[k],
            {"exp": other, "dp": lax.div(j, APART)},
        )

    def sum_last(j):
        mine = my_dp == lax.div(j, APART)
        for t in range(2):
            rs_arrive(j, 3, t)
            total = (
                line[lax.rem(j, 4), t, my[axes[t][0]]].astype(f32)
                + room_of(j, t)[3, 1].astype(f32)
                + room_of(j, t)[3, 2].astype(f32)
            )

            @pl.when(j == 2 * APART)
            def _():
                q = 2 * APART + t
                columns = columns_of(q)
                out[:, columns] = (hidden[:, columns].astype(f32) + total).astype(bf16)
                out_store(q).start()

            @pl.when(j < 2 * APART)
            def _():
                s = lax.rem(j, 2)
                sums[s, t] = total.astype(bf16).reshape(GROUPS, BLOCK, WIDTH)
                for o in range(1, GROUPS):
                    back_copy(j, t, o).start()

                @pl.when(mine)
                def _():
                    k = 2 * lax.rem(j, APART) + t
                    returned[k, rows_of(owner, BLOCK)] = sums[s, t, my_exp]

                @pl.when(jnp.logical_not(mine))
                def _():
                    back_copy(j, t, 0).start()

        rs_sent(j, (2, 3))

    def out_store(q):
        columns = columns_of(q)
        return pltpu.make_async_copy(out.at[:, columns], out_ref.at[:, columns], done_sem.at[q])

    def sum_back(j):
        mine = my_dp == lax.div(j, APART)
        for t in range(2):
            q = 2 * lax.rem(j, APART) + t

            def sent(count):
                ref = sums.at[lax.rem(j, 2), t, pl.ds(0, count)]
                remote(
                    ref, ref, back_send.at[2 * j + t], back_recv.at[0], partner(1)[1]
                ).wait_send()

            @pl.when(mine)
            def _():
                ref = returned.at[q, pl.ds(0, (EXPERTS - 1) * BLOCK)]
                remote(ref, ref, back_send.at[0], back_recv.at[q], partner(1)[1]).wait_recv()
                columns = columns_of(q)
                total = hidden[:, columns].astype(f32)
                for n in range(2):
                    total = total + lax.dot_general(
                        shares[n],
                        returned[q],
                        (((0,), (0,)), ((), ())),
                        preferred_element_type=f32,
                    )
                out[:, columns] = total.astype(bf16)
                out_store(q).start()
                sent(GROUPS - 1)

            pl.when(jnp.logical_not(mine))(functools.partial(sent, GROUPS))

    def weigh():
        match = [
            lax.broadcasted_iota(jnp.int32, (EXPERTS, TOKENS), 0) == chosen[i : i + 1, :]
            for i in range(2)
        ]
        picked = [jnp.sum(jnp.where(m, logits[...], 0.0), axis=0, keepdims=True) for m in match]
        weight = jnp.zeros((EXPERTS * BLOCK, TOKENS), f32)
        for i in range(2):
            share = 1.0 / (1.0 + jnp.exp(picked[1 - i] - picked[i]))
            weight = weight + jnp.where(place_id == target[i : i + 1, :], share, 0.0)
        coarse = weight.astype(bf16)
        shares[0] = coarse
        shares[1] = (weight - coarse.astype(f32)).astype(bf16)
        weights[here] = weight.T.astype(bf16)
        each(lambda k: weight_copy(k).start())

    def stages(tick, count, steps):
        for lag, action in steps:
            pl.when(jnp.logical_and(tick >= lag, tick < count + lag))(
                functools.partial(action, tick - lag)
            )

    @pl.loop(0, 1 + SUMS + ROUNDS + LAST)
    def _(turn):
        tick = turn - 1
        own = tick - my_dp * QUADS
        stages(
            tick,
            PAIRS,
            ((5, gather_last), (4, gather_third), (3, gather_second), (2, gather_first)),
        )
        stages(tick - SUMS, ROUNDS, ((4, sum_second), (2, sum_first)))
        stages(own, QUADS, ((3, rows_sent), (1, tokens), (-1, mix)))
        stages(tick, PAIRS, ((6, gathered),))
        pl.when(tick == SUMS)(weigh)
        stages(tick - SUMS, ROUNDS, ((0, sum_start), (5, sum_third), (6, sum_last)))
        stages(tick - SUMS, 2 * APART, ((7, sum_back),))
        for h in range(2):
            pl.when(tick == SUMS + APART * h)(functools.partial(apart_start, h))

    apart_sent(1)
    each(lambda k: weight_copy(k).wait_send())
    for q in range(2 * QUADS):
        out_store(q).wait()


def layer(*args):
    units = args[-1].shape[1]
    bf16, f32 = jnp.bfloat16, jnp.float32
    any_space = pl.BlockSpec(memory_space=pl.ANY)
    return pl.pallas_call(
        layer_kernel,
        out_shape=jax.ShapeDtypeStruct((TOKENS, D), bf16),
        in_specs=[any_space] * len(args),
        out_specs=any_space,
        scratch_shapes=[
            pltpu.VMEM((LENGTH, INNER), bf16),
            pltpu.VMEM((LENGTH, INNER), bf16),
            pltpu.VMEM((LENGTH, STATE), bf16),
            pltpu.VMEM((LENGTH, STATE), bf16),
            pltpu.VMEM((HEADS, LENGTH), f32),
            pltpu.VMEM((SIZE, STATE), f32),
            pltpu.VMEM((TOKENS, D), bf16),
            pltpu.VMEM((EXPERTS, D), bf16),
            pltpu.VMEM((2, TOKENS), jnp.int32),
            pltpu.VMEM((2, TOKENS), jnp.int32),
            pltpu.VMEM((2, TOKENS), jnp.int32),
            pltpu.VMEM((1, HEADS), f32),
            pltpu.VMEM((1, INNER), f32),
            pltpu.VMEM((TOKENS, D), bf16),
            pltpu.VMEM((LENGTH, INNER), f32),
            pltpu.VMEM((CTX, MESSAGE, STATE), bf16),
            pltpu.VMEM((CTX, MESSAGE, STATE), bf16),
            pltpu.VMEM((CTX, SIZE, STATE), bf16),
            pltpu.VMEM((CTX, SIZE, STATE), bf16),
            pltpu.VMEM((LENGTH, INNER), bf16),
            pltpu.VMEM((4 + 2 * QUADS * (GROUPS - 1) // GROUPS, GROUPS, TOKENS, WIDTH), bf16),
            pltpu.VMEM((TOKENS, D), bf16),
            pltpu.VMEM((EXPERTS * BLOCK, TOKENS), bf16),
            pltpu.VMEM((2, EXPERTS * BLOCK, TOKENS), bf16),
            pltpu.VMEM((EXPERTS, TOKENS), f32),
            pltpu.VMEM((2, 2, EXPERTS, BLOCK, WIDTH), bf16),
            pltpu.VMEM((2, 2, GROUPS, BLOCK, WIDTH), bf16),
            pltpu.VMEM((2 * APART, EXPERTS * BLOCK, WIDTH), bf16),
            pltpu.VMEM((2 * PAIRS, SIDE, SIDE, PIECE, WIDTH), bf16),
            pltpu.VMEM((2, 2 * PLANE, units), f32),
            pltpu.VMEM((2 * PLANE, units), bf16),
            pltpu.VMEM((D, units), bf16),
            pltpu.VMEM((D, units), bf16),
            pltpu.VMEM((D, units), bf16),
            pltpu.VMEM((4, 2, SIDE, SIDE, PIECE, WIDTH), bf16),
            pltpu.VMEM((4, 2, SIDE, PIECE, WIDTH), bf16),
            pltpu.VMEM((2, GROUPS, SIDE, PIECE, WIDTH), bf16),
            pltpu.VMEM((CTX, TOKENS, EXPERTS * BLOCK), bf16),
            pltpu.SemaphoreType.DMA((PAIRS, 2, 8)),
            pltpu.SemaphoreType.DMA((PAIRS, 2, 8)),
            pltpu.SemaphoreType.DMA((PAIRS, 2, 8)),
            pltpu.SemaphoreType.DMA((PAIRS, 2, 8)),
            pltpu.SemaphoreType.DMA((2 * QUADS, GROUPS - 1)),
            pltpu.SemaphoreType.DMA((2 * QUADS, GROUPS - 1)),
            pltpu.SemaphoreType.DMA((2 * QUADS,)),
            pltpu.SemaphoreType.DMA((2 * PAIRS,)),
            pltpu.SemaphoreType.DMA((2 * PAIRS,)),
            pltpu.SemaphoreType.DMA((2 * QUADS,)),
            pltpu.SemaphoreType.DMA((2, 2)),
            pltpu.SemaphoreType.DMA((2,)),
            pltpu.SemaphoreType.DMA((CTX,)),
            pltpu.SemaphoreType.DMA((CTX,)),
            pltpu.SemaphoreType.REGULAR,
            pltpu.SemaphoreType.DMA((3,)),
            pltpu.SemaphoreType.DMA((2 * QUADS,)),
            pltpu.SemaphoreType.DMA((13,)),
            pltpu.SemaphoreType.DMA((2 * QUADS,)),
            pltpu.SemaphoreType.DMA((CTX,)),
            pltpu.SemaphoreType.DMA((CTX,)),
            pltpu.SemaphoreType.DMA((CTX,)),
            pltpu.SemaphoreType.DMA((CTX,)),
        ],
        compiler_params=pltpu.CompilerParams(
            collective_id=0, has_side_effects=True, vmem_limit_bytes=63 << 20
        ),
        cost_estimate=pl.CostEstimate(
            flops=6 * 2048 * D * 512, bytes_accessed=24 << 20, transcendentals=1 << 20
        ),
    )(*args)


def shards(
    mixer_in,
    gate_in,
    state_write,
    state_read,
    decay_rate,
    skip_gain,
    norm_gain,
    start_state,
    out_weight,
    residual,
    router_weight,
    chosen,
    slot_index,
    spill_index,
    gate_weight,
    up_weight,
    down_weight,
):
    return layer(
        mixer_in[0],
        gate_in[0],
        state_write[0, :, 0],
        state_read[0, :, 0],
        decay_rate[0],
        skip_gain[None],
        norm_gain[None],
        start_state[0].reshape(HEADS * SIZE, STATE),
        out_weight.reshape(SIDE, SIDE, PIECE, D),
        residual[0],
        router_weight.T,
        chosen[0].T,
        slot_index[0].T,
        spill_index[0].T,
        gate_weight[0],
        up_weight[0],
        down_weight[0],
    )[None]


def solution(mesh):
    placed = (
        P("dp", "ctx", "exp"),
        P("dp", "ctx", "exp"),
        P("dp", "ctx", "exp", None),
        P("dp", "ctx", "exp", None),
        P("dp", "exp", "ctx"),
        P("exp"),
        P("exp"),
        P("dp", "exp", None, None),
        P("exp", None),
        P("dp", ("ctx", "exp"), None),
        P(),
        P("dp", ("ctx", "exp"), None),
        P("dp", ("ctx", "exp"), None),
        P("dp", ("ctx", "exp"), None),
        P(("exp", "dp"), None, "ctx"),
        P(("exp", "dp"), None, "ctx"),
        P(("exp", "dp"), None, "ctx"),
    )
    return jax.shard_map(
        shards, mesh=mesh, in_specs=placed, out_specs=P("dp", ("ctx", "exp"), None), check_vma=False
    )
```

```python
import functools

import jax
import jax.numpy as jnp
from jax import lax
from jax.experimental import pallas as pl
from jax.experimental.pallas import tpu as pltpu
from jax.sharding import PartitionSpec as P

D = 4096
EXPERTS = 8
CAP = 14
BLOCK = 16
TOKENS = 64
GROUPS = 4
SIDE = 4
WIDTH = 512
QUADS = D // WIDTH // 2
PAIRS = 2 * QUADS
PIECE = GROUPS * BLOCK
HALF = PIECE // 2
PLANE = SIDE * SIDE * PIECE
HEADS = 16
SIZE = 64
STATE = 128
CTX = SIDE * SIDE
LENGTH = 256
INNER = HEADS * SIZE
MESSAGE = SIZE + 16
EARLY = 3
APART = QUADS - 1
ROUNDS = 2 * (QUADS - 1) + 1
SUMS = 10
SPREAD, SPREAD_LATER = 5, 2
DONE = (9, 13)
LAST = 7
MESH = pl.DeviceIdType.MESH


def layer_kernel(
    mixer_ref,
    switch_ref,
    write_ref,
    read_ref,
    decay_ref,
    skip_ref,
    gain_ref,
    start_ref,
    mix_ref,
    residual_ref,
    router_ref,
    chosen_ref,
    slot_ref,
    spill_ref,
    gate_ref,
    up_ref,
    down_ref,
    out_ref,
    mixer,
    switch,
    write,
    read,
    decay,
    start,
    residual,
    router,
    chosen,
    slots,
    spills,
    skips,
    gains,
    out,
    inner,
    states,
    gathered_states,
    entering,
    entered,
    normed,
    pool,
    hidden,
    placing,
    shares,
    logits,
    leaving,
    sums,
    returned,
    xg,
    acc,
    act,
    w_gate,
    w_up,
    w_down,
    part,
    line,
    apart,
    weights,
    placings,
    ag_send,
    ag_recv,
    rs_send,
    rs_recv,
    mix_send,
    mix_recv,
    row_send,
    row_recv,
    back_send,
    back_recv,
    apart_send,
    apart_recv,
    weight_send,
    weight_recv,
    placing_send,
    placing_recv,
    spread_send,
    spread_recv,
    ready,
    load_sem,
    mix_sem,
    input_sem,
    done_sem,
    out_send,
    out_recv,
    in_send,
    in_recv,
):
    f32, bf16 = jnp.float32, jnp.bfloat16
    here = lax.axis_index("ctx")
    my = {"x": lax.rem(here, SIDE), "z": lax.div(here, SIDE)}
    my_exp, my_dp = lax.axis_index("exp"), lax.axis_index("dp")
    owner = my_exp * 2 + my_dp

    def around(axis, step):
        return lax.rem(my[axis] + step + SIDE, SIDE)

    def neighbour(axis, step):
        other = around(axis, step)
        if axis == "x":
            return {"ctx": my["z"] * SIDE + other}
        return {"ctx": other * SIDE + my["x"]}

    def along(axis, ref, place, at):
        if axis == "z":
            return ref.at[place, at]
        return ref.at[at, place]

    def partner(o):
        other = lax.rem(owner + o, EXPERTS)
        return other, {"exp": lax.div(other, 2), "dp": lax.rem(other, 2)}

    def remote(src, dst, send, recv, place):
        return pltpu.make_async_remote_copy(
            src_ref=src,
            dst_ref=dst,
            send_sem=send,
            recv_sem=recv,
            device_id=place,
            device_id_type=MESH,
        )

    def columns_of(q):
        return pl.ds(pl.multiple_of(q * WIDTH, WIDTH), WIDTH)

    def rows_of(index, count):
        return pl.ds(pl.multiple_of(index * count, count), count)

    def mix_room(q):
        return part.at[lax.div(q, 2), lax.rem(q, 2)]

    def mix_load(q):
        return pltpu.make_async_copy(
            mix_ref.at[:, :, :, columns_of(q)], mix_room(q), mix_sem.at[q]
        )

    barrier = pltpu.get_barrier_semaphore()

    def greet(k, _):
        other = lax.rem(here + k, CTX)
        pl.semaphore_signal(barrier, inc=1, device_id={"ctx": other}, device_id_type=MESH)
        return 0

    lax.fori_loop(1, CTX, greet, 0)
    for o in range(1, EXPERTS):
        pl.semaphore_signal(barrier, inc=1, device_id=partner(o)[1], device_id_type=MESH)

    inputs = {
        name: pltpu.make_async_copy(src, dst, input_sem.at[i])
        for i, (name, src, dst) in enumerate(
            (
                ("decay", decay_ref, decay),
                ("mixer", mixer_ref, mixer),
                ("write", write_ref, write),
                ("read", read_ref, read),
                ("start", start_ref.at[rows_of(here, SIZE), :], start),
                ("switch", switch_ref, switch),
                ("residual", residual_ref, residual),
                ("router", router_ref, router),
                ("skip", skip_ref, skips),
                ("gain", gain_ref, gains),
                ("chosen", chosen_ref, chosen),
                ("slots", slot_ref, slots),
                ("spills", spill_ref, spills),
            )
        )
    }
    for copy in inputs.values():
        copy.start()
    loads = [
        pltpu.make_async_copy(src, dst, load_sem.at[i])
        for i, (src, dst) in enumerate(((gate_ref, w_gate), (up_ref, w_up), (down_ref, w_down)))
    ]


    row_id = lax.broadcasted_iota(jnp.int32, (LENGTH, LENGTH), 0)
    col_id = lax.broadcasted_iota(jnp.int32, (LENGTH, LENGTH), 1)
    causal = row_id >= col_id
    upper = jnp.where(row_id <= col_id, 1.0, 0.0).astype(f32)
    inputs["decay"].wait()
    levels = jnp.dot(
        decay[...], upper, precision=lax.Precision.HIGHEST, preferred_element_type=f32
    )
    last = levels[:, LENGTH - 1 : LENGTH]
    to_end = jnp.exp(levels - last).T
    total_decay = jnp.exp(-last)
    levels_t = levels.T
    from_start = jnp.exp(-levels_t)
    low = lax.broadcasted_iota(jnp.int32, (LENGTH, 2 * SIZE), 1) < SIZE
    top = lax.broadcasted_iota(jnp.int32, (16, STATE), 0) < 8

    def spread(columns, q):
        return jnp.where(low, columns[:, 2 * q : 2 * q + 1], columns[:, 2 * q + 1 : 2 * q + 2])

    inputs["mixer"].wait()
    inputs["write"].wait()
    for q in range(HEADS // 2):
        lanes = pl.ds(q * 2 * SIZE, 2 * SIZE)
        scaled = (spread(to_end, q) * mixer[:, lanes].astype(f32)).astype(bf16)
        local = lax.dot_general(
            scaled, write[...], (((0,), (0,)), ((), ())), preferred_element_type=f32
        )
        for i in range(2):
            h = 2 * q + i
            states[h, 0:SIZE] = local[i * SIZE : (i + 1) * SIZE].astype(bf16)
            value = jnp.broadcast_to(total_decay[h : h + 1, :], (16, STATE))
            coarse = value.astype(bf16)
            rest = (value - coarse.astype(f32)).astype(bf16)
            states[h, SIZE:MESSAGE] = jnp.where(top, coarse, rest)

    pl.semaphore_wait(barrier, CTX - 1 + EXPERTS - 1)

    def out_copy(k):
        other = lax.rem(here + k, CTX)
        return remote(
            states.at[other],
            gathered_states.at[here],
            out_send.at[k],
            out_recv.at[k],
            {"ctx": other},
        )

    def in_copy(k):
        other = lax.rem(here + k, CTX)
        return remote(
            entering.at[other], entered.at[here], in_send.at[k], in_recv.at[k], {"ctx": other}
        )

    def each(action):
        def step(k, _):
            action(k)
            return 0

        lax.fori_loop(1, CTX, step, 0)

    each(lambda k: out_copy(k).start())
    gathered_states[here] = states[here]

    def load_mix(q, _):
        mix_load(q).start()
        return 0

    lax.fori_loop(0, 2 * QUADS, load_mix, 0)
    for load in loads:
        load.start()


    inputs["read"].wait()
    inputs["skip"].wait()
    meet = lax.dot_general(
        read[...], write[...], (((1,), (1,)), ((), ())), preferred_element_type=f32
    )

    def within(q):
        lanes = pl.ds(q * 2 * SIZE, 2 * SIZE)
        pair = mixer[:, lanes]
        heads = []
        for i in range(2):
            h = 2 * q + i
            span = levels[h : h + 1, :] - levels_t[:, h : h + 1]
            weight = jnp.exp(jnp.where(causal, span, -1e30)) * meet
            heads.append(jnp.dot(weight.astype(bf16), pair, preferred_element_type=f32))
        skip = spread(skips[...], q)
        inner[:, lanes] = jnp.where(low, heads[0], heads[1]) + skip * pair.astype(f32)

    for q in range(EARLY):
        within(q)


    inputs["start"].wait()
    each(lambda k: out_copy(k).wait_recv())
    state = start[...]
    for k in range(CTX):
        entering[k] = state.astype(bf16)
        if k < CTX - 1:
            factor = gathered_states[k, SIZE:MESSAGE].astype(f32)
            factor = factor[0:1, :] + factor[8:9, :]
            state = factor * state + gathered_states[k, 0:SIZE].astype(f32)
    each(lambda k: in_copy(k).start())
    entered[here] = entering[here]

    for q in range(EARLY, HEADS // 2):
        within(q)

    for name in ("chosen", "slots", "spills", "gain"):
        inputs[name].wait()

    place_id = lax.broadcasted_iota(jnp.int32, (EXPERTS * BLOCK, TOKENS), 0)
    expert_ids, slot_ids, spill_ids = chosen[...], slots[...], spills[...]
    target = jnp.where(
        slot_ids >= 0,
        expert_ids * BLOCK + slot_ids,
        jnp.where(
            spill_ids >= 0,
            jnp.right_shift(spill_ids, 1) * BLOCK + CAP + jnp.bitwise_and(spill_ids, 1),
            -1,
        ),
    )
    places = [place_id == target[i : i + 1, :] for i in range(2)]
    place = places[0].astype(f32) + places[1].astype(f32)
    placing[...] = place.astype(bf16)
    placings[here] = place.T.astype(bf16)
    logits[...] = jnp.zeros_like(logits)
    acc[...] = jnp.zeros_like(acc)

    inputs["switch"].wait()
    each(lambda k: in_copy(k).wait_recv())
    square = jnp.zeros((LENGTH, 1), f32)
    for q in range(HEADS // 2):
        lanes = pl.ds(q * 2 * SIZE, 2 * SIZE)
        carried = lax.dot_general(
            read[...],
            entered[2 * q : 2 * q + 2].reshape(2 * SIZE, STATE),
            (((1,), (1,)), ((), ())),
            preferred_element_type=f32,
        )
        gate = switch[:, lanes].astype(f32)
        gated = (inner[:, lanes] + carried * spread(from_start, q)) * (
            gate / (1.0 + jnp.exp(-gate))
        )
        inner[:, lanes] = gated
        square = square + jnp.sum(gated * gated, axis=1, keepdims=True)
    scale = lax.rsqrt(square / INNER + 1e-05)
    for q in range(HEADS // 2):
        lanes = pl.ds(q * 2 * SIZE, 2 * SIZE)
        normed[:, lanes] = (inner[:, lanes] * scale * gains[:, lanes]).astype(bf16)

    inputs["residual"].wait()
    inputs["router"].wait()
    each(lambda k: out_copy(k).wait_send())
    each(lambda k: in_copy(k).wait_send())

    every = pl.ds(0, SIDE)
    halves = {1: pl.ds(0, SIDE // 2), -1: pl.ds(SIDE // 2, SIDE // 2)}
    half_rows = {1: pl.ds(0, HALF), -1: pl.ds(HALF, HALF)}
    axes = (("x", "z"), ("z", "x"))
    slot = {1: 0, -1: 1}
    both = [(t, d) for t in range(2) for d in (1, -1)]


    def mixed(c, t):
        return pool.at[lax.rem(c, 2) * 2 + t]

    def term(q, i):
        b = q * (GROUPS - 1) + i - 1
        return pool.at[4 + lax.div(b, GROUPS), lax.rem(b, GROUPS)]

    def term_copy(c, t, i):
        other = lax.rem(my_exp + i, GROUPS)
        q = 2 * c + t
        return remote(
            mixed(c, t).at[other],
            term(q, i),
            mix_send.at[q, i - 1],
            mix_recv.at[q, i - 1],
            {"exp": other},
        )

    def mix(c):
        for t in range(2):
            q = 2 * c + t
            mix_load(q).wait()
            value = jnp.dot(
                normed[...],
                mix_room(q)[...].reshape(INNER, WIDTH),
                preferred_element_type=f32,
            )
            mixed(c, t)[...] = value.astype(bf16).reshape(GROUPS, TOKENS, WIDTH)
            for i in range(1, GROUPS):
                term_copy(c, t, i).start()


    def row_copy(c, t, o):
        other, place = partner(o)
        k = 2 * (my_dp * QUADS + c) + t
        return remote(
            leaving.at[lax.rem(c, 2), t, other],
            xg.at[k, my["z"], my["x"], rows_of(my_exp, BLOCK)],
            row_send.at[2 * c + t],
            row_recv.at[k],
            place,
        )

    def tokens(c, by_token=False):
        for t in range(2):
            q = 2 * c + t
            columns = columns_of(q)
            for i in range(1, GROUPS):
                term_copy(c, t, i).wait_recv()
            total = mixed(c, t)[my_exp].astype(f32)
            for i in range(1, GROUPS):
                total = total + term(q, i)[...].astype(f32)
            value = (residual[:, columns].astype(f32) + total).astype(bf16)
            hidden[:, columns] = value
            if by_token:
                apart[t, my["z"], my["x"]] = value
                for d in (1, -1):
                    ag_copy(c, t, 0, d, False, by_token=True).start()
                for d in (1, -1):
                    ag_copy(c, t, 2, d, False, by_token=True).start()
            else:
                rows = jnp.dot(placing[...], value, preferred_element_type=f32).astype(bf16)
                leaving[lax.rem(c, 2), t] = rows.reshape(EXPERTS, BLOCK, WIDTH)
                for o in range(1, EXPERTS):
                    row_copy(c, t, o).start()
                k = 2 * (my_dp * QUADS + c) + t
                xg[k, my["z"], my["x"], rows_of(my_exp, BLOCK)] = leaving[
                    lax.rem(c, 2), t, owner
                ]
            logits[...] += lax.dot_general(
                router[:, columns],
                value,
                (((1,), (1,)), ((), ())),
                preferred_element_type=f32,
            )
        for t in range(2):
            for i in range(1, GROUPS):
                term_copy(c, t, i).wait_send()

    def rows_sent(c):
        for t in range(2):
            ref = leaving.at[lax.rem(c, 2), t, pl.ds(0, EXPERTS - 1)]
            remote(ref, ref, row_send.at[2 * c + t], row_recv.at[0], partner(1)[1]).wait_send()


    def pair_of(j):
        return j + lax.div(j - 1, QUADS - 1)

    def ag_copy(j, t, step, d, landing, off=0, by_token=False):
        near, far = axes[t]
        chunk = apart.at[t] if by_token else xg.at[2 * pair_of(j) + t]
        back = -d if landing else 0
        if step == 0:
            ref, to = along(near, chunk, around(near, back), my[far]), near
        elif step == 1:
            ref = along(near, chunk, around(near, -2 * d if landing else -d), my[far])
            ref, to = ref.at[half_rows[d]], near
        elif step == 2 and off is None:
            ref, to = along(far, chunk, around(far, back), every), far
        elif step == 2:
            ref, to = along(near, chunk, around(near, off), my[far]), far
        else:
            ref = along(far, chunk, around(far, -2 * d if landing else -d), halves[d])
            to = far
        m = step * 2 + slot[d]
        return remote(ref, ref, ag_send.at[j, t, m], ag_recv.at[j, t, m], neighbour(to, d))

    def ag_arrive(j, step, by_token):
        for t, d in both:
            ag_copy(j, t, step, d, True, None, by_token).wait_recv()

    def gather_first(j):
        pair = pair_of(j)
        mine = my_dp == lax.div(pair, QUADS)
        for t in range(2):
            k = 2 * pair + t

            def arrive(count):
                ref = xg.at[k, my["z"], my["x"], pl.ds(0, count)]
                remote(ref, ref, row_send.at[0], row_recv.at[k], partner(1)[1]).wait_recv()

            pl.when(mine)(functools.partial(arrive, PIECE - BLOCK))
            pl.when(jnp.logical_not(mine))(functools.partial(arrive, PIECE))
            for d in (1, -1):
                ag_copy(j, t, 0, d, False).start()
        for t, d in both:
            ag_copy(j, t, 2, d, False, 0).start()

    def gather_second(j, by_token=False):
        ag_arrive(j, 0, by_token)
        for t, d in both:
            ag_copy(j, t, 1, d, False, 0, by_token).start()
        for t, d in both:
            for off in (1, -1):
                ag_copy(j, t, 2, d, False, off, by_token).start()

    def gather_third(j, by_token=False):
        ag_arrive(j, 1, by_token)
        for t, d in both:
            ag_copy(j, t, 2, d, False, 2, by_token).start()

    def gather_last(j, by_token=False):
        ag_arrive(j, 2, by_token)
        for t, d in both:
            ag_copy(j, t, 3, d, False, 0, by_token).start()

    def gather_done(j, by_token=False):
        ag_arrive(j, 3, by_token)
        for step in range(4):
            for t, d in both:
                ag_copy(j, t, step, d, False, None, by_token).wait_send()

    def multiply(h, c):
        @pl.loop(0, 2)
        def _(b):
            rows = rows_of(h * 2 + b, PLANE // 2)
            for n, weight in enumerate((w_gate, w_up)):
                total = acc[n, rows, :]
                for t in range(2):
                    total += jnp.dot(
                        xg[2 * (h * QUADS + c) + t, pl.ds(b * 2, 2)].reshape(PLANE // 2, WIDTH),
                        weight[columns_of(2 * c + t), :],
                        preferred_element_type=f32,
                    )
                acc[n, rows, :] = total

    def gathered(j):
        gather_done(j)

        @pl.when(j == 1)
        def _():
            for load in loads:
                load.wait()

        multiply(lax.div(j - 1, QUADS - 1), lax.rem(j - 1, QUADS - 1) + 1)

        @pl.when(j == QUADS - 1)
        def _():
            for o in range(1, EXPERTS):
                pl.semaphore_signal(ready, inc=1, device_id=partner(o)[1], device_id_type=MESH)


    def placing_copy(k):
        other = lax.rem(here + k, CTX)
        return remote(
            placings.at[here],
            placings.at[here],
            placing_send.at[k],
            placing_recv.at[k],
            {"ctx": other},
        )

    def spread_room(t, e):
        return part.at[2 + t, lax.div(e, SIDE), lax.rem(e, SIDE)]

    def spread_copy(t, o, x):
        other, place = partner(o)
        return remote(
            spread_room(t, other).at[:, pl.ds(x * BLOCK, BLOCK)],
            xg.at[2 * my_dp * QUADS + t, :, x, rows_of(my_exp, BLOCK)],
            spread_send.at[t],
            spread_recv.at[2 * my_dp + t],
            place,
        )

    def spread_rows():
        each(lambda k: placing_copy(k).wait_recv())
        for t in range(2):

            @pl.loop(0, SIDE)
            def _(z):
                for x in range(SIDE):
                    rows = lax.dot_general(
                        placings[z * SIDE + x],
                        apart[t, z, x],
                        (((0,), (0,)), ((), ())),
                        preferred_element_type=f32,
                    ).astype(bf16)
                    for e in range(EXPERTS):
                        part[2 + t, e // SIDE, e % SIDE, z, x * BLOCK : (x + 1) * BLOCK] = rows[
                            e * BLOCK : (e + 1) * BLOCK
                        ]

            for o in range(1, EXPERTS):
                for x in range(SIDE):
                    spread_copy(t, o, x).start()
            for x in range(SIDE):
                xg[2 * my_dp * QUADS + t, :, x, rows_of(my_exp, BLOCK)] = spread_room(t, owner)[
                    :, x * BLOCK : (x + 1) * BLOCK
                ]

    def spread_sent():
        for t in range(2):
            ref = pool.at[pl.ds(0, EXPERTS - 1)]
            remote(ref, ref, spread_send.at[t], spread_recv.at[0], partner(1)[1]).wait_send()

    def rows_done(h):
        for t in range(2):

            def arrive(count):
                ref = pool.at[pl.ds(0, count)]
                remote(
                    ref, ref, spread_send.at[0], spread_recv.at[2 * h + t], partner(1)[1]
                ).wait_recv()

            pl.when(my_dp == h)(functools.partial(arrive, GROUPS - 1))
            pl.when(my_dp != h)(functools.partial(arrive, GROUPS))
        multiply(h, 0)

        @pl.loop(0, 8)
        def _(b):
            rows = rows_of(h * 8 + b, PLANE // 8)
            gate = acc[0, rows, :]
            act[rows, :] = (gate / (1.0 + jnp.exp(-gate)) * acc[1, rows, :]).astype(bf16)


    def room_of(j, t):
        pair = lax.div(j, APART) * QUADS + lax.rem(j + 1, APART) - 2 * lax.div(j, 2 * APART)
        return xg.at[2 * pair + t]

    def rs_copy(j, t, step, d):
        near, far = axes[t]
        p = part.at[lax.rem(j, 4), t]
        room = room_of(j, t)
        if step == 0:
            src = along(far, p, around(far, 2), halves[d])
            dst, to = room.at[0, halves[d]], far
        elif step == 1:
            src = along(far, p, around(far, d), every)
            dst, to = room.at[1 + slot[d]], far
        elif step == 2:
            src = line.at[lax.rem(j, 4), t, around(near, 2), half_rows[d]]
            dst, to = room.at[3, 0, half_rows[d]], near
        else:
            src = line.at[lax.rem(j, 4), t, around(near, d)]
            dst, to = room.at[3, 1 + slot[d]], near
        m = step * 2 + slot[d]
        return remote(src, dst, rs_send.at[j, t, m], rs_recv.at[j, t, m], neighbour(to, d))

    def rs_start(j, step, t):
        for d in (1, -1):
            rs_copy(j, t, step, d).start()

    def rs_arrive(j, step, t):
        for d in (1, -1):
            rs_copy(j, t, step, d).wait_recv()

    def rs_sent(j, steps):
        for step in steps:
            for t, d in both:
                rs_copy(j, t, step, d).wait_send()

    def down(h, b, q):
        rows = rows_of(h * 2 + b, PLANE // 2)
        value = lax.dot_general(
            act[rows, :],
            w_down[columns_of(q), :],
            (((1,), (1,)), ((), ())),
            preferred_element_type=f32,
        )
        return value.astype(bf16)

    def by_rows(j):
        h = lax.div(j, APART)
        c = lax.rem(j, APART)

        @pl.loop(0, 2)
        def _(b):
            for t in range(2):
                part[lax.rem(j, 4), t, pl.ds(b * 2, 2)] = down(h, b, 2 * c + t).reshape(
                    2, SIDE, PIECE, WIDTH
                )


    def apart_room(t, e):
        if t == 0:
            return xg.at[2 * APART + lax.div(e, SIDE), lax.rem(e, SIDE)]
        return pool.at[e]

    def apart_copy(h, t, o):
        other = lax.rem(my_exp + o, GROUPS)
        return remote(
            apart.at[t, other],
            apart_room(t, owner),
            apart_send.at[h, t],
            apart_recv.at[t],
            {"exp": other, "dp": h},
        )

    def apart_sent(h):
        for t in range(2):

            def sent(count):
                ref = pool.at[pl.ds(0, count)]
                remote(
                    ref, ref, apart_send.at[h, t], apart_recv.at[0], partner(1)[1]
                ).wait_send()

            pl.when(my_dp == h)(functools.partial(sent, GROUPS - 1))
            pl.when(my_dp != h)(functools.partial(sent, GROUPS))

    def apart_start(h):
        if h == 0:
            pl.semaphore_wait(ready, EXPERTS - 1)
        else:
            apart_sent(0)
        for t in range(2):

            @pl.loop(0, 2)
            def _(b):
                value = down(h, b, 2 * APART + t)
                for i in range(2):
                    for x in range(SIDE):
                        for y in range(GROUPS):
                            low_row = (i * SIDE + x) * PIECE + y * BLOCK
                            apart[t, y, 2 * b + i, x * BLOCK : (x + 1) * BLOCK] = value[
                                low_row : low_row + BLOCK
                            ]

            for o in range(1, GROUPS):
                apart_copy(h, t, o).start()

            @pl.when(my_dp == h)
            def _():
                apart_room(t, owner)[...] = apart[t, my_exp]

            @pl.when(my_dp != h)
            def _():
                apart_copy(h, t, 0).start()

    def weight_copy(k):
        other = lax.rem(here + k, CTX)
        return remote(
            weights.at[here],
            weights.at[here],
            weight_send.at[k],
            weight_recv.at[k],
            {"ctx": other},
        )

    def by_tokens(j):
        each(lambda k: weight_copy(k).wait_recv())
        for t in range(2):
            ref = pool.at[pl.ds(0, EXPERTS - 1)]
            remote(ref, ref, apart_send.at[0, 0], apart_recv.at[t], partner(1)[1]).wait_recv()

            @pl.loop(0, SIDE)
            def _(z):
                for x in range(SIDE):
                    rows = jnp.concatenate(
                        [
                            apart_room(t, e)[z, x * BLOCK : (x + 1) * BLOCK]
                            for e in range(EXPERTS)
                        ],
                        axis=0,
                    )
                    value = jnp.dot(
                        weights[z * SIDE + x], rows, preferred_element_type=f32
                    )
                    part[lax.rem(j, 4), t, z, x] = value.astype(bf16)

    def sum_start(j):
        pl.when(j < 2 * APART)(functools.partial(by_rows, j))
        pl.when(j == 2 * APART)(functools.partial(by_tokens, j))
        for t in range(2):
            rs_start(j, 0, t)

    def sum_first(j):
        s = lax.rem(j, 4)
        for t in range(2):
            far = axes[t][1]
            rs_arrive(j, 0, t)
            for d in (1, -1):
                base = 0 if d == 1 else SIDE // 2
                place = around(far, d)

                @pl.loop(0, SIDE // 2)
                def _(i):
                    at = (place, base + i) if far == "z" else (base + i, place)
                    part[s, t, at[0], at[1]] = (
                        part[s, t, at[0], at[1]].astype(f32)
                        + room_of(j, t)[0, base + i].astype(f32)
                    ).astype(bf16)

            rs_start(j, 1, t)

    def sum_second(j):
        s = lax.rem(j, 4)
        for t in range(2):
            far = axes[t][1]
            rs_arrive(j, 1, t)

            @pl.loop(0, SIDE)
            def _(i):
                at = (my[far], i) if far == "z" else (i, my[far])
                line[s, t, i] = (
                    part[s, t, at[0], at[1]].astype(f32)
                    + room_of(j, t)[1, i].astype(f32)
                    + room_of(j, t)[2, i].astype(f32)
                ).astype(bf16)

            rs_start(j, 2, t)
        rs_sent(j, (0, 1))

    def sum_third(j):
        s = lax.rem(j, 4)
        for t in range(2):
            rs_arrive(j, 2, t)
            for d in (1, -1):
                at = around(axes[t][0], d)
                line[s, t, at, half_rows[d]] = (
                    line[s, t, at, half_rows[d]].astype(f32)
                    + room_of(j, t)[3, 0, half_rows[d]].astype(f32)
                ).astype(bf16)
            rs_start(j, 3, t)


    def back_copy(j, t, o):
        other = lax.rem(my_exp + o, GROUPS)
        k = 2 * lax.rem(j, APART) + t
        return remote(
            sums.at[lax.rem(j, 2), t, other],
            returned.at[k, rows_of(owner, BLOCK)],
            back_send.at[2 * j + t],
            back_recv.at[k],
            {"exp": other, "dp": lax.div(j, APART)},
        )

    def sum_last(j):
        mine = my_dp == lax.div(j, APART)
        for t in range(2):
            rs_arrive(j, 3, t)
            total = (
                line[lax.rem(j, 4), t, my[axes[t][0]]].astype(f32)
                + room_of(j, t)[3, 1].astype(f32)
                + room_of(j, t)[3, 2].astype(f32)
            )

            @pl.when(j == 2 * APART)
            def _():
                q = 2 * APART + t
                columns = columns_of(q)
                out[:, columns] = (hidden[:, columns].astype(f32) + total).astype(bf16)
                out_store(q).start()

            @pl.when(j < 2 * APART)
            def _():
                s = lax.rem(j, 2)
                sums[s, t] = total.astype(bf16).reshape(GROUPS, BLOCK, WIDTH)
                for o in range(1, GROUPS):
                    back_copy(j, t, o).start()

                @pl.when(mine)
                def _():
                    k = 2 * lax.rem(j, APART) + t
                    returned[k, rows_of(owner, BLOCK)] = sums[s, t, my_exp]

                @pl.when(jnp.logical_not(mine))
                def _():
                    back_copy(j, t, 0).start()

        rs_sent(j, (2, 3))

    def out_store(q):
        columns = columns_of(q)
        return pltpu.make_async_copy(out.at[:, columns], out_ref.at[:, columns], done_sem.at[q])

    def sum_back(j):
        mine = my_dp == lax.div(j, APART)
        for t in range(2):
            q = 2 * lax.rem(j, APART) + t

            def sent(count):
                ref = sums.at[lax.rem(j, 2), t, pl.ds(0, count)]
                remote(
                    ref, ref, back_send.at[2 * j + t], back_recv.at[0], partner(1)[1]
                ).wait_send()

            @pl.when(mine)
            def _():
                ref = returned.at[q, pl.ds(0, (EXPERTS - 1) * BLOCK)]
                remote(ref, ref, back_send.at[0], back_recv.at[q], partner(1)[1]).wait_recv()
                columns = columns_of(q)
                total = hidden[:, columns].astype(f32)
                for n in range(2):
                    total = total + lax.dot_general(
                        shares[n],
                        returned[q],
                        (((0,), (0,)), ((), ())),
                        preferred_element_type=f32,
                    )
                out[:, columns] = total.astype(bf16)
                out_store(q).start()
                sent(GROUPS - 1)

            pl.when(jnp.logical_not(mine))(functools.partial(sent, GROUPS))

    def weigh():
        match = [
            lax.broadcasted_iota(jnp.int32, (EXPERTS, TOKENS), 0) == chosen[i : i + 1, :]
            for i in range(2)
        ]
        picked = [jnp.sum(jnp.where(m, logits[...], 0.0), axis=0, keepdims=True) for m in match]
        weight = jnp.zeros((EXPERTS * BLOCK, TOKENS), f32)
        for i in range(2):
            share = 1.0 / (1.0 + jnp.exp(picked[1 - i] - picked[i]))
            weight = weight + jnp.where(place_id == target[i : i + 1, :], share, 0.0)
        coarse = weight.astype(bf16)
        shares[0] = coarse
        shares[1] = (weight - coarse.astype(f32)).astype(bf16)
        weights[here] = weight.T.astype(bf16)
        each(lambda k: weight_copy(k).start())

    def stages(tick, count, steps):
        for lag, action in steps:
            pl.when(jnp.logical_and(tick >= lag, tick < count + lag))(
                functools.partial(action, tick - lag)
            )

    each(lambda k: placing_copy(k).start())

    def later(action):
        return lambda j: action(j + 1)

    @pl.loop(0, 1 + SUMS + ROUNDS + LAST)
    def _(turn):
        tick = turn - 1
        own = tick - my_dp * (QUADS - 1)

        def first(when, action):
            pl.when(tick == when)(functools.partial(action, tick - when, True))

        first(4, gather_last)
        stages(tick - 1, 2 * QUADS - 2, ((5, later(gather_last)),))
        first(3, gather_third)
        stages(tick - 1, 2 * QUADS - 2, ((4, later(gather_third)),))
        first(2, gather_second)
        stages(tick - 1, 2 * QUADS - 2, ((3, later(gather_second)), (2, later(gather_first))))
        stages(tick - SUMS, ROUNDS, ((4, sum_second), (2, sum_first)))
        stages(own - 1, QUADS - 1, ((3, later(rows_sent)),))
        first(1, tokens)
        stages(own - 1, QUADS - 1, ((1, later(tokens)),))
        stages(tick, 1, ((-1, mix),))
        stages(own - 1, QUADS - 1, ((-1, later(mix)),))
        first(5, gather_done)
        pl.when(tick == SPREAD + SPREAD_LATER * my_dp)(spread_rows)
        stages(tick - 1, 2 * QUADS - 2, ((6, later(gathered)),))
        pl.when(tick == SUMS + 2)(spread_sent)
        for h in range(2):
            pl.when(tick == DONE[h])(functools.partial(rows_done, h))
        pl.when(tick == SUMS)(weigh)
        stages(tick - SUMS, ROUNDS, ((0, sum_start), (5, sum_third), (6, sum_last)))
        stages(tick - SUMS, 2 * APART, ((7, sum_back),))
        for h in range(2):
            pl.when(tick == SUMS + APART * h)(functools.partial(apart_start, h))

    apart_sent(1)
    each(lambda k: weight_copy(k).wait_send())
    each(lambda k: placing_copy(k).wait_send())
    for q in range(2 * QUADS):
        out_store(q).wait()


def layer(*args):
    units = args[-1].shape[1]
    bf16, f32 = jnp.bfloat16, jnp.float32
    any_space = pl.BlockSpec(memory_space=pl.ANY)
    return pl.pallas_call(
        layer_kernel,
        out_shape=jax.ShapeDtypeStruct((TOKENS, D), bf16),
        in_specs=[any_space] * len(args),
        out_specs=any_space,
        scratch_shapes=[
            pltpu.VMEM((LENGTH, INNER), bf16),
            pltpu.VMEM((LENGTH, INNER), bf16),
            pltpu.VMEM((LENGTH, STATE), bf16),
            pltpu.VMEM((LENGTH, STATE), bf16),
            pltpu.VMEM((HEADS, LENGTH), f32),
            pltpu.VMEM((SIZE, STATE), f32),
            pltpu.VMEM((TOKENS, D), bf16),
            pltpu.VMEM((EXPERTS, D), bf16),
            pltpu.VMEM((2, TOKENS), jnp.int32),
            pltpu.VMEM((2, TOKENS), jnp.int32),
            pltpu.VMEM((2, TOKENS), jnp.int32),
            pltpu.VMEM((1, HEADS), f32),
            pltpu.VMEM((1, INNER), f32),
            pltpu.VMEM((TOKENS, D), bf16),
            pltpu.VMEM((LENGTH, INNER), f32),
            pltpu.VMEM((CTX, MESSAGE, STATE), bf16),
            pltpu.VMEM((CTX, MESSAGE, STATE), bf16),
            pltpu.VMEM((CTX, SIZE, STATE), bf16),
            pltpu.VMEM((CTX, SIZE, STATE), bf16),
            pltpu.VMEM((LENGTH, INNER), bf16),
            pltpu.VMEM((4 + 2 * QUADS * (GROUPS - 1) // GROUPS, GROUPS, TOKENS, WIDTH), bf16),
            pltpu.VMEM((TOKENS, D), bf16),
            pltpu.VMEM((EXPERTS * BLOCK, TOKENS), bf16),
            pltpu.VMEM((2, EXPERTS * BLOCK, TOKENS), bf16),
            pltpu.VMEM((EXPERTS, TOKENS), f32),
            pltpu.VMEM((2, 2, EXPERTS, BLOCK, WIDTH), bf16),
            pltpu.VMEM((2, 2, GROUPS, BLOCK, WIDTH), bf16),
            pltpu.VMEM((2 * APART, EXPERTS * BLOCK, WIDTH), bf16),
            pltpu.VMEM((2 * PAIRS, SIDE, SIDE, PIECE, WIDTH), bf16),
            pltpu.VMEM((2, 2 * PLANE, units), f32),
            pltpu.VMEM((2 * PLANE, units), bf16),
            pltpu.VMEM((D, units), bf16),
            pltpu.VMEM((D, units), bf16),
            pltpu.VMEM((D, units), bf16),
            pltpu.VMEM((4, 2, SIDE, SIDE, PIECE, WIDTH), bf16),
            pltpu.VMEM((4, 2, SIDE, PIECE, WIDTH), bf16),
            pltpu.VMEM((2, GROUPS, SIDE, PIECE, WIDTH), bf16),
            pltpu.VMEM((CTX, TOKENS, EXPERTS * BLOCK), bf16),
            pltpu.VMEM((CTX, TOKENS, EXPERTS * BLOCK), bf16),
            pltpu.SemaphoreType.DMA((PAIRS, 2, 8)),
            pltpu.SemaphoreType.DMA((PAIRS, 2, 8)),
            pltpu.SemaphoreType.DMA((PAIRS, 2, 8)),
            pltpu.SemaphoreType.DMA((PAIRS, 2, 8)),
            pltpu.SemaphoreType.DMA((2 * QUADS, GROUPS - 1)),
            pltpu.SemaphoreType.DMA((2 * QUADS, GROUPS - 1)),
            pltpu.SemaphoreType.DMA((2 * QUADS,)),
            pltpu.SemaphoreType.DMA((2 * PAIRS,)),
            pltpu.SemaphoreType.DMA((2 * PAIRS,)),
            pltpu.SemaphoreType.DMA((2 * QUADS,)),
            pltpu.SemaphoreType.DMA((2, 2)),
            pltpu.SemaphoreType.DMA((2,)),
            pltpu.SemaphoreType.DMA((CTX,)),
            pltpu.SemaphoreType.DMA((CTX,)),
            pltpu.SemaphoreType.DMA((CTX,)),
            pltpu.SemaphoreType.DMA((CTX,)),
            pltpu.SemaphoreType.DMA((2,)),
            pltpu.SemaphoreType.DMA((4,)),
            pltpu.SemaphoreType.REGULAR,
            pltpu.SemaphoreType.DMA((3,)),
            pltpu.SemaphoreType.DMA((2 * QUADS,)),
            pltpu.SemaphoreType.DMA((13,)),
            pltpu.SemaphoreType.DMA((2 * QUADS,)),
            pltpu.SemaphoreType.DMA((CTX,)),
            pltpu.SemaphoreType.DMA((CTX,)),
            pltpu.SemaphoreType.DMA((CTX,)),
            pltpu.SemaphoreType.DMA((CTX,)),
        ],
        compiler_params=pltpu.CompilerParams(
            collective_id=0, has_side_effects=True, vmem_limit_bytes=63 << 20
        ),
        cost_estimate=pl.CostEstimate(
            flops=6 * 2048 * D * 512, bytes_accessed=24 << 20, transcendentals=1 << 20
        ),
    )(*args)


def shards(
    mixer_in,
    gate_in,
    state_write,
    state_read,
    decay_rate,
    skip_gain,
    norm_gain,
    start_state,
    out_weight,
    residual,
    router_weight,
    chosen,
    slot_index,
    spill_index,
    gate_weight,
    up_weight,
    down_weight,
):
    return layer(
        mixer_in[0],
        gate_in[0],
        state_write[0, :, 0],
        state_read[0, :, 0],
        decay_rate[0],
        skip_gain[None],
        norm_gain[None],
        start_state[0].reshape(HEADS * SIZE, STATE),
        out_weight.reshape(SIDE, SIDE, PIECE, D),
        residual[0],
        router_weight.T,
        chosen[0].T,
        slot_index[0].T,
        spill_index[0].T,
        gate_weight[0],
        up_weight[0],
        down_weight[0],
    )[None]


def solution(mesh):
    placed = (
        P("dp", "ctx", "exp"),
        P("dp", "ctx", "exp"),
        P("dp", "ctx", "exp", None),
        P("dp", "ctx", "exp", None),
        P("dp", "exp", "ctx"),
        P("exp"),
        P("exp"),
        P("dp", "exp", None, None),
        P("exp", None),
        P("dp", ("ctx", "exp"), None),
        P(),
        P("dp", ("ctx", "exp"), None),
        P("dp", ("ctx", "exp"), None),
        P("dp", ("ctx", "exp"), None),
        P(("exp", "dp"), None, "ctx"),
        P(("exp", "dp"), None, "ctx"),
        P(("exp", "dp"), None, "ctx"),
    )
    return jax.shard_map(
        shards, mesh=mesh, in_specs=placed, out_specs=P("dp", ("ctx", "exp"), None), check_vma=False
    )
```

```python
import functools

import jax
import jax.numpy as jnp
from jax import lax
from jax.experimental import pallas as pl
from jax.experimental.pallas import tpu as pltpu
from jax.sharding import PartitionSpec as P

D = 4096
EXPERTS = 8
CAP = 14
BLOCK = 16
TOKENS = 64
GROUPS = 4
SIDE = 4
WIDTH = 512
QUADS = D // WIDTH // 2
PAIRS = 2 * QUADS
PIECE = GROUPS * BLOCK
HALF = PIECE // 2
PLANE = SIDE * SIDE * PIECE
HEADS = 16
SIZE = 64
STATE = 128
CTX = SIDE * SIDE
LENGTH = 256
INNER = HEADS * SIZE
MESSAGE = SIZE + 16
EARLY = 3
APART = QUADS - 1
ROUNDS = 2 * (QUADS - 1) + 1
SUMS = 10
SPREAD, SPREAD_LATER = 5, 2
DONE = (9, 13)
LAST = 7
MESH = pl.DeviceIdType.MESH


def layer_kernel(
    mixer_ref,
    switch_ref,
    write_ref,
    read_ref,
    decay_ref,
    skip_ref,
    gain_ref,
    start_ref,
    mix_ref,
    residual_ref,
    router_ref,
    chosen_ref,
    slot_ref,
    spill_ref,
    gate_ref,
    up_ref,
    down_ref,
    out_ref,
    mixer,
    switch,
    write,
    read,
    decay,
    start,
    residual,
    router,
    chosen,
    slots,
    spills,
    skips,
    gains,
    out,
    inner,
    states,
    gathered_states,
    entering,
    entered,
    normed,
    pool,
    hidden,
    placing,
    shares,
    logits,
    leaving,
    sums,
    returned,
    xg,
    acc,
    act,
    w_gate,
    w_up,
    w_down,
    part,
    line,
    apart,
    weights,
    placings,
    ag_send,
    ag_recv,
    rs_send,
    rs_recv,
    mix_send,
    mix_recv,
    row_send,
    row_recv,
    back_send,
    back_recv,
    apart_send,
    apart_recv,
    weight_send,
    weight_recv,
    placing_send,
    placing_recv,
    spread_send,
    spread_recv,
    ready,
    load_sem,
    mix_sem,
    input_sem,
    done_sem,
    out_send,
    out_recv,
    in_send,
    in_recv,
):
    f32, bf16 = jnp.float32, jnp.bfloat16
    here = lax.axis_index("ctx")
    my = {"x": lax.rem(here, SIDE), "z": lax.div(here, SIDE)}
    my_exp, my_dp = lax.axis_index("exp"), lax.axis_index("dp")
    owner = my_exp * 2 + my_dp

    def around(axis, step):
        return lax.rem(my[axis] + step + SIDE, SIDE)

    def neighbour(axis, step):
        other = around(axis, step)
        if axis == "x":
            return {"ctx": my["z"] * SIDE + other}
        return {"ctx": other * SIDE + my["x"]}

    def along(axis, ref, place, at):
        if axis == "z":
            return ref.at[place, at]
        return ref.at[at, place]

    def partner(o):
        other = lax.rem(owner + o, EXPERTS)
        return other, {"exp": lax.div(other, 2), "dp": lax.rem(other, 2)}

    def remote(src, dst, send, recv, place):
        return pltpu.make_async_remote_copy(
            src_ref=src,
            dst_ref=dst,
            send_sem=send,
            recv_sem=recv,
            device_id=place,
            device_id_type=MESH,
        )

    def columns_of(q):
        return pl.ds(pl.multiple_of(q * WIDTH, WIDTH), WIDTH)

    def rows_of(index, count):
        return pl.ds(pl.multiple_of(index * count, count), count)

    def mix_room(q):
        return part.at[lax.div(q, 2), lax.rem(q, 2)]

    def mix_load(q):
        return pltpu.make_async_copy(
            mix_ref.at[:, :, :, columns_of(q)], mix_room(q), mix_sem.at[q]
        )

    barrier = pltpu.get_barrier_semaphore()

    def greet(k, _):
        other = lax.rem(here + k, CTX)
        pl.semaphore_signal(barrier, inc=1, device_id={"ctx": other}, device_id_type=MESH)
        return 0

    lax.fori_loop(1, CTX, greet, 0)
    for o in range(1, EXPERTS):
        pl.semaphore_signal(barrier, inc=1, device_id=partner(o)[1], device_id_type=MESH)

    inputs = {
        name: pltpu.make_async_copy(src, dst, input_sem.at[i])
        for i, (name, src, dst) in enumerate(
            (
                ("decay", decay_ref, decay),
                ("mixer", mixer_ref, mixer),
                ("write", write_ref, write),
                ("read", read_ref, read),
                ("start", start_ref.at[rows_of(here, SIZE), :], start),
                ("switch", switch_ref, switch),
                ("residual", residual_ref, residual),
                ("router", router_ref, router),
                ("skip", skip_ref, skips),
                ("gain", gain_ref, gains),
                ("chosen", chosen_ref, chosen),
                ("slots", slot_ref, slots),
                ("spills", spill_ref, spills),
            )
        )
    }
    for copy in inputs.values():
        copy.start()
    loads = [
        pltpu.make_async_copy(src, dst, load_sem.at[i])
        for i, (src, dst) in enumerate(((gate_ref, w_gate), (up_ref, w_up), (down_ref, w_down)))
    ]


    row_id = lax.broadcasted_iota(jnp.int32, (LENGTH, LENGTH), 0)
    col_id = lax.broadcasted_iota(jnp.int32, (LENGTH, LENGTH), 1)
    causal = row_id >= col_id
    upper = jnp.where(row_id <= col_id, 1.0, 0.0).astype(f32)
    inputs["decay"].wait()
    levels = jnp.dot(
        decay[...], upper, precision=lax.Precision.HIGHEST, preferred_element_type=f32
    )
    last = levels[:, LENGTH - 1 : LENGTH]
    to_end = jnp.exp(levels - last).T
    total_decay = jnp.exp(-last)
    levels_t = levels.T
    from_start = jnp.exp(-levels_t)
    low = lax.broadcasted_iota(jnp.int32, (LENGTH, 2 * SIZE), 1) < SIZE
    top = lax.broadcasted_iota(jnp.int32, (16, STATE), 0) < 8

    def spread(columns, q):
        return jnp.where(low, columns[:, 2 * q : 2 * q + 1], columns[:, 2 * q + 1 : 2 * q + 2])

    inputs["mixer"].wait()
    inputs["write"].wait()
    for q in range(HEADS // 2):
        lanes = pl.ds(q * 2 * SIZE, 2 * SIZE)
        scaled = (spread(to_end, q) * mixer[:, lanes].astype(f32)).astype(bf16)
        local = lax.dot_general(
            scaled, write[...], (((0,), (0,)), ((), ())), preferred_element_type=f32
        )
        for i in range(2):
            h = 2 * q + i
            states[h, 0:SIZE] = local[i * SIZE : (i + 1) * SIZE].astype(bf16)
            value = jnp.broadcast_to(total_decay[h : h + 1, :], (16, STATE))
            coarse = value.astype(bf16)
            rest = (value - coarse.astype(f32)).astype(bf16)
            states[h, SIZE:MESSAGE] = jnp.where(top, coarse, rest)

    pl.semaphore_wait(barrier, CTX - 1 + EXPERTS - 1)

    def out_copy(k):
        other = lax.rem(here + k, CTX)
        return remote(
            states.at[other],
            gathered_states.at[here],
            out_send.at[k],
            out_recv.at[k],
            {"ctx": other},
        )

    def in_copy(k):
        other = lax.rem(here + k, CTX)
        return remote(
            entering.at[other], entered.at[here], in_send.at[k], in_recv.at[k], {"ctx": other}
        )

    def each(action):
        def step(k, _):
            action(k)
            return 0

        lax.fori_loop(1, CTX, step, 0)

    each(lambda k: out_copy(k).start())
    gathered_states[here] = states[here]

    def load_mix(q, _):
        mix_load(q).start()
        return 0

    lax.fori_loop(0, 2 * QUADS, load_mix, 0)
    for load in loads:
        load.start()


    inputs["read"].wait()
    inputs["skip"].wait()
    meet = lax.dot_general(
        read[...], write[...], (((1,), (1,)), ((), ())), preferred_element_type=f32
    )

    def within(q):
        lanes = pl.ds(q * 2 * SIZE, 2 * SIZE)
        pair = mixer[:, lanes]
        heads = []
        for i in range(2):
            h = 2 * q + i
            span = levels[h : h + 1, :] - levels_t[:, h : h + 1]
            weight = jnp.exp(jnp.where(causal, span, -1e30)) * meet
            heads.append(jnp.dot(weight.astype(bf16), pair, preferred_element_type=f32))
        skip = spread(skips[...], q)
        inner[:, lanes] = jnp.where(low, heads[0], heads[1]) + skip * pair.astype(f32)

    for q in range(EARLY):
        within(q)


    inputs["start"].wait()
    state = start[...]
    for k in range(CTX):
        entering[k] = state.astype(bf16)
        behind = lax.rem(here - k + CTX, CTX)

        @pl.when(behind != 0)
        def _():
            in_copy(lax.rem(k - here + CTX, CTX)).start()
            out_copy(behind).wait_recv()

        if k < CTX - 1:
            factor = gathered_states[k, SIZE:MESSAGE].astype(f32)
            factor = factor[0:1, :] + factor[8:9, :]
            state = factor * state + gathered_states[k, 0:SIZE].astype(f32)
    entered[here] = entering[here]

    for q in range(EARLY, HEADS // 2):
        within(q)

    for name in ("chosen", "slots", "spills", "gain"):
        inputs[name].wait()

    place_id = lax.broadcasted_iota(jnp.int32, (EXPERTS * BLOCK, TOKENS), 0)
    expert_ids, slot_ids, spill_ids = chosen[...], slots[...], spills[...]
    target = jnp.where(
        slot_ids >= 0,
        expert_ids * BLOCK + slot_ids,
        jnp.where(
            spill_ids >= 0,
            jnp.right_shift(spill_ids, 1) * BLOCK + CAP + jnp.bitwise_and(spill_ids, 1),
            -1,
        ),
    )
    places = [place_id == target[i : i + 1, :] for i in range(2)]
    place = places[0].astype(f32) + places[1].astype(f32)
    placing[...] = place.astype(bf16)
    placings[here] = place.T.astype(bf16)
    logits[...] = jnp.zeros_like(logits)
    acc[...] = jnp.zeros_like(acc)

    inputs["switch"].wait()
    each(lambda k: in_copy(k).wait_recv())
    square = jnp.zeros((LENGTH, 1), f32)
    for q in range(HEADS // 2):
        lanes = pl.ds(q * 2 * SIZE, 2 * SIZE)
        carried = lax.dot_general(
            read[...],
            entered[2 * q : 2 * q + 2].reshape(2 * SIZE, STATE),
            (((1,), (1,)), ((), ())),
            preferred_element_type=f32,
        )
        gate = switch[:, lanes].astype(f32)
        gated = (inner[:, lanes] + carried * spread(from_start, q)) * (
            gate / (1.0 + jnp.exp(-gate))
        )
        inner[:, lanes] = gated
        square = square + jnp.sum(gated * gated, axis=1, keepdims=True)
    scale = lax.rsqrt(square / INNER + 1e-05)
    for q in range(HEADS // 2):
        lanes = pl.ds(q * 2 * SIZE, 2 * SIZE)
        normed[:, lanes] = (inner[:, lanes] * scale * gains[:, lanes]).astype(bf16)

    inputs["residual"].wait()
    inputs["router"].wait()
    each(lambda k: out_copy(k).wait_send())
    each(lambda k: in_copy(k).wait_send())

    every = pl.ds(0, SIDE)
    halves = {1: pl.ds(0, SIDE // 2), -1: pl.ds(SIDE // 2, SIDE // 2)}
    half_rows = {1: pl.ds(0, HALF), -1: pl.ds(HALF, HALF)}
    axes = (("x", "z"), ("z", "x"))
    slot = {1: 0, -1: 1}
    both = [(t, d) for t in range(2) for d in (1, -1)]


    def mixed(c, t):
        return pool.at[lax.rem(c, 2) * 2 + t]

    def term(q, i):
        b = q * (GROUPS - 1) + i - 1
        return pool.at[4 + lax.div(b, GROUPS), lax.rem(b, GROUPS)]

    def term_copy(c, t, i):
        other = lax.rem(my_exp + i, GROUPS)
        q = 2 * c + t
        return remote(
            mixed(c, t).at[other],
            term(q, i),
            mix_send.at[q, i - 1],
            mix_recv.at[q, i - 1],
            {"exp": other},
        )

    def mix(c):
        for t in range(2):
            q = 2 * c + t
            mix_load(q).wait()
            value = jnp.dot(
                normed[...],
                mix_room(q)[...].reshape(INNER, WIDTH),
                preferred_element_type=f32,
            )
            mixed(c, t)[...] = value.astype(bf16).reshape(GROUPS, TOKENS, WIDTH)
            for i in range(1, GROUPS):
                term_copy(c, t, i).start()


    def row_copy(c, t, o):
        other, place = partner(o)
        k = 2 * (my_dp * QUADS + c) + t
        return remote(
            leaving.at[lax.rem(c, 2), t, other],
            xg.at[k, my["z"], my["x"], rows_of(my_exp, BLOCK)],
            row_send.at[2 * c + t],
            row_recv.at[k],
            place,
        )

    def tokens(c, by_token=False):
        for t in range(2):
            q = 2 * c + t
            columns = columns_of(q)
            for i in range(1, GROUPS):
                term_copy(c, t, i).wait_recv()
            total = mixed(c, t)[my_exp].astype(f32)
            for i in range(1, GROUPS):
                total = total + term(q, i)[...].astype(f32)
            value = (residual[:, columns].astype(f32) + total).astype(bf16)
            hidden[:, columns] = value
            if by_token:
                apart[t, my["z"], my["x"]] = value
                for d in (1, -1):
                    ag_copy(c, t, 0, d, False, by_token=True).start()
                for d in (1, -1):
                    ag_copy(c, t, 2, d, False, by_token=True).start()
            else:
                rows = jnp.dot(placing[...], value, preferred_element_type=f32).astype(bf16)
                leaving[lax.rem(c, 2), t] = rows.reshape(EXPERTS, BLOCK, WIDTH)
                for o in range(1, EXPERTS):
                    row_copy(c, t, o).start()
                k = 2 * (my_dp * QUADS + c) + t
                xg[k, my["z"], my["x"], rows_of(my_exp, BLOCK)] = leaving[
                    lax.rem(c, 2), t, owner
                ]
            logits[...] += lax.dot_general(
                router[:, columns],
                value,
                (((1,), (1,)), ((), ())),
                preferred_element_type=f32,
            )
        for t in range(2):
            for i in range(1, GROUPS):
                term_copy(c, t, i).wait_send()

    def rows_sent(c):
        for t in range(2):
            ref = leaving.at[lax.rem(c, 2), t, pl.ds(0, EXPERTS - 1)]
            remote(ref, ref, row_send.at[2 * c + t], row_recv.at[0], partner(1)[1]).wait_send()


    def pair_of(j):
        return j + lax.div(j - 1, QUADS - 1)

    def ag_copy(j, t, step, d, landing, off=0, by_token=False):
        near, far = axes[t]
        chunk = apart.at[t] if by_token else xg.at[2 * pair_of(j) + t]
        back = -d if landing else 0
        if step == 0:
            ref, to = along(near, chunk, around(near, back), my[far]), near
        elif step == 1:
            ref = along(near, chunk, around(near, -2 * d if landing else -d), my[far])
            ref, to = ref.at[half_rows[d]], near
        elif step == 2 and off is None:
            ref, to = along(far, chunk, around(far, back), every), far
        elif step == 2:
            ref, to = along(near, chunk, around(near, off), my[far]), far
        else:
            ref = along(far, chunk, around(far, -2 * d if landing else -d), halves[d])
            to = far
        m = step * 2 + slot[d]
        return remote(ref, ref, ag_send.at[j, t, m], ag_recv.at[j, t, m], neighbour(to, d))

    def gather_first(j):
        pair = pair_of(j)
        mine = my_dp == lax.div(pair, QUADS)
        for t in range(2):
            k = 2 * pair + t

            def arrive(count):
                ref = xg.at[k, my["z"], my["x"], pl.ds(0, count)]
                remote(ref, ref, row_send.at[0], row_recv.at[k], partner(1)[1]).wait_recv()

            pl.when(mine)(functools.partial(arrive, PIECE - BLOCK))
            pl.when(jnp.logical_not(mine))(functools.partial(arrive, PIECE))
            for step in (0, 2):
                for d in (1, -1):
                    ag_copy(j, t, step, d, False).start()

    def gather_second(j, by_token=False):
        for t, d in both:
            ag_copy(j, t, 0, d, True, None, by_token).wait_recv()
            ag_copy(j, t, 1, d, False, 0, by_token).start()
            for e in (1, -1):
                ag_copy(j, t, 2, e, False, -d, by_token).start()

    def gather_third(j, by_token=False):
        for t in range(2):
            for d in (1, -1):
                ag_copy(j, t, 1, d, True, None, by_token).wait_recv()
            for d in (1, -1):
                ag_copy(j, t, 2, d, False, 2, by_token).start()

    def gather_last(j, by_token=False):
        for t, d in both:
            ag_copy(j, t, 2, d, True, None, by_token).wait_recv()
            ag_copy(j, t, 3, d, False, 0, by_token).start()

    def gather_done(j, by_token=False):
        for t, d in both:
            ag_copy(j, t, 3, d, True, None, by_token).wait_recv()
        for step in range(4):
            for t, d in both:
                ag_copy(j, t, step, d, False, None, by_token).wait_send()

    def multiply(h, c):
        @pl.loop(0, 2)
        def _(b):
            rows = rows_of(h * 2 + b, PLANE // 2)
            for n, weight in enumerate((w_gate, w_up)):
                total = acc[n, rows, :]
                for t in range(2):
                    total += jnp.dot(
                        xg[2 * (h * QUADS + c) + t, pl.ds(b * 2, 2)].reshape(PLANE // 2, WIDTH),
                        weight[columns_of(2 * c + t), :],
                        preferred_element_type=f32,
                    )
                acc[n, rows, :] = total

    def gathered(j):
        gather_done(j)

        @pl.when(j == 1)
        def _():
            for load in loads:
                load.wait()

        multiply(lax.div(j - 1, QUADS - 1), lax.rem(j - 1, QUADS - 1) + 1)

        @pl.when(j == QUADS - 1)
        def _():
            for o in range(1, EXPERTS):
                pl.semaphore_signal(ready, inc=1, device_id=partner(o)[1], device_id_type=MESH)


    def placing_copy(k):
        other = lax.rem(here + k, CTX)
        return remote(
            placings.at[here],
            placings.at[here],
            placing_send.at[k],
            placing_recv.at[k],
            {"ctx": other},
        )

    def spread_room(t, e):
        return part.at[2 + t, lax.div(e, SIDE), lax.rem(e, SIDE)]

    def spread_copy(t, o, x):
        other, place = partner(o)
        return remote(
            spread_room(t, other).at[:, pl.ds(x * BLOCK, BLOCK)],
            xg.at[2 * my_dp * QUADS + t, :, x, rows_of(my_exp, BLOCK)],
            spread_send.at[t],
            spread_recv.at[2 * my_dp + t],
            place,
        )

    def spread_rows():
        each(lambda k: placing_copy(k).wait_recv())
        for t in range(2):

            @pl.loop(0, SIDE)
            def _(z):
                for x in range(SIDE):
                    rows = lax.dot_general(
                        placings[z * SIDE + x],
                        apart[t, z, x],
                        (((0,), (0,)), ((), ())),
                        preferred_element_type=f32,
                    ).astype(bf16)
                    for e in range(EXPERTS):
                        part[2 + t, e // SIDE, e % SIDE, z, x * BLOCK : (x + 1) * BLOCK] = rows[
                            e * BLOCK : (e + 1) * BLOCK
                        ]

            for o in range(1, EXPERTS):
                for x in range(SIDE):
                    spread_copy(t, o, x).start()
            for x in range(SIDE):
                xg[2 * my_dp * QUADS + t, :, x, rows_of(my_exp, BLOCK)] = spread_room(t, owner)[
                    :, x * BLOCK : (x + 1) * BLOCK
                ]

    def spread_sent():
        for t in range(2):
            ref = pool.at[pl.ds(0, EXPERTS - 1)]
            remote(ref, ref, spread_send.at[t], spread_recv.at[0], partner(1)[1]).wait_send()

    def rows_done(h):
        for t in range(2):

            def arrive(count):
                ref = pool.at[pl.ds(0, count)]
                remote(
                    ref, ref, spread_send.at[0], spread_recv.at[2 * h + t], partner(1)[1]
                ).wait_recv()

            pl.when(my_dp == h)(functools.partial(arrive, GROUPS - 1))
            pl.when(my_dp != h)(functools.partial(arrive, GROUPS))
        multiply(h, 0)

        @pl.loop(0, 8)
        def _(b):
            rows = rows_of(h * 8 + b, PLANE // 8)
            gate = acc[0, rows, :]
            act[rows, :] = (gate / (1.0 + jnp.exp(-gate)) * acc[1, rows, :]).astype(bf16)


    def room_of(j, t):
        pair = lax.div(j, APART) * QUADS + lax.rem(j + 1, APART) - 2 * lax.div(j, 2 * APART)
        return xg.at[2 * pair + t]

    def rs_copy(j, t, step, d):
        near, far = axes[t]
        p = part.at[lax.rem(j, 4), t]
        room = room_of(j, t)
        if step == 0:
            src = along(far, p, around(far, 2), halves[d])
            dst, to = room.at[0, halves[d]], far
        elif step == 1:
            src = along(far, p, around(far, d), every)
            dst, to = room.at[1 + slot[d]], far
        elif step == 2:
            src = line.at[lax.rem(j, 4), t, around(near, 2), half_rows[d]]
            dst, to = room.at[3, 0, half_rows[d]], near
        else:
            src = line.at[lax.rem(j, 4), t, around(near, d)]
            dst, to = room.at[3, 1 + slot[d]], near
        m = step * 2 + slot[d]
        return remote(src, dst, rs_send.at[j, t, m], rs_recv.at[j, t, m], neighbour(to, d))

    def rs_start(j, step, t):
        for d in (1, -1):
            rs_copy(j, t, step, d).start()

    def rs_arrive(j, step, t):
        for d in (1, -1):
            rs_copy(j, t, step, d).wait_recv()

    def rs_sent(j, steps):
        for step in steps:
            for t, d in both:
                rs_copy(j, t, step, d).wait_send()

    def down(h, b, q):
        rows = rows_of(h * 2 + b, PLANE // 2)
        value = lax.dot_general(
            act[rows, :],
            w_down[columns_of(q), :],
            (((1,), (1,)), ((), ())),
            preferred_element_type=f32,
        )
        return value.astype(bf16)

    def by_rows(j):
        h = lax.div(j, APART)
        c = lax.rem(j, APART)

        @pl.loop(0, 2)
        def _(b):
            for t in range(2):
                part[lax.rem(j, 4), t, pl.ds(b * 2, 2)] = down(h, b, 2 * c + t).reshape(
                    2, SIDE, PIECE, WIDTH
                )


    def apart_room(t, e):
        if t == 0:
            return xg.at[2 * APART + lax.div(e, SIDE), lax.rem(e, SIDE)]
        return pool.at[e]

    def apart_copy(h, t, o):
        other = lax.rem(my_exp + o, GROUPS)
        return remote(
            apart.at[t, other],
            apart_room(t, owner),
            apart_send.at[h, t],
            apart_recv.at[t],
            {"exp": other, "dp": h},
        )

    def apart_sent(h):
        for t in range(2):

            def sent(count):
                ref = pool.at[pl.ds(0, count)]
                remote(
                    ref, ref, apart_send.at[h, t], apart_recv.at[0], partner(1)[1]
                ).wait_send()

            pl.when(my_dp == h)(functools.partial(sent, GROUPS - 1))
            pl.when(my_dp != h)(functools.partial(sent, GROUPS))

    def apart_start(h):
        if h == 0:
            pl.semaphore_wait(ready, EXPERTS - 1)
        else:
            apart_sent(0)
        for t in range(2):

            @pl.loop(0, 2)
            def _(b):
                value = down(h, b, 2 * APART + t)
                for i in range(2):
                    for x in range(SIDE):
                        for y in range(GROUPS):
                            low_row = (i * SIDE + x) * PIECE + y * BLOCK
                            apart[t, y, 2 * b + i, x * BLOCK : (x + 1) * BLOCK] = value[
                                low_row : low_row + BLOCK
                            ]

            for o in range(1, GROUPS):
                apart_copy(h, t, o).start()

            @pl.when(my_dp == h)
            def _():
                apart_room(t, owner)[...] = apart[t, my_exp]

            @pl.when(my_dp != h)
            def _():
                apart_copy(h, t, 0).start()

    def weight_copy(k):
        other = lax.rem(here + k, CTX)
        return remote(
            weights.at[here],
            weights.at[here],
            weight_send.at[k],
            weight_recv.at[k],
            {"ctx": other},
        )

    def by_tokens(j):
        each(lambda k: weight_copy(k).wait_recv())
        for t in range(2):
            ref = pool.at[pl.ds(0, EXPERTS - 1)]
            remote(ref, ref, apart_send.at[0, 0], apart_recv.at[t], partner(1)[1]).wait_recv()

            @pl.loop(0, SIDE)
            def _(z):
                for x in range(SIDE):
                    rows = jnp.concatenate(
                        [
                            apart_room(t, e)[z, x * BLOCK : (x + 1) * BLOCK]
                            for e in range(EXPERTS)
                        ],
                        axis=0,
                    )
                    value = jnp.dot(
                        weights[z * SIDE + x], rows, preferred_element_type=f32
                    )
                    part[lax.rem(j, 4), t, z, x] = value.astype(bf16)

    def sum_start(j):
        pl.when(j < 2 * APART)(functools.partial(by_rows, j))
        pl.when(j == 2 * APART)(functools.partial(by_tokens, j))
        for t in range(2):
            rs_start(j, 0, t)

    def sum_first(j):
        s = lax.rem(j, 4)
        for t, d in both:
            far = axes[t][1]
            base = 0 if d == 1 else SIDE // 2
            place = around(far, d)
            rs_copy(j, t, 0, d).wait_recv()

            @pl.loop(0, SIDE // 2)
            def _(i):
                at = (place, base + i) if far == "z" else (base + i, place)
                part[s, t, at[0], at[1]] = (
                    part[s, t, at[0], at[1]].astype(f32)
                    + room_of(j, t)[0, base + i].astype(f32)
                ).astype(bf16)

            rs_copy(j, t, 1, d).start()

    def sum_second(j):
        s = lax.rem(j, 4)
        for t in range(2):
            far = axes[t][1]
            rs_arrive(j, 1, t)

            @pl.loop(0, SIDE)
            def _(i):
                at = (my[far], i) if far == "z" else (i, my[far])
                line[s, t, i] = (
                    part[s, t, at[0], at[1]].astype(f32)
                    + room_of(j, t)[1, i].astype(f32)
                    + room_of(j, t)[2, i].astype(f32)
                ).astype(bf16)

            rs_start(j, 2, t)
        rs_sent(j, (0, 1))

    def sum_third(j):
        s = lax.rem(j, 4)
        for t, d in both:
            at = around(axes[t][0], d)
            rs_copy(j, t, 2, d).wait_recv()
            line[s, t, at, half_rows[d]] = (
                line[s, t, at, half_rows[d]].astype(f32)
                + room_of(j, t)[3, 0, half_rows[d]].astype(f32)
            ).astype(bf16)
            rs_copy(j, t, 3, d).start()


    def back_copy(j, t, o):
        other = lax.rem(my_exp + o, GROUPS)
        k = 2 * lax.rem(j, APART) + t
        return remote(
            sums.at[lax.rem(j, 2), t, other],
            returned.at[k, rows_of(owner, BLOCK)],
            back_send.at[2 * j + t],
            back_recv.at[k],
            {"exp": other, "dp": lax.div(j, APART)},
        )

    def sum_last(j):
        mine = my_dp == lax.div(j, APART)
        for t in range(2):
            rs_arrive(j, 3, t)
            total = (
                line[lax.rem(j, 4), t, my[axes[t][0]]].astype(f32)
                + room_of(j, t)[3, 1].astype(f32)
                + room_of(j, t)[3, 2].astype(f32)
            )

            @pl.when(j == 2 * APART)
            def _():
                q = 2 * APART + t
                columns = columns_of(q)
                out[:, columns] = (hidden[:, columns].astype(f32) + total).astype(bf16)
                out_store(q).start()

            @pl.when(j < 2 * APART)
            def _():
                s = lax.rem(j, 2)
                sums[s, t] = total.astype(bf16).reshape(GROUPS, BLOCK, WIDTH)
                for o in range(1, GROUPS):
                    back_copy(j, t, o).start()

                @pl.when(mine)
                def _():
                    k = 2 * lax.rem(j, APART) + t
                    returned[k, rows_of(owner, BLOCK)] = sums[s, t, my_exp]

                @pl.when(jnp.logical_not(mine))
                def _():
                    back_copy(j, t, 0).start()

        rs_sent(j, (2, 3))

    def out_store(q):
        columns = columns_of(q)
        return pltpu.make_async_copy(out.at[:, columns], out_ref.at[:, columns], done_sem.at[q])

    def sum_back(j):
        mine = my_dp == lax.div(j, APART)
        for t in range(2):
            q = 2 * lax.rem(j, APART) + t

            def sent(count):
                ref = sums.at[lax.rem(j, 2), t, pl.ds(0, count)]
                remote(
                    ref, ref, back_send.at[2 * j + t], back_recv.at[0], partner(1)[1]
                ).wait_send()

            @pl.when(mine)
            def _():
                ref = returned.at[q, pl.ds(0, (EXPERTS - 1) * BLOCK)]
                remote(ref, ref, back_send.at[0], back_recv.at[q], partner(1)[1]).wait_recv()
                columns = columns_of(q)
                total = hidden[:, columns].astype(f32)
                for n in range(2):
                    total = total + lax.dot_general(
                        shares[n],
                        returned[q],
                        (((0,), (0,)), ((), ())),
                        preferred_element_type=f32,
                    )
                out[:, columns] = total.astype(bf16)
                out_store(q).start()
                sent(GROUPS - 1)

            pl.when(jnp.logical_not(mine))(functools.partial(sent, GROUPS))

    def weigh():
        match = [
            lax.broadcasted_iota(jnp.int32, (EXPERTS, TOKENS), 0) == chosen[i : i + 1, :]
            for i in range(2)
        ]
        picked = [jnp.sum(jnp.where(m, logits[...], 0.0), axis=0, keepdims=True) for m in match]
        weight = jnp.zeros((EXPERTS * BLOCK, TOKENS), f32)
        for i in range(2):
            share = 1.0 / (1.0 + jnp.exp(picked[1 - i] - picked[i]))
            weight = weight + jnp.where(place_id == target[i : i + 1, :], share, 0.0)
        coarse = weight.astype(bf16)
        shares[0] = coarse
        shares[1] = (weight - coarse.astype(f32)).astype(bf16)
        weights[here] = weight.T.astype(bf16)
        each(lambda k: weight_copy(k).start())

    def stages(tick, count, steps):
        for lag, action in steps:
            pl.when(jnp.logical_and(tick >= lag, tick < count + lag))(
                functools.partial(action, tick - lag)
            )

    each(lambda k: placing_copy(k).start())

    def later(action):
        return lambda j: action(j + 1)

    @pl.loop(0, 1 + SUMS + ROUNDS + LAST)
    def _(turn):
        tick = turn - 1
        own = tick - my_dp * (QUADS - 1)

        def first(when, action):
            pl.when(tick == when)(functools.partial(action, tick - when, True))

        first(4, gather_last)
        stages(tick - 1, 2 * QUADS - 2, ((5, later(gather_last)),))
        first(3, gather_third)
        stages(tick - 1, 2 * QUADS - 2, ((4, later(gather_third)),))
        first(2, gather_second)
        stages(tick - 1, 2 * QUADS - 2, ((3, later(gather_second)), (2, later(gather_first))))
        stages(tick - SUMS, ROUNDS, ((4, sum_second), (2, sum_first)))
        stages(own - 1, QUADS - 1, ((3, later(rows_sent)),))
        first(1, tokens)
        stages(own - 1, QUADS - 1, ((1, later(tokens)),))
        stages(tick, 1, ((-1, mix),))
        stages(own - 1, QUADS - 1, ((-1, later(mix)),))
        first(5, gather_done)
        pl.when(tick == SPREAD + SPREAD_LATER * my_dp)(spread_rows)
        stages(tick - 1, 2 * QUADS - 2, ((6, later(gathered)),))
        pl.when(tick == SUMS + 2)(spread_sent)
        for h in range(2):
            pl.when(tick == DONE[h])(functools.partial(rows_done, h))
        pl.when(tick == SUMS)(weigh)
        stages(tick - SUMS, ROUNDS, ((0, sum_start), (5, sum_third), (6, sum_last)))
        stages(tick - SUMS, 2 * APART, ((7, sum_back),))
        for h in range(2):
            pl.when(tick == SUMS + APART * h)(functools.partial(apart_start, h))

    apart_sent(1)
    each(lambda k: weight_copy(k).wait_send())
    each(lambda k: placing_copy(k).wait_send())
    for q in range(2 * QUADS):
        out_store(q).wait()


def layer(*args):
    units = args[-1].shape[1]
    bf16, f32 = jnp.bfloat16, jnp.float32
    any_space = pl.BlockSpec(memory_space=pl.ANY)
    return pl.pallas_call(
        layer_kernel,
        out_shape=jax.ShapeDtypeStruct((TOKENS, D), bf16),
        in_specs=[any_space] * len(args),
        out_specs=any_space,
        scratch_shapes=[
            pltpu.VMEM((LENGTH, INNER), bf16),
            pltpu.VMEM((LENGTH, INNER), bf16),
            pltpu.VMEM((LENGTH, STATE), bf16),
            pltpu.VMEM((LENGTH, STATE), bf16),
            pltpu.VMEM((HEADS, LENGTH), f32),
            pltpu.VMEM((SIZE, STATE), f32),
            pltpu.VMEM((TOKENS, D), bf16),
            pltpu.VMEM((EXPERTS, D), bf16),
            pltpu.VMEM((2, TOKENS), jnp.int32),
            pltpu.VMEM((2, TOKENS), jnp.int32),
            pltpu.VMEM((2, TOKENS), jnp.int32),
            pltpu.VMEM((1, HEADS), f32),
            pltpu.VMEM((1, INNER), f32),
            pltpu.VMEM((TOKENS, D), bf16),
            pltpu.VMEM((LENGTH, INNER), f32),
            pltpu.VMEM((CTX, MESSAGE, STATE), bf16),
            pltpu.VMEM((CTX, MESSAGE, STATE), bf16),
            pltpu.VMEM((CTX, SIZE, STATE), bf16),
            pltpu.VMEM((CTX, SIZE, STATE), bf16),
            pltpu.VMEM((LENGTH, INNER), bf16),
            pltpu.VMEM((4 + 2 * QUADS * (GROUPS - 1) // GROUPS, GROUPS, TOKENS, WIDTH), bf16),
            pltpu.VMEM((TOKENS, D), bf16),
            pltpu.VMEM((EXPERTS * BLOCK, TOKENS), bf16),
            pltpu.VMEM((2, EXPERTS * BLOCK, TOKENS), bf16),
            pltpu.VMEM((EXPERTS, TOKENS), f32),
            pltpu.VMEM((2, 2, EXPERTS, BLOCK, WIDTH), bf16),
            pltpu.VMEM((2, 2, GROUPS, BLOCK, WIDTH), bf16),
            pltpu.VMEM((2 * APART, EXPERTS * BLOCK, WIDTH), bf16),
            pltpu.VMEM((2 * PAIRS, SIDE, SIDE, PIECE, WIDTH), bf16),
            pltpu.VMEM((2, 2 * PLANE, units), f32),
            pltpu.VMEM((2 * PLANE, units), bf16),
            pltpu.VMEM((D, units), bf16),
            pltpu.VMEM((D, units), bf16),
            pltpu.VMEM((D, units), bf16),
            pltpu.VMEM((4, 2, SIDE, SIDE, PIECE, WIDTH), bf16),
            pltpu.VMEM((4, 2, SIDE, PIECE, WIDTH), bf16),
            pltpu.VMEM((2, GROUPS, SIDE, PIECE, WIDTH), bf16),
            pltpu.VMEM((CTX, TOKENS, EXPERTS * BLOCK), bf16),
            pltpu.VMEM((CTX, TOKENS, EXPERTS * BLOCK), bf16),
            pltpu.SemaphoreType.DMA((PAIRS, 2, 8)),
            pltpu.SemaphoreType.DMA((PAIRS, 2, 8)),
            pltpu.SemaphoreType.DMA((PAIRS, 2, 8)),
            pltpu.SemaphoreType.DMA((PAIRS, 2, 8)),
            pltpu.SemaphoreType.DMA((2 * QUADS, GROUPS - 1)),
            pltpu.SemaphoreType.DMA((2 * QUADS, GROUPS - 1)),
            pltpu.SemaphoreType.DMA((2 * QUADS,)),
            pltpu.SemaphoreType.DMA((2 * PAIRS,)),
            pltpu.SemaphoreType.DMA((2 * PAIRS,)),
            pltpu.SemaphoreType.DMA((2 * QUADS,)),
            pltpu.SemaphoreType.DMA((2, 2)),
            pltpu.SemaphoreType.DMA((2,)),
            pltpu.SemaphoreType.DMA((CTX,)),
            pltpu.SemaphoreType.DMA((CTX,)),
            pltpu.SemaphoreType.DMA((CTX,)),
            pltpu.SemaphoreType.DMA((CTX,)),
            pltpu.SemaphoreType.DMA((2,)),
            pltpu.SemaphoreType.DMA((4,)),
            pltpu.SemaphoreType.REGULAR,
            pltpu.SemaphoreType.DMA((3,)),
            pltpu.SemaphoreType.DMA((2 * QUADS,)),
            pltpu.SemaphoreType.DMA((13,)),
            pltpu.SemaphoreType.DMA((2 * QUADS,)),
            pltpu.SemaphoreType.DMA((CTX,)),
            pltpu.SemaphoreType.DMA((CTX,)),
            pltpu.SemaphoreType.DMA((CTX,)),
            pltpu.SemaphoreType.DMA((CTX,)),
        ],
        compiler_params=pltpu.CompilerParams(
            collective_id=0, has_side_effects=True, vmem_limit_bytes=63 << 20
        ),
        cost_estimate=pl.CostEstimate(
            flops=6 * 2048 * D * 512, bytes_accessed=24 << 20, transcendentals=1 << 20
        ),
    )(*args)


def shards(
    mixer_in,
    gate_in,
    state_write,
    state_read,
    decay_rate,
    skip_gain,
    norm_gain,
    start_state,
    out_weight,
    residual,
    router_weight,
    chosen,
    slot_index,
    spill_index,
    gate_weight,
    up_weight,
    down_weight,
):
    return layer(
        mixer_in[0],
        gate_in[0],
        state_write[0, :, 0],
        state_read[0, :, 0],
        decay_rate[0],
        skip_gain[None],
        norm_gain[None],
        start_state[0].reshape(HEADS * SIZE, STATE),
        out_weight.reshape(SIDE, SIDE, PIECE, D),
        residual[0],
        router_weight.T,
        chosen[0].T,
        slot_index[0].T,
        spill_index[0].T,
        gate_weight[0],
        up_weight[0],
        down_weight[0],
    )[None]


def solution(mesh):
    placed = (
        P("dp", "ctx", "exp"),
        P("dp", "ctx", "exp"),
        P("dp", "ctx", "exp", None),
        P("dp", "ctx", "exp", None),
        P("dp", "exp", "ctx"),
        P("exp"),
        P("exp"),
        P("dp", "exp", None, None),
        P("exp", None),
        P("dp", ("ctx", "exp"), None),
        P(),
        P("dp", ("ctx", "exp"), None),
        P("dp", ("ctx", "exp"), None),
        P("dp", ("ctx", "exp"), None),
        P(("exp", "dp"), None, "ctx"),
        P(("exp", "dp"), None, "ctx"),
        P(("exp", "dp"), None, "ctx"),
    )
    return jax.shard_map(
        shards, mesh=mesh, in_specs=placed, out_specs=P("dp", ("ctx", "exp"), None), check_vma=False
    )
```
